128 devices in a mesh: ctx: 16 (over x_lo, z, core), tp: 8 (over y, x_hi).
Axes of the slice: x: 4 (x_hi: 2, x_lo: 2; x = x_hi * 2 + x_lo), y: 4, z: 4, core: 2. Of those that a mesh axis runs over, the one named last changes fastest.
Arguments:
- base_qkv: bfloat16 [3, 8192, 2048], P(None, 'ctx', 'tp'), may hold values from -64 to 64
- frames: bfloat16 [128, 32, 1024], P(('ctx', 'tp')), may hold values from -6 to 6
- frame_block: int32 [128], P(('ctx', 'tp')), may hold values from 0 to 15, as said below
- frame_slot: int32 [128], P(('ctx', 'tp')), may hold values from 0 to 15
- frame_live: int32 [128], P(('ctx', 'tp')), may hold values from 0 to 1
- start_block: int32 [64], replicated, may hold values from 0 to 63, as said below
- conn_w: bfloat16 [1024, 3, 2048], P(None, None, 'tp'), may hold values from -0.1875 to 0.1875
- d_out: bfloat16 [8192, 2048], P('ctx', 'tp'), may hold values from -6 to 6
Outputs:
- attn_out: bfloat16 [8192, 2048], P('ctx', 'tp')
- qkv_grad: bfloat16 [3, 8192, 2048], P(None, 'ctx', 'tp')
- conn_grad: float32 [1024, 3, 2048], P(None, None, 'tp')
The draws below stay inside these ranges and needn't reach their ends.
Inputs may be any that keep to these rules, and one draw needn't show every extreme that they name: A frame f with frame_live[f] = 1 fills the 32 positions from frame_block[f] * 512 + frame_slot[f] * 32; no two such frames share block and slot; the frame slots of the devices of one ctx index go to different blocks. start_block[i] <= i, never falls, and start_block[0] = 0.
All inputs are finite; a program needn't handle non-finite values.
Results may differ from the reference program's by a relative error of at most 0.012.
The reference program's roundings to bfloat16 on the way count: a program that leaves them out, or rounds other values in their place, can miss the bound.
Values may be sent and summed in bfloat16 or wider, within the bound.
A program may use at most 128 MiB of HBM per device.

```python
import math
import jax
import jax.numpy as jnp
from jax import lax

ROWS = 512
HEADS = 16
HEAD_DIM = 128
VIS_W = 1024
FRAME_TOK = 32
MASK_BLK = 128
SEQ = 8192
QKV_W = 2048
FRAMES = 128
MASK_BLOCKS = 64
N_CTX = 16
N_TP = 8


def top_first(sub_key):
    slot_count = ROWS // FRAME_TOK
    order = jax.random.permutation(sub_key, slot_count).astype(jnp.int32)
    where_top = jnp.sum(jnp.where(order == slot_count - 1, jnp.arange(slot_count, dtype=jnp.int32), 0))
    return order[(jnp.arange(slot_count, dtype=jnp.int32) + where_top) % slot_count]


def frame_plan(key):
    plan_key = jax.random.fold_in(key, 101)
    key_offsets, key_slots, key_live = jax.random.split(plan_key, 3)
    shuffled = jax.random.permutation(key_offsets, N_CTX).astype(jnp.int32)
    ctx_ids = jnp.arange(N_CTX, dtype=jnp.int32)
    where_half = jnp.sum(jnp.where(shuffled == N_CTX // 2, ctx_ids, 0))
    offsets = shuffled[(jnp.arange(N_TP, dtype=jnp.int32) + where_half) % N_CTX]
    frame_ids = jnp.arange(FRAMES, dtype=jnp.int32)
    row_ids = frame_ids // N_TP
    col_ids = frame_ids % N_TP
    target = ((row_ids + offsets[col_ids]) % N_CTX).astype(jnp.int32)
    orders = jax.vmap(top_first)(jax.random.split(key_slots, N_CTX))
    slot_ids = orders[target, col_ids].astype(jnp.int32)
    coins = jax.random.randint(key_live, (FRAMES,), 0, 4)
    live_ids = jnp.where((frame_ids < N_TP) | (coins > 0), 1, 0).astype(jnp.int32)
    return (target, slot_ids, live_ids)


def draw_frame_block(key, part):
    return frame_plan(key)[0]


def draw_frame_slot(key, part):
    return frame_plan(key)[1]


def draw_frame_live(key, part):
    return frame_plan(key)[2]


def draw_start_block(key, part):
    key = jax.random.fold_in(key, 7)
    coins = jax.random.randint(key, (MASK_BLOCKS,), 0, 16)
    block_ids = jnp.arange(MASK_BLOCKS, dtype=jnp.int32)
    starts = jnp.where((coins == 0) | (block_ids == 0) | (block_ids == MASK_BLOCKS - 1), block_ids, 0)
    return lax.cummax(starts).astype(jnp.int32)


def draw_base_qkv(key, part):
    key = jax.random.fold_in(key, 13)
    key_main = jax.random.fold_in(key, 0)
    values_all = jax.random.normal(key_main, (3, SEQ, QKV_W), jnp.float32)
    return values_all.astype(jnp.bfloat16)


def level_of(own_key, extent, pieces, low, largest):
    loudness, own = 1.0, jax.random.fold_in(own_key, 6)
    for dim, parts in pieces:
        heights = jnp.exp(jax.random.uniform(jax.random.fold_in(own, dim), (parts,), jnp.float32, low / len(pieces), largest / len(pieces)))
        loudness = loudness * jnp.repeat(heights, extent[dim] // parts).reshape([-1 if axis == dim else 1 for axis in range(len(extent))])
    return loudness


def normal_values(stream_key, shape, scale, limit, shards=(), kind=jnp.bfloat16):
    drawn = scale * jax.random.normal(stream_key, shape, jnp.float32)
    if shards:
        drawn = drawn * level_of(stream_key, shape, shards, -0.22, 0.18)
    return jnp.clip(drawn, -limit, limit).astype(kind)


def setup_inputs(seed: int = 0) -> dict:
    seeds = jax.random.split(jax.random.key(seed), 9)
    base_qkv = draw_base_qkv(jax.random.fold_in(seeds[8], 71), 0)
    frames = normal_values(seeds[1], (FRAMES, FRAME_TOK, VIS_W), 1.0, 6.0, ((0, 128),))
    frame_block = draw_frame_block(jax.random.fold_in(seeds[8], 71), 0)
    frame_slot = draw_frame_slot(jax.random.fold_in(seeds[8], 71), 0)
    frame_live = draw_frame_live(jax.random.fold_in(seeds[8], 71), 0)
    start_block = draw_start_block(jax.random.fold_in(seeds[8], 71), 0)
    conn_w = normal_values(seeds[6], (VIS_W, 3, QKV_W), VIS_W ** -0.5, 0.1875, ((2, 8),))
    d_out = normal_values(seeds[7], (SEQ, QKV_W), 1.0, 6.0, ((0, 16), (1, 8)))
    return dict(base_qkv=base_qkv, frames=frames, frame_block=frame_block, frame_slot=frame_slot, frame_live=frame_live, start_block=start_block, conn_w=conn_w, d_out=d_out)


def visible_pairs(positions, start_block):
    query_start = start_block[positions // MASK_BLK]
    return (positions[None, :] <= positions[:, None]) & ((positions // MASK_BLK)[None, :] >= query_start[:, None])

def reference(base_qkv, frames, frame_block, frame_slot, frame_live, start_block, conn_w, d_out):
    slot_count = ROWS // FRAME_TOK
    slots_total = N_CTX * slot_count
    frame_code = jnp.where(frame_live == 1, frame_block * slot_count + frame_slot, slots_total).astype(jnp.int32)
    placed = jnp.zeros((slots_total, FRAME_TOK, VIS_W), jnp.bfloat16).at[frame_code].set(frames, mode='drop')
    placed = placed.reshape(SEQ, VIS_W)
    vision_terms = jnp.einsum('sv,vcw->csw', placed.astype(jnp.float32), conn_w.astype(jnp.float32))
    projected = (base_qkv.astype(jnp.float32) + vision_terms).astype(jnp.bfloat16)
    score_scale = 1.0 / math.sqrt(HEAD_DIM)
    positions = jnp.arange(SEQ, dtype=jnp.int32)
    allowed = visible_pairs(positions, start_block)

    def by_head(matrix):
        return matrix.reshape(SEQ, HEADS, HEAD_DIM).transpose(1, 0, 2)

    def head_terms(operands):
        queries, keys_now, values_now, out_grad = operands
        scores = jnp.dot(queries, keys_now.T, preferred_element_type=jnp.float32) * score_scale
        log_norm = jax.nn.logsumexp(jnp.where(allowed, scores, -jnp.inf), axis=1)
        weights = jnp.where(allowed, jnp.exp(scores - log_norm[:, None]), 0.0)
        probs = weights.astype(jnp.bfloat16)
        attn = jnp.dot(probs, values_now, preferred_element_type=jnp.float32).astype(jnp.bfloat16)
        row_dot = lax.optimization_barrier(jnp.sum(out_grad.astype(jnp.float32) * attn.astype(jnp.float32), axis=1))
        prob_grad = jnp.dot(out_grad, values_now.T, preferred_element_type=jnp.float32)
        score_grad = (weights * (prob_grad - row_dot[:, None]) * score_scale).astype(jnp.bfloat16)
        query_grad = jnp.dot(score_grad, keys_now, preferred_element_type=jnp.float32).astype(jnp.bfloat16)
        key_grad = jnp.dot(score_grad.T, queries, preferred_element_type=jnp.float32).astype(jnp.bfloat16)
        value_grad = jnp.dot(probs.T, out_grad, preferred_element_type=jnp.float32).astype(jnp.bfloat16)
        return (attn, query_grad, key_grad, value_grad)
    results = lax.map(head_terms, (by_head(projected[0]), by_head(projected[1]), by_head(projected[2]), by_head(d_out)))

    def merged(stacked):
        return stacked.transpose(1, 0, 2).reshape(SEQ, QKV_W)
    attn_out = merged(results[0])
    qkv_grad = jnp.stack([merged(results[1]), merged(results[2]), merged(results[3])])
    conn_grad = jnp.einsum('sv,csw->vcw', placed.astype(jnp.float32), qkv_grad.astype(jnp.float32))
    return (attn_out, qkv_grad, conn_grad)
```

```python
import math

import jax
import jax.numpy as jnp
from jax import lax
from jax.experimental import pallas as pl
from jax.experimental.pallas import tpu as pltpu
from jax.sharding import PartitionSpec as P

HEAD_DIM = 128
FRAME_TOK = 32
MASK_BLK = 128
CODE_ROWS = 16
N_Z = 4
KEY_TILE = 256
MASKED = -1e30
MESH = pl.DeviceIdType.MESH
F32 = jnp.float32
BF16 = jnp.bfloat16
VMEM_LIMIT = 56 * 1024 * 1024

NT = (((1,), (1,)), ((), ()))
TN = (((0,), (0,)), ((), ()))


def place():
    c = lax.axis_index("ctx")
    core = c % 2
    z = (c // 2) % N_Z
    xl = c // (2 * N_Z)
    return c, core, z, xl


def ctx_id(xl, z, core):
    return xl * (2 * N_Z) + lax.rem(z, N_Z) * 2 + core


def entry_barrier(n_ctx, n_tp, c, t):
    barrier = pltpu.get_barrier_semaphore()
    for k in range(1, n_tp):
        pl.semaphore_signal(barrier, inc=1, device_id={"tp": lax.rem(t + k, n_tp)}, device_id_type=MESH)
    for k in range(1, n_ctx):
        pl.semaphore_signal(barrier, inc=1, device_id={"ctx": lax.rem(c + k, n_ctx)}, device_id_type=MESH)
    pl.semaphore_wait(barrier, n_tp - 1 + n_ctx - 1)


def remote(src, dst, send, recv, **where):
    return pltpu.make_async_remote_copy(
        src_ref=src, dst_ref=dst, send_sem=send, recv_sem=recv, device_id=where, device_id_type=MESH
    )


def gather_kernel(
    n_ctx, n_tp, fb, fs, fl, frames, base_hbm, w_hbm, dout,
    placed, q2, do2, kv,
    s_a, r_a, s_b, r_b, base, w, qkv, xs, xq, xd,
    load_sem, a_send, a_recv, b_send, b_recv, c_send, c_recv,
    x_send, x_recv, z_send, z_recv, s_send, s_recv,
):
    c, core, z, xl = place()
    t = lax.axis_index("tp")
    pw = frames.shape[2] // n_tp
    rows = placed.shape[0]
    half = rows // 2
    ox = 1 - xl
    cx = ctx_id(ox, z, core)
    sib = ctx_id(xl, z, 1 - core)
    mine = pl.ds(pl.multiple_of(xl * HEAD_DIM, HEAD_DIM), HEAD_DIM)
    other = pl.ds(pl.multiple_of(ox * HEAD_DIM, HEAD_DIM), HEAD_DIM)

    load_w = pltpu.make_async_copy(w_hbm, w, load_sem.at[0])
    load_b = pltpu.make_async_copy(base_hbm, base, load_sem.at[1])
    load_w.start()
    load_b.start()

    code = jnp.where(fl[0] == 1, fb[0] * (rows // FRAME_TOK) + fs[0] + 1, 0).astype(F32)
    code_rows = jnp.full((CODE_ROWS, pw), code, F32).astype(BF16)
    for p in range(n_tp):
        s_a[p, :FRAME_TOK, :] = frames[0, :, p * pw:(p + 1) * pw]
        s_a[p, FRAME_TOK:, :] = code_rows
    xd[...] = dout[:, other]
    do2[xl] = dout[:, mine]

    entry_barrier(n_ctx, n_tp, c, t)

    sends = []

    def go(copy):
        copy.start()
        sends.append(copy)

    for k in range(1, n_tp):
        p = lax.rem(t + k, n_tp)
        go(remote(s_a.at[p], r_a.at[t], a_send.at[k], a_recv.at[k], tp=p))
    r_a[t] = s_a[t]
    go(remote(xd, do2.at[xl], x_send.at[0], x_recv.at[0], ctx=cx))
    for k in range(1, n_tp):
        p = lax.rem(t + n_tp - k, n_tp)
        remote(s_a.at[p], r_a.at[p], a_send.at[k], a_recv.at[k], tp=p).wait_recv()

    slots = rows // FRAME_TOK
    pieces = r_a[...].astype(F32)
    codes = pieces[:, FRAME_TOK:FRAME_TOK + 1, :]
    for k in range(n_ctx):
        d = lax.rem(c + k, n_ctx)
        low = (d * slots).astype(F32)
        hit = (codes > low) & (codes < low + (slots + 0.5))
        s_b[k] = jnp.sum(jnp.where(hit, pieces, 0.0), axis=0).astype(BF16)
        if k:
            go(remote(s_b.at[k], r_b.at[c], b_send.at[k], b_recv.at[k], ctx=d))
    r_b[c] = s_b[0]
    for k in range(1, n_ctx):
        d = lax.rem(c + n_ctx - k, n_ctx)
        remote(s_b.at[k], r_b.at[d], b_send.at[k], b_recv.at[k], ctx=d).wait_recv()

    arrived = r_b[...].astype(F32)
    codes = arrived[:, FRAME_TOK:FRAME_TOK + 1, :]
    rows_in = arrived[:, :FRAME_TOK, :]
    own_cols = pl.ds(pl.multiple_of(t * pw, pw), pw)
    for s in range(slots):
        want = (c * slots + (s + 1)).astype(F32)
        placed[s * FRAME_TOK:(s + 1) * FRAME_TOK, own_cols] = jnp.sum(
            jnp.where(codes == want, rows_in, 0.0), axis=0
        ).astype(BF16)
    for k in range(1, n_tp):
        p = lax.rem(t + k, n_tp)
        go(remote(placed.at[:, own_cols], placed.at[:, own_cols], c_send.at[k], c_recv.at[k], tp=p))
    load_w.wait()
    load_b.wait()
    for k in range(1, n_tp):
        p = lax.rem(t + n_tp - k, n_tp)
        cols = pl.ds(pl.multiple_of(p * pw, pw), pw)
        remote(placed.at[:, cols], placed.at[:, cols], c_send.at[k], c_recv.at[k], tp=p).wait_recv()

    width = base.shape[2]

    def project(i):
        term = jnp.dot(placed[...], w[:, i * width:(i + 1) * width], preferred_element_type=F32)
        qkv[i] = (base[i].astype(F32) + term).astype(BF16)

    project(1)
    project(2)
    xs[:, :HEAD_DIM] = qkv[1, :, other]
    xs[:, HEAD_DIM:] = qkv[2, :, other]
    kv[c, :, :HEAD_DIM] = qkv[1, :, mine]
    kv[c, :, HEAD_DIM:] = qkv[2, :, mine]

    right = ctx_id(xl, z + 1, core)
    left = ctx_id(xl, z + N_Z - 1, core)
    far = ctx_id(xl, z + 2, core)
    right_x = ctx_id(ox, z + 1, core)
    left_x = ctx_id(ox, z + N_Z - 1, core)
    far_x = ctx_id(ox, z + 2, core)

    def block(i):
        return kv.at[i]

    def top(i):
        return kv.at[i, pl.ds(0, half)]

    def low_half(i):
        return kv.at[i, pl.ds(half, half)]

    def to_right(ref, n):
        go(remote(ref, ref, z_send.at[n], z_recv.at[n], ctx=right))

    def to_left(ref, n):
        go(remote(ref, ref, z_send.at[4 + n], z_recv.at[4 + n], ctx=left))

    def to_sib(ref, n):
        go(remote(ref, ref, s_send.at[n], s_recv.at[n], ctx=sib))

    def from_left(ref, n):
        remote(ref, ref, z_send.at[n], z_recv.at[n], ctx=left).wait_recv()

    def from_right(ref, n):
        remote(ref, ref, z_send.at[4 + n], z_recv.at[4 + n], ctx=right).wait_recv()

    go(remote(xs, kv.at[c], x_send.at[1], x_recv.at[1], ctx=cx))
    to_right(block(c), 0)
    to_left(block(c), 0)
    to_sib(block(c), 0)
    project(0)
    xq[...] = qkv[0, :, other]
    q2[xl] = qkv[0, :, mine]
    go(remote(xq, q2.at[xl], x_send.at[2], x_recv.at[2], ctx=cx))

    remote(xs, kv.at[cx], x_send.at[1], x_recv.at[1], ctx=cx).wait_recv()
    to_right(block(cx), 1)
    to_left(block(cx), 1)
    to_sib(block(cx), 1)
    from_left(block(left), 0)
    to_right(top(left), 2)
    to_sib(block(left), 2)
    from_right(block(right), 0)
    to_left(low_half(right), 2)
    to_sib(block(right), 3)
    from_left(block(left_x), 1)
    to_right(top(left_x), 3)
    to_sib(block(left_x), 4)
    from_right(block(right_x), 1)
    to_left(low_half(right_x), 3)
    to_sib(block(right_x), 5)
    from_left(top(far), 2)
    to_sib(top(far), 6)
    from_right(low_half(far), 2)
    to_sib(low_half(far), 7)
    from_left(top(far_x), 3)
    to_sib(top(far_x), 8)
    from_right(low_half(far_x), 3)
    to_sib(low_half(far_x), 9)

    sc = 1 - core
    theirs = [
        kv.at[ctx_id(xl, z, sc)], kv.at[ctx_id(ox, z, sc)],
        kv.at[ctx_id(xl, z + N_Z - 1, sc)], kv.at[ctx_id(xl, z + 1, sc)],
        kv.at[ctx_id(ox, z + N_Z - 1, sc)], kv.at[ctx_id(ox, z + 1, sc)],
        top(ctx_id(xl, z + 2, sc)), low_half(ctx_id(xl, z + 2, sc)),
        top(ctx_id(ox, z + 2, sc)), low_half(ctx_id(ox, z + 2, sc)),
    ]
    for n, ref in enumerate(theirs):
        remote(ref, ref, s_send.at[n], s_recv.at[n], ctx=sib).wait_recv()
    remote(xd, do2.at[ox], x_send.at[0], x_recv.at[0], ctx=cx).wait_recv()
    remote(xq, q2.at[ox], x_send.at[2], x_recv.at[2], ctx=cx).wait_recv()
    for copy in sends:
        copy.wait_send()


def attention_kernel(
    start, q2, do2, kv, o2, dq2, dkv, dkv_acc, acc, m_ref, l_ref
):
    c, core, z, xl = place()
    lower = lax.rem(c, 2 * N_Z)
    rows = q2.shape[1]
    tile = KEY_TILE
    per_block = rows // tile
    mask_per = rows // MASK_BLK
    scale = 1.0 / math.sqrt(HEAD_DIM)
    scale2 = scale * math.log2(math.e)

    dkv_acc[...] = jnp.zeros_like(dkv_acc)

    for qi in range(2):
        blk = lower + 2 * N_Z * qi
        q0 = blk * rows
        queries = q2[qi]
        out_grad = do2[qi]
        starts = [start[blk * mask_per + i] for i in range(mask_per)]
        q_start = jnp.concatenate(
            [jnp.full((1, MASK_BLK), s * MASK_BLK, jnp.int32) for s in starts], axis=1
        )
        first_diag = blk * per_block
        low = (starts[0] * MASK_BLK) // tile
        low = jnp.minimum(low, first_diag)
        clear = jnp.minimum((starts[-1] * MASK_BLK + tile - 1) // tile, first_diag)

        def keys_at(kt):
            b = kt // per_block
            off = pl.multiple_of((kt - b * per_block) * tile, tile)
            return b, pl.ds(off, tile)

        def allowed(kt):
            key_pos = kt * tile + lax.broadcasted_iota(jnp.int32, (tile, rows), 0)
            q_pos = q0 + lax.broadcasted_iota(jnp.int32, (tile, rows), 1)
            return (key_pos <= q_pos) & (key_pos >= q_start)

        m_ref[...] = jnp.full_like(m_ref, MASKED)
        l_ref[...] = jnp.zeros_like(l_ref)
        acc[...] = jnp.zeros_like(acc)

        def forward(kt, masked):
            b, sl = keys_at(kt)
            s = lax.dot_general(kv[b, sl, :HEAD_DIM], queries, NT, preferred_element_type=F32) * scale2
            if masked:
                s = jnp.where(allowed(kt), s, MASKED)
            m_old = m_ref[...]
            m_new = jnp.maximum(m_old, jnp.max(s, axis=0, keepdims=True))
            p = jnp.exp2(s - m_new)
            alpha = jnp.exp2(m_old - m_new)
            m_ref[...] = m_new
            l_ref[...] = l_ref[...] * alpha + jnp.sum(p, axis=0, keepdims=True)
            acc[...] = acc[...] * alpha + lax.dot_general(
                kv[b, sl, HEAD_DIM:], p.astype(BF16), TN, preferred_element_type=F32
            )

        def loop(lo, hi, step, masked):
            def body(i, carry):
                step(i, masked)
                return carry

            lax.fori_loop(lo, hi, body, 0)

        loop(first_diag, first_diag + per_block, forward, True)
        loop(clear, first_diag, forward, False)
        loop(low, clear, forward, True)

        total = l_ref[...]
        out_t = (acc[...] / total).astype(BF16).astype(F32)
        o2[qi] = out_t.T.astype(BF16)
        row_dot = jnp.sum(out_t * out_grad.astype(F32).T, axis=0, keepdims=True)
        log_norm = m_ref[...] + jnp.log2(total)
        acc[...] = jnp.zeros_like(acc)

        def backward(kt, masked):
            b, sl = keys_at(kt)
            keys = kv[b, sl, :HEAD_DIM]
            s = lax.dot_general(keys, queries, NT, preferred_element_type=F32) * scale2
            p = jnp.exp2(s - log_norm)
            if masked:
                p = jnp.where(allowed(kt), p, 0.0)
            dp = lax.dot_general(kv[b, sl, HEAD_DIM:], out_grad, NT, preferred_element_type=F32)
            ds = (p * (dp - row_dot) * scale).astype(BF16)
            at = pl.ds(pl.multiple_of(kt * tile, tile), tile)
            dkv_acc[at, :HEAD_DIM] += jnp.dot(ds, queries, preferred_element_type=F32)
            dkv_acc[at, HEAD_DIM:] += jnp.dot(p.astype(BF16), out_grad, preferred_element_type=F32)
            acc[...] += lax.dot_general(keys, ds, TN, preferred_element_type=F32)

        loop(first_diag, first_diag + per_block, backward, True)
        loop(clear, first_diag, backward, False)
        loop(low, clear, backward, True)
        dq2[qi] = acc[...].T.astype(BF16)

    def write(b, carry):
        at = pl.ds(pl.multiple_of(b * rows, rows), rows)
        dkv[b] = dkv_acc[at, :].astype(BF16)
        return carry

    lax.fori_loop(0, dkv.shape[0], write, 0)


def reduce_kernel(
    n_ctx, dkv, dq2, o2, placed,
    attn_out, qkv_grad, conn,
    own, sb, part, far_l, far_r, in_l, in_r, res, gx, gdq, go_in,
    placed_t, cs_send, cs_recv, mine_sum, rs_out, rs_in, cg,
    load_sem, s_send, s_recv, f_send, f_recv, n_send, n_recv, x_send, x_recv,
    p_send, p_recv, r_send, r_recv, g_send, g_recv, e_send, e_recv,
):
    c, core, z, xl = place()
    ox = 1 - xl
    cx = ctx_id(ox, z, core)
    sib = ctx_id(xl, z, 1 - core)
    right = ctx_id(xl, z + 1, core)
    left = ctx_id(xl, z + N_Z - 1, core)
    rows = placed.shape[0]
    half = rows // 2
    mine = pl.ds(pl.multiple_of(xl * HEAD_DIM, HEAD_DIM), HEAD_DIM)
    other = pl.ds(pl.multiple_of(ox * HEAD_DIM, HEAD_DIM), HEAD_DIM)
    top, bottom = pl.ds(0, half), pl.ds(half, half)

    order = [(dz, x) for dz in (2, 1, 3, 0) for x in (ox, xl)]
    loads = []
    for j, (dz, x) in enumerate(order):
        copy = pltpu.make_async_copy(dkv.at[ctx_id(x, z + dz, core)], own.at[j], load_sem.at[j])
        copy.start()
        loads.append(copy)

    entry_barrier(n_ctx, 1, c, 0)
    sends = []

    def go(copy):
        copy.start()
        sends.append(copy)

    for j, (dz, x) in enumerate(order):
        go(remote(dkv.at[ctx_id(x, z + dz, 1 - core)], sb.at[j], s_send.at[j], s_recv.at[j], ctx=sib))
    go(remote(dq2.at[ox], gdq, x_send.at[0], x_recv.at[0], ctx=cx))
    go(remote(o2.at[ox], go_in, x_send.at[1], x_recv.at[1], ctx=cx))

    def chip_sum(j):
        loads[j].wait()
        remote(dkv.at[0], sb.at[j], s_send.at[j], s_recv.at[j], ctx=sib).wait_recv()

    def pair(j, at):
        return own[j, at, :].astype(F32) + sb[j, at, :].astype(F32)

    for e in range(2):
        chip_sum(e)
        part[e] = pair(e, pl.ds(0, rows)).astype(BF16)
        go(remote(part.at[e, top], far_l.at[e], f_send.at[e], f_recv.at[e], ctx=right))
        go(remote(part.at[e, bottom], far_r.at[e], f_send.at[2 + e], f_recv.at[2 + e], ctx=left))
    for e in range(2):
        chip_sum(2 + e)
        part[2 + e, bottom, :] = pair(2 + e, bottom).astype(BF16)
        go(remote(part.at[2 + e, bottom], in_l.at[e, bottom], n_send.at[e], n_recv.at[e], ctx=right))
        chip_sum(4 + e)
        part[4 + e, top, :] = pair(4 + e, top).astype(BF16)
        go(remote(part.at[4 + e, top], in_r.at[e, top], n_send.at[2 + e], n_recv.at[2 + e], ctx=left))
    for e in range(2):
        remote(part.at[e, top], far_l.at[e], f_send.at[e], f_recv.at[e], ctx=left).wait_recv()
        part[2 + e, top, :] = (pair(2 + e, top) + far_l[e].astype(F32)).astype(BF16)
        go(remote(part.at[2 + e, top], in_l.at[e, top], n_send.at[4 + e], n_recv.at[4 + e], ctx=right))
        remote(part.at[e, bottom], far_r.at[e], f_send.at[2 + e], f_recv.at[2 + e], ctx=right).wait_recv()
        part[4 + e, bottom, :] = (pair(4 + e, bottom) + far_r[e].astype(F32)).astype(BF16)
        go(remote(part.at[4 + e, bottom], in_r.at[e, bottom], n_send.at[6 + e], n_recv.at[6 + e], ctx=left))

    vis = placed.shape[1]
    width = attn_out.shape[1]
    vis_half = vis // 2
    n_chip = n_ctx // 2
    chunk = vis_half // n_chip
    chip = c // 2
    own_rows = pl.ds(pl.multiple_of(core * vis_half, vis_half), vis_half)
    sib_rows = pl.ds(pl.multiple_of((1 - core) * vis_half, vis_half), vis_half)

    def chunk_at(g):
        return pl.ds(pl.multiple_of(g * chunk, chunk), chunk)

    def final_at(g):
        return pl.ds(pl.multiple_of(core * vis_half + g * chunk, chunk), chunk)

    def conn_start(i):
        grads = qkv_grad[i]
        cs_send[i] = jnp.dot(placed_t[sib_rows, :], grads, preferred_element_type=F32).astype(BF16)
        go(remote(cs_send.at[i], cs_recv.at[i], p_send.at[i], p_recv.at[i], ctx=sib))
        mine_sum[i] = jnp.dot(placed_t[own_rows, :], grads, preferred_element_type=F32)

    def conn_scatter(i):
        remote(cs_send.at[i], cs_recv.at[i], p_send.at[i], p_recv.at[i], ctx=sib).wait_recv()
        total = mine_sum[i] + cs_recv[i].astype(F32)
        mine_sum[i] = total
        rs_out[i] = total.astype(BF16)
        for k in range(1, n_chip):
            g = lax.rem(chip + k, n_chip)
            go(remote(rs_out.at[i, chunk_at(g)], rs_in.at[i, k], r_send.at[i, k], r_recv.at[i, k], ctx=g * 2 + core))

    def conn_gather(i):
        total = mine_sum[i, chunk_at(chip), :]
        for k in range(1, n_chip):
            g = lax.rem(chip + n_chip - k, n_chip)
            remote(rs_out.at[i, chunk_at(g)], rs_in.at[i, k], r_send.at[i, k], r_recv.at[i, k], ctx=g * 2 + core).wait_recv()
            total = total + rs_in[i, k].astype(F32)
        cg[i, final_at(chip), :] = total.astype(BF16)
        for k in range(1, n_chip):
            g = lax.rem(chip + k, n_chip)
            ref = cg.at[i, final_at(chip)]
            go(remote(ref, ref, g_send.at[i, k], g_recv.at[i, k], ctx=g * 2 + core))

    def conn_share(i):
        for k in range(1, n_chip):
            g = lax.rem(chip + n_chip - k, n_chip)
            ref = cg.at[i, final_at(g)]
            remote(ref, ref, g_send.at[i, k], g_recv.at[i, k], ctx=g * 2 + core).wait_recv()
        ref = cg.at[i, own_rows]
        go(remote(ref, ref, e_send.at[i], e_recv.at[i], ctx=sib))

    def conn_finish(i):
        cols = slice(i * width, (i + 1) * width)
        conn[own_rows, cols] = cg[i, own_rows, :].astype(F32)
        ref = cg.at[i, sib_rows]
        remote(ref, ref, e_send.at[i], e_recv.at[i], ctx=sib).wait_recv()
        conn[sib_rows, cols] = cg[i, sib_rows, :].astype(F32)

    placed_t[...] = placed[...].T
    remote(dq2.at[ox], gdq, x_send.at[0], x_recv.at[0], ctx=cx).wait_recv()
    qkv_grad[0, :, mine] = dq2[xl]
    qkv_grad[0, :, other] = gdq[...]
    remote(o2.at[ox], go_in, x_send.at[1], x_recv.at[1], ctx=cx).wait_recv()
    attn_out[:, mine] = o2[xl]
    attn_out[:, other] = go_in[...]

    for e in range(2):
        j = 6 + e
        chip_sum(j)
        for n, buf, at, src in (
            (e, in_l, bottom, left), (2 + e, in_r, top, right), (4 + e, in_l, top, left), (6 + e, in_r, bottom, right)
        ):
            remote(part.at[2 + e, top], buf.at[e, at], n_send.at[n], n_recv.at[n], ctx=src).wait_recv()
        res[e] = (pair(j, pl.ds(0, rows)) + in_l[e].astype(F32) + in_r[e].astype(F32)).astype(BF16)
        if e == 0:
            go(remote(res.at[0], gx, x_send.at[2], x_recv.at[2], ctx=cx))
            conn_start(0)
            conn_scatter(0)
    remote(res.at[0], gx, x_send.at[2], x_recv.at[2], ctx=cx).wait_recv()
    for i in range(2):
        at = slice(i * HEAD_DIM, (i + 1) * HEAD_DIM)
        qkv_grad[1 + i, :, mine] = res[1, :, at]
        qkv_grad[1 + i, :, other] = gx[:, at]
    conn_start(1)
    conn_start(2)
    conn_scatter(1)
    conn_scatter(2)
    for i in range(3):
        conn_gather(i)
    for i in range(3):
        conn_share(i)
    for i in range(3):
        conn_finish(i)
    for copy in sends:
        copy.wait_send()


def local(base_qkv, frames, frame_block, frame_slot, frame_live, start_block, conn_w, d_out):
    n_ctx = lax.axis_size("ctx")
    n_tp = lax.axis_size("tp")
    _, rows, width = base_qkv.shape
    vis = frames.shape[2]
    pw = vis // n_tp
    half = rows // 2
    two = 2 * HEAD_DIM
    piece = FRAME_TOK + CODE_ROWS
    vmem = pl.BlockSpec(memory_space=pltpu.VMEM)
    smem = pl.BlockSpec(memory_space=pltpu.SMEM)
    hbm = pl.BlockSpec(memory_space=pl.ANY)
    dma = pltpu.SemaphoreType.DMA

    def struct(shape, dtype=BF16):
        return jax.ShapeDtypeStruct(shape, dtype)

    def params(n):
        return pltpu.CompilerParams(collective_id=n, has_side_effects=True, vmem_limit_bytes=VMEM_LIMIT)

    placed, q2, do2, kv = pl.pallas_call(
        lambda *refs: gather_kernel(n_ctx, n_tp, *refs),
        out_shape=(
            struct((rows, vis)), struct((2, rows, HEAD_DIM)), struct((2, rows, HEAD_DIM)),
            struct((n_ctx, rows, two)),
        ),
        in_specs=[smem, smem, smem, vmem, hbm, hbm, vmem],
        out_specs=(vmem, vmem, vmem, vmem),
        scratch_shapes=[
            pltpu.VMEM((n_tp, piece, pw), BF16),
            pltpu.VMEM((n_tp, piece, pw), BF16),
            pltpu.VMEM((n_ctx, piece, pw), BF16),
            pltpu.VMEM((n_ctx, piece, pw), BF16),
            pltpu.VMEM((3, rows, width), BF16),
            pltpu.VMEM((vis, 3 * width), BF16),
            pltpu.VMEM((3, rows, width), BF16),
            pltpu.VMEM((rows, two), BF16),
            pltpu.VMEM((rows, HEAD_DIM), BF16),
            pltpu.VMEM((rows, HEAD_DIM), BF16),
            dma((2,)), dma((n_tp,)), dma((n_tp,)), dma((n_ctx,)), dma((n_ctx,)), dma((n_tp,)), dma((n_tp,)),
            dma((3,)), dma((3,)), dma((8,)), dma((8,)), dma((10,)), dma((10,)),
        ],
        compiler_params=params(0),
        name="gather",
    )(frame_block, frame_slot, frame_live, frames, base_qkv, conn_w.reshape(vis, 3 * width), d_out)

    o2, dq2, dkv = pl.pallas_call(
        attention_kernel,
        out_shape=(
            struct((2, rows, HEAD_DIM)), struct((2, rows, HEAD_DIM)), struct((n_ctx, rows, two)),
        ),
        in_specs=[smem, vmem, vmem, vmem],
        out_specs=(vmem, vmem, vmem),
        scratch_shapes=[
            pltpu.VMEM((n_ctx * rows, two), F32),
            pltpu.VMEM((HEAD_DIM, rows), F32),
            pltpu.VMEM((1, rows), F32),
            pltpu.VMEM((1, rows), F32),
        ],
        compiler_params=pltpu.CompilerParams(vmem_limit_bytes=VMEM_LIMIT),
        name="attention",
    )(start_block, q2, do2, kv)

    vis_half = vis // 2
    n_chip = n_ctx // 2
    attn_out, qkv_grad, conn = pl.pallas_call(
        lambda *refs: reduce_kernel(n_ctx, *refs),
        out_shape=(struct((rows, width)), struct((3, rows, width)), struct((vis, 3 * width), F32)),
        in_specs=[hbm, vmem, vmem, vmem],
        out_specs=(vmem, vmem, vmem),
        scratch_shapes=[
            pltpu.VMEM((8, rows, two), BF16),
            pltpu.VMEM((8, rows, two), BF16),
            pltpu.VMEM((6, rows, two), BF16),
            pltpu.VMEM((2, half, two), BF16),
            pltpu.VMEM((2, half, two), BF16),
            pltpu.VMEM((2, rows, two), BF16),
            pltpu.VMEM((2, rows, two), BF16),
            pltpu.VMEM((2, rows, two), BF16),
            pltpu.VMEM((rows, two), BF16),
            pltpu.VMEM((rows, HEAD_DIM), BF16),
            pltpu.VMEM((rows, HEAD_DIM), BF16),
            pltpu.VMEM((vis, rows), BF16),
            pltpu.VMEM((3, vis_half, width), BF16),
            pltpu.VMEM((3, vis_half, width), BF16),
            pltpu.VMEM((3, vis_half, width), F32),
            pltpu.VMEM((3, vis_half, width), BF16),
            pltpu.VMEM((3, n_chip, vis_half // n_chip, width), BF16),
            pltpu.VMEM((3, vis, width), BF16),
            dma((8,)), dma((8,)), dma((8,)), dma((4,)), dma((4,)), dma((8,)), dma((8,)), dma((3,)), dma((3,)),
            dma((3,)), dma((3,)), dma((3, n_chip)), dma((3, n_chip)), dma((3, n_chip)), dma((3, n_chip)),
            dma((3,)), dma((3,)),
        ],
        compiler_params=params(1),
        name="reduce",
    )(dkv, dq2, o2, placed)
    return (attn_out, qkv_grad, conn.reshape(vis, 3, width))


def solution(mesh):
    return jax.shard_map(
        local,
        mesh=mesh,
        in_specs=(
            P(None, "ctx", "tp"),
            P(("ctx", "tp"), None, None),
            P(("ctx", "tp")),
            P(("ctx", "tp")),
            P(("ctx", "tp")),
            P(),
            P(None, None, "tp"),
            P("ctx", "tp"),
        ),
        out_specs=(P("ctx", "tp"), P(None, "ctx", "tp"), P(None, None, "tp")),
        check_vma=False,
    )
```

```python
import math

import jax
import jax.numpy as jnp
from jax import lax
from jax.experimental import pallas as pl
from jax.experimental.pallas import tpu as pltpu
from jax.sharding import PartitionSpec as P

HEAD_DIM = 128
FRAME_TOK = 32
MASK_BLK = 128
CODE_ROWS = 16
N_Z = 4
MASKED = -1e30
MESH = pl.DeviceIdType.MESH
F32 = jnp.float32
BF16 = jnp.bfloat16
VMEM_LIMIT = 20 * 1024 * 1024

NN = (((1,), (0,)), ((), ()))
TN = (((0,), (0,)), ((), ()))


def place():
    c = lax.axis_index("ctx")
    core = c % 2
    z = (c // 2) % N_Z
    xl = c // (2 * N_Z)
    return c, core, z, xl


def ctx_id(xl, z, core):
    return xl * (2 * N_Z) + lax.rem(z, N_Z) * 2 + core


def entry_barrier(n_ctx, n_tp, c, t):
    barrier = pltpu.get_barrier_semaphore()
    for k in range(1, n_tp):
        pl.semaphore_signal(barrier, inc=1, device_id={"tp": lax.rem(t + k, n_tp)}, device_id_type=MESH)
    for k in range(1, n_ctx):
        pl.semaphore_signal(barrier, inc=1, device_id={"ctx": lax.rem(c + k, n_ctx)}, device_id_type=MESH)
    pl.semaphore_wait(barrier, n_tp - 1 + n_ctx - 1)


def remote(src, dst, send, recv, **where):
    return pltpu.make_async_remote_copy(
        src_ref=src, dst_ref=dst, send_sem=send, recv_sem=recv, device_id=where, device_id_type=MESH
    )


def gather_kernel(
    n_ctx, n_tp, fb, fs, fl, frames, base_hbm, w_hbm, dout,
    placed, q2, do2, kv,
    s_a, r_a, s_b, r_b, base, w, qkv, xs, xq, xd,
    load_sem, a_send, a_recv, b_send, b_recv, c_send, c_recv,
    x_send, x_recv, z_send, z_recv, s_send, s_recv,
):
    c, core, z, xl = place()
    t = lax.axis_index("tp")
    pw = frames.shape[2] // n_tp
    rows = placed.shape[0]
    half = rows // 2
    ox = 1 - xl
    cx = ctx_id(ox, z, core)
    sib = ctx_id(xl, z, 1 - core)
    mine = pl.ds(pl.multiple_of(xl * HEAD_DIM, HEAD_DIM), HEAD_DIM)
    other = pl.ds(pl.multiple_of(ox * HEAD_DIM, HEAD_DIM), HEAD_DIM)

    load_w = pltpu.make_async_copy(w_hbm, w, load_sem.at[0])
    load_b = pltpu.make_async_copy(base_hbm, base, load_sem.at[1])
    load_w.start()
    load_b.start()

    code = jnp.where(fl[0] == 1, fb[0] * (rows // FRAME_TOK) + fs[0] + 1, 0).astype(F32)
    code_rows = jnp.full((CODE_ROWS, pw), code, F32).astype(BF16)
    for p in range(n_tp):
        s_a[p, :FRAME_TOK, :] = frames[0, :, p * pw:(p + 1) * pw]
        s_a[p, FRAME_TOK:, :] = code_rows
    xd[...] = dout[:, other]
    do2[xl] = dout[:, mine]

    entry_barrier(n_ctx, n_tp, c, t)

    sends = []

    def go(copy):
        copy.start()
        sends.append(copy)

    for k in range(1, n_tp):
        p = lax.rem(t + k, n_tp)
        go(remote(s_a.at[p], r_a.at[t], a_send.at[k], a_recv.at[k], tp=p))
    r_a[t] = s_a[t]
    for k in range(1, n_tp):
        p = lax.rem(t + n_tp - k, n_tp)
        remote(s_a.at[p], r_a.at[p], a_send.at[k], a_recv.at[k], tp=p).wait_recv()

    slots = rows // FRAME_TOK
    pieces = r_a[...].astype(F32)
    codes = pieces[:, FRAME_TOK:FRAME_TOK + 1, :]
    for k in range(n_ctx):
        d = lax.rem(c + k, n_ctx)
        low = (d * slots).astype(F32)
        hit = (codes > low) & (codes < low + (slots + 0.5))
        s_b[k] = jnp.sum(jnp.where(hit, pieces, 0.0), axis=0).astype(BF16)
        if k:
            go(remote(s_b.at[k], r_b.at[c], b_send.at[k], b_recv.at[k], ctx=d))
    r_b[c] = s_b[0]
    for k in range(1, n_ctx):
        d = lax.rem(c + n_ctx - k, n_ctx)
        remote(s_b.at[k], r_b.at[d], b_send.at[k], b_recv.at[k], ctx=d).wait_recv()

    arrived = r_b[...].astype(F32)
    codes = arrived[:, FRAME_TOK:FRAME_TOK + 1, :]
    rows_in = arrived[:, :FRAME_TOK, :]
    y = t // 2
    xh = t % 2

    def tp_id(y_at, x_at):
        return lax.rem(y_at, n_tp // 2) * 2 + x_at

    def piece(p, first, count):
        return placed.at[pl.ds(first, count), pl.ds(pl.multiple_of(p * pw, pw), pw)]

    if n_tp > 1:
        n_y = n_tp // 2
        up, up_x = tp_id(y + 1, xh), tp_id(y + 1, 1 - xh)
        down, down_x = tp_id(y + n_y - 1, xh), tp_id(y + n_y - 1, 1 - xh)
        far, far_x = tp_id(y + 2, xh), tp_id(y + 2, 1 - xh)
        xp = tp_id(y, 1 - xh)

    def c_copy(r, n, p, first, count, to):
        ref = piece(p, first, count)
        return remote(ref, ref, c_send.at[r, n], c_recv.at[r, n], tp=to)

    for r in range(2):
        for s in range(r * slots // 2, (r + 1) * slots // 2):
            want = (c * slots + (s + 1)).astype(F32)
            piece(t, s * FRAME_TOK, FRAME_TOK)[...] = jnp.sum(
                jnp.where(codes == want, rows_in, 0.0), axis=0
            ).astype(BF16)
        if n_tp > 1:
            at = r * half
            go(c_copy(r, 2, t, at, half, xp))
            go(c_copy(r, 0, t, at, half, up))
            go(c_copy(r, 1, t, at, half, down))

    def gather_pieces(r):
        at, quarter = r * half, half // 2
        low_at = at + quarter
        c_copy(r, 2, xp, at, half, xp).wait_recv()
        go(c_copy(r, 3, xp, at, half, up))
        go(c_copy(r, 4, xp, at, half, down))
        c_copy(r, 0, down, at, half, down).wait_recv()
        go(c_copy(r, 5, down, at, quarter, up))
        c_copy(r, 1, up, at, half, up).wait_recv()
        go(c_copy(r, 6, up, low_at, quarter, down))
        c_copy(r, 3, down_x, at, half, down).wait_recv()
        go(c_copy(r, 7, down_x, at, quarter, up))
        c_copy(r, 4, up_x, at, half, up).wait_recv()
        go(c_copy(r, 8, up_x, low_at, quarter, down))
        c_copy(r, 5, far, at, quarter, down).wait_recv()
        c_copy(r, 6, far, low_at, quarter, up).wait_recv()
        c_copy(r, 7, far_x, at, quarter, down).wait_recv()
        c_copy(r, 8, far_x, low_at, quarter, up).wait_recv()

    right = ctx_id(xl, z + 1, core)
    left = ctx_id(xl, z + N_Z - 1, core)
    opp = ctx_id(xl, z + 2, core)
    right_x = ctx_id(ox, z + 1, core)
    left_x = ctx_id(ox, z + N_Z - 1, core)
    opp_x = ctx_id(ox, z + 2, core)

    def unit(i, r):
        return kv.at[i, pl.ds(r * half, half)]

    def to_right(i, r, n):
        go(remote(unit(i, r), unit(i, r), z_send.at[0, n], z_recv.at[0, n], ctx=right))

    def to_left(i, r, n):
        go(remote(unit(i, r), unit(i, r), z_send.at[1, n], z_recv.at[1, n], ctx=left))

    def to_sib(i, r, n):
        go(remote(unit(i, r), unit(i, r), s_send.at[r, n], s_recv.at[r, n], ctx=sib))

    def from_left(i, r, n):
        remote(unit(i, r), unit(i, r), z_send.at[0, n], z_recv.at[0, n], ctx=left).wait_recv()

    def from_right(i, r, n):
        remote(unit(i, r), unit(i, r), z_send.at[1, n], z_recv.at[1, n], ctx=right).wait_recv()

    def from_partner(r):
        remote(xs.at[r], unit(cx, r), x_send.at[r], x_recv.at[r], ctx=cx).wait_recv()

    def project(i, r):
        at = slice(r * half, (r + 1) * half)
        term = jnp.dot(placed[at, :], w[i], preferred_element_type=F32)
        qkv[i, at, :] = (base[i, at, :].astype(F32) + term).astype(BF16)

    load_w.wait()
    load_b.wait()
    for r in range(2):
        at = slice(r * half, (r + 1) * half)
        if n_tp > 1:
            gather_pieces(r)
        project(1, r)
        project(2, r)
        xs[r, :, :HEAD_DIM] = qkv[1, at, other]
        xs[r, :, HEAD_DIM:] = qkv[2, at, other]
        kv[c, at, :HEAD_DIM] = qkv[1, at, mine]
        kv[c, at, HEAD_DIM:] = qkv[2, at, mine]
        go(remote(xs.at[r], unit(c, r), x_send.at[r], x_recv.at[r], ctx=cx))
        to_right(c, r, r)
        to_left(c, r, r)
        to_sib(c, r, 0)
    from_partner(0)
    to_right(cx, 0, 2)
    to_left(cx, 0, 2)
    to_sib(cx, 0, 1)
    project(0, 0)
    project(0, 1)
    xq[...] = qkv[0, :, other]
    q2[xl] = qkv[0, :, mine]
    from_partner(1)
    to_right(cx, 1, 3)
    to_left(cx, 1, 3)
    to_sib(cx, 1, 1)
    go(remote(xq, q2.at[xl], x_send.at[2], x_recv.at[2], ctx=cx))
    go(remote(xd, do2.at[xl], x_send.at[3], x_recv.at[3], ctx=cx))
    from_left(left, 0, 0)
    to_right(left, 0, 4)
    to_sib(left, 0, 2)
    from_right(right, 0, 0)
    to_sib(right, 0, 3)
    from_left(left, 1, 1)
    to_sib(left, 1, 2)
    from_right(right, 1, 1)
    to_left(right, 1, 4)
    to_sib(right, 1, 3)
    from_left(left_x, 0, 2)
    to_right(left_x, 0, 5)
    to_sib(left_x, 0, 4)
    from_right(right_x, 0, 2)
    to_sib(right_x, 0, 5)
    from_left(left_x, 1, 3)
    to_sib(left_x, 1, 4)
    from_right(right_x, 1, 3)
    to_left(right_x, 1, 5)
    to_sib(right_x, 1, 5)
    from_left(opp, 0, 4)
    to_sib(opp, 0, 6)
    from_right(opp, 1, 4)
    to_sib(opp, 1, 6)
    from_left(opp_x, 0, 5)
    to_sib(opp_x, 0, 7)
    from_right(opp_x, 1, 5)
    to_sib(opp_x, 1, 7)

    remote(xq, q2.at[ox], x_send.at[2], x_recv.at[2], ctx=cx).wait_recv()
    remote(xd, do2.at[ox], x_send.at[3], x_recv.at[3], ctx=cx).wait_recv()
    sc = 1 - core
    theirs = [ctx_id(x, z + dz, sc) for x, dz in ((xl, 0), (ox, 0), (xl, 3), (xl, 1), (ox, 3), (ox, 1), (xl, 2), (ox, 2))]
    for n, i in enumerate(theirs):
        for r in range(2):
            remote(unit(i, r), unit(i, r), s_send.at[r, n], s_recv.at[r, n], ctx=sib).wait_recv()
    for copy in sends:
        copy.wait_send()


def attention_kernel(
    start, q2, do2, kv, o2, dq2, dkv, dkv_acc, acc, m_ref, l_ref
):
    c, core, z, xl = place()
    lower = lax.rem(c, 2 * N_Z)
    n_blk, rows, _ = kv.shape
    mask_per = rows // MASK_BLK
    scale = 1.0 / math.sqrt(HEAD_DIM)
    scale2 = scale * math.log2(math.e)

    def window(blk):
        first = start[blk * mask_per]
        last = start[blk * mask_per + mask_per - 1]
        low = jnp.minimum(first // mask_per, blk)
        clear = jnp.minimum((last + mask_per - 1) // mask_per, blk)
        return low, clear

    low_hi = window(lower + 2 * N_Z)[0]

    for qi in (1, 0):
        blk = lower + 2 * N_Z * qi
        q0 = blk * rows
        queries = q2[qi]
        out_grad = do2[qi]
        queries_t = queries.astype(F32).T.astype(BF16)
        grad_t = out_grad.astype(F32).T.astype(BF16)
        low, clear = window(blk)
        q_start = jnp.concatenate(
            [jnp.full((1, MASK_BLK), start[blk * mask_per + i] * MASK_BLK, jnp.int32) for i in range(mask_per)], axis=1
        )

        def allowed(b):
            key_pos = b * rows + lax.broadcasted_iota(jnp.int32, (rows, rows), 0)
            q_pos = q0 + lax.broadcasted_iota(jnp.int32, (rows, rows), 1)
            return (key_pos <= q_pos) & (key_pos >= q_start)

        m_ref[...] = jnp.full_like(m_ref, MASKED)
        l_ref[...] = jnp.zeros_like(l_ref)
        acc[...] = jnp.zeros_like(acc)

        def forward(blocks, masked):
            scores = [
                lax.dot_general(kv[b, :, :HEAD_DIM], queries_t, NN, preferred_element_type=F32) * scale2 for b in blocks
            ]
            if masked:
                scores = [jnp.where(allowed(b), s, MASKED) for b, s in zip(blocks, scores)]
            m_old = m_ref[...]
            m_new = m_old
            for s in scores:
                m_new = jnp.maximum(m_new, jnp.max(s, axis=0, keepdims=True))
            alpha = jnp.exp2(m_old - m_new)
            m_ref[...] = m_new
            total = l_ref[...] * alpha
            out = acc[...] * alpha
            for b, s in zip(blocks, scores):
                p = jnp.exp2(s - m_new)
                total = total + jnp.sum(p, axis=0, keepdims=True)
                out = out + lax.dot_general(kv[b, :, HEAD_DIM:], p.astype(BF16), TN, preferred_element_type=F32)
            l_ref[...] = total
            acc[...] = out

        def sweep(lo, hi, step):
            pairs = (hi - lo) // 2

            def body(i, carry):
                step([lo + i * 2, lo + i * 2 + 1], False)
                return carry

            def rest(b, carry):
                step([b], False)
                return carry

            lax.fori_loop(0, pairs, body, 0)
            lax.fori_loop(lo + pairs * 2, hi, rest, 0)

        def masked_sweep(lo, hi, step):
            def body(b, carry):
                step([b], True)
                return carry
            lax.fori_loop(lo, hi, body, 0)

        forward([blk], True)
        sweep(clear, blk, forward)
        masked_sweep(low, clear, forward)

        total = l_ref[...]
        out_t = (acc[...] / total).astype(BF16).astype(F32)
        o2[qi] = out_t.T.astype(BF16)
        row_dot = jnp.sum(out_t * out_grad.astype(F32).T, axis=0, keepdims=True)
        log_norm = m_ref[...] + jnp.log2(total)
        acc[...] = jnp.zeros_like(acc)

        def backward(blocks, masked):
            dq = acc[...]
            tiles = []
            for b in blocks:
                s = lax.dot_general(kv[b, :, :HEAD_DIM], queries_t, NN, preferred_element_type=F32)
                dp = lax.dot_general(kv[b, :, HEAD_DIM:], grad_t, NN, preferred_element_type=F32)
                tiles.append((b, s, dp))
            for b, s, dp in tiles:
                p = jnp.exp2(s * scale2 - log_norm)
                if masked:
                    p = jnp.where(allowed(b), p, 0.0)
                ds = (p * (dp - row_dot) * scale).astype(BF16)
                at = pl.ds(pl.multiple_of(b * rows, rows), rows)
                dk = jnp.dot(ds, queries, preferred_element_type=F32)
                dv = jnp.dot(p.astype(BF16), out_grad, preferred_element_type=F32)
                if qi == 1:
                    dkv_acc[at, :HEAD_DIM] = dk
                    dkv_acc[at, HEAD_DIM:] = dv
                else:
                    dkv_acc[at, :HEAD_DIM] += dk
                    dkv_acc[at, HEAD_DIM:] += dv
                dq = dq + lax.dot_general(kv[b, :, :HEAD_DIM], ds, TN, preferred_element_type=F32)
            acc[...] = dq

        if qi == 0:
            def clean(b, carry):
                dkv_acc[pl.ds(pl.multiple_of(b * rows, rows), rows), :] = jnp.zeros((rows, 2 * HEAD_DIM), F32)
                return carry
            lax.fori_loop(low, jnp.minimum(low_hi, blk + 1), clean, 0)
        backward([blk], True)
        sweep(clear, blk, backward)
        masked_sweep(low, clear, backward)
        dq2[qi] = acc[...].T.astype(BF16)

    low_lo = window(lower)[0]

    def write(b, carry):
        at = pl.ds(pl.multiple_of(b * rows, rows), rows)
        dkv[b] = dkv_acc[at, :].astype(BF16)
        return carry

    def blank(b, carry):
        dkv[b] = jnp.zeros((rows, 2 * HEAD_DIM), BF16)
        return carry

    mid = jnp.maximum(low_hi, lower + 1)
    lax.fori_loop(0, low_lo, blank, 0)
    lax.fori_loop(low_lo, lower + 1, write, 0)
    lax.fori_loop(lower + 1, mid, blank, 0)
    lax.fori_loop(mid, lower + 2 * N_Z + 1, write, 0)
    lax.fori_loop(lower + 2 * N_Z + 1, n_blk, blank, 0)


def reduce_kernel(
    n_ctx, dkv, dq2, o2, placed,
    attn_out, qkv_grad, cg,
    sb, part, far_l, far_r, in_l, in_r, res, gx, gdq, go_in,
    placed_t, cs_send, cs_recv, mine_sum, rs_out, rs_in,
    s_send, s_recv, f_send, f_recv, n_send, n_recv, x_send, x_recv,
    p_send, p_recv, r_send, r_recv, g_send, g_recv, e_send, e_recv,
):
    c, core, z, xl = place()
    ox = 1 - xl
    cx = ctx_id(ox, z, core)
    sib = ctx_id(xl, z, 1 - core)
    right = ctx_id(xl, z + 1, core)
    left = ctx_id(xl, z + N_Z - 1, core)
    rows = placed.shape[0]
    half = rows // 2
    mine = pl.ds(pl.multiple_of(xl * HEAD_DIM, HEAD_DIM), HEAD_DIM)
    other = pl.ds(pl.multiple_of(ox * HEAD_DIM, HEAD_DIM), HEAD_DIM)
    top, bottom = pl.ds(0, half), pl.ds(half, half)

    order = [(dz, x) for dz in (2, 1, 3, 0) for x in (ox, xl)]
    entry_barrier(n_ctx, 1, c, 0)
    sends = []

    def go(copy):
        copy.start()
        sends.append(copy)

    for j, (dz, x) in enumerate(order):
        go(remote(dkv.at[ctx_id(x, z + dz, 1 - core)], sb.at[j], s_send.at[j], s_recv.at[j], ctx=sib))
    go(remote(dq2.at[ox], gdq, x_send.at[0], x_recv.at[0], ctx=cx))
    go(remote(o2.at[ox], go_in, x_send.at[1], x_recv.at[1], ctx=cx))

    def chip_sum(j):
        remote(dkv.at[0], sb.at[j], s_send.at[j], s_recv.at[j], ctx=sib).wait_recv()

    def pair(j, at):
        dz, x = order[j]
        return dkv[ctx_id(x, z + dz, core), at, :].astype(F32) + sb[j, at, :].astype(F32)

    for e in range(2):
        chip_sum(e)
        part[e] = pair(e, pl.ds(0, rows)).astype(BF16)
        go(remote(part.at[e, top], far_l.at[e], f_send.at[e], f_recv.at[e], ctx=right))
        go(remote(part.at[e, bottom], far_r.at[e], f_send.at[2 + e], f_recv.at[2 + e], ctx=left))
    for e in range(2):
        chip_sum(2 + e)
        part[2 + e, bottom, :] = pair(2 + e, bottom).astype(BF16)
        go(remote(part.at[2 + e, bottom], in_l.at[e, bottom], n_send.at[e], n_recv.at[e], ctx=right))
        chip_sum(4 + e)
        part[4 + e, top, :] = pair(4 + e, top).astype(BF16)
        go(remote(part.at[4 + e, top], in_r.at[e, top], n_send.at[2 + e], n_recv.at[2 + e], ctx=left))
    for e in range(2):
        remote(part.at[e, top], far_l.at[e], f_send.at[e], f_recv.at[e], ctx=left).wait_recv()
        part[2 + e, top, :] = (pair(2 + e, top) + far_l[e].astype(F32)).astype(BF16)
        go(remote(part.at[2 + e, top], in_l.at[e, top], n_send.at[4 + e], n_recv.at[4 + e], ctx=right))
        remote(part.at[e, bottom], far_r.at[e], f_send.at[2 + e], f_recv.at[2 + e], ctx=right).wait_recv()
        part[4 + e, bottom, :] = (pair(4 + e, bottom) + far_r[e].astype(F32)).astype(BF16)
        go(remote(part.at[4 + e, bottom], in_r.at[e, bottom], n_send.at[6 + e], n_recv.at[6 + e], ctx=left))

    vis = placed.shape[1]
    width = attn_out.shape[1]
    vis_half = vis // 2
    n_chip = n_ctx // 2
    chunk = vis_half // n_chip
    chip = c // 2
    own_rows = pl.ds(pl.multiple_of(core * vis_half, vis_half), vis_half)
    sib_rows = pl.ds(pl.multiple_of((1 - core) * vis_half, vis_half), vis_half)

    def chunk_at(g):
        return pl.ds(pl.multiple_of(g * chunk, chunk), chunk)

    def final_at(g):
        return pl.ds(pl.multiple_of(core * vis_half + g * chunk, chunk), chunk)

    def conn_start(i):
        grads = qkv_grad[i]
        cs_send[i] = jnp.dot(placed_t[sib_rows, :], grads, preferred_element_type=F32).astype(BF16)
        go(remote(cs_send.at[i], cs_recv.at[i], p_send.at[i], p_recv.at[i], ctx=sib))
        mine_sum[i] = jnp.dot(placed_t[own_rows, :], grads, preferred_element_type=F32)

    def conn_scatter(i):
        remote(cs_send.at[i], cs_recv.at[i], p_send.at[i], p_recv.at[i], ctx=sib).wait_recv()
        total = mine_sum[i] + cs_recv[i].astype(F32)
        mine_sum[i] = total
        rs_out[i] = total.astype(BF16)
        for k in range(1, n_chip):
            g = lax.rem(chip + k, n_chip)
            go(remote(rs_out.at[i, chunk_at(g)], rs_in.at[i, k], r_send.at[i, k], r_recv.at[i, k], ctx=g * 2 + core))

    def conn_gather(i):
        total = mine_sum[i, chunk_at(chip), :]
        for k in range(1, n_chip):
            g = lax.rem(chip + n_chip - k, n_chip)
            remote(rs_out.at[i, chunk_at(g)], rs_in.at[i, k], r_send.at[i, k], r_recv.at[i, k], ctx=g * 2 + core).wait_recv()
            total = total + rs_in[i, k].astype(F32)
        cg[i, final_at(chip), :] = total.astype(BF16)
        for k in range(1, n_chip):
            g = lax.rem(chip + k, n_chip)
            ref = cg.at[i, final_at(chip)]
            go(remote(ref, ref, g_send.at[i, k], g_recv.at[i, k], ctx=g * 2 + core))

    def conn_share(i):
        for k in range(1, n_chip):
            g = lax.rem(chip + n_chip - k, n_chip)
            ref = cg.at[i, final_at(g)]
            remote(ref, ref, g_send.at[i, k], g_recv.at[i, k], ctx=g * 2 + core).wait_recv()
        ref = cg.at[i, own_rows]
        go(remote(ref, ref, e_send.at[i], e_recv.at[i], ctx=sib))

    def conn_finish(i):
        ref = cg.at[i, sib_rows]
        remote(ref, ref, e_send.at[i], e_recv.at[i], ctx=sib).wait_recv()

    placed_t[...] = placed[...].T
    remote(dq2.at[ox], gdq, x_send.at[0], x_recv.at[0], ctx=cx).wait_recv()
    qkv_grad[0, :, mine] = dq2[xl]
    qkv_grad[0, :, other] = gdq[...]
    remote(o2.at[ox], go_in, x_send.at[1], x_recv.at[1], ctx=cx).wait_recv()
    attn_out[:, mine] = o2[xl]
    attn_out[:, other] = go_in[...]

    for e in range(2):
        j = 6 + e
        chip_sum(j)
        for n, buf, at, src in (
            (e, in_l, bottom, left), (2 + e, in_r, top, right), (4 + e, in_l, top, left), (6 + e, in_r, bottom, right)
        ):
            remote(part.at[2 + e, top], buf.at[e, at], n_send.at[n], n_recv.at[n], ctx=src).wait_recv()
        res[e] = (pair(j, pl.ds(0, rows)) + in_l[e].astype(F32) + in_r[e].astype(F32)).astype(BF16)
        if e == 0:
            go(remote(res.at[0], gx, x_send.at[2], x_recv.at[2], ctx=cx))
            conn_start(0)
            conn_scatter(0)
    remote(res.at[0], gx, x_send.at[2], x_recv.at[2], ctx=cx).wait_recv()
    for i in range(2):
        at = slice(i * HEAD_DIM, (i + 1) * HEAD_DIM)
        qkv_grad[1 + i, :, mine] = res[1, :, at]
        qkv_grad[1 + i, :, other] = gx[:, at]
    conn_start(1)
    conn_start(2)
    conn_scatter(1)
    conn_scatter(2)
    for i in range(3):
        conn_gather(i)
    for i in range(3):
        conn_share(i)
    for i in range(3):
        conn_finish(i)
    for copy in sends:
        copy.wait_send()


def local(base_qkv, frames, frame_block, frame_slot, frame_live, start_block, conn_w, d_out):
    n_ctx = lax.axis_size("ctx")
    n_tp = lax.axis_size("tp")
    _, rows, width = base_qkv.shape
    vis = frames.shape[2]
    pw = vis // n_tp
    half = rows // 2
    two = 2 * HEAD_DIM
    piece = FRAME_TOK + CODE_ROWS
    vmem = pl.BlockSpec(memory_space=pltpu.VMEM)
    smem = pl.BlockSpec(memory_space=pltpu.SMEM)
    hbm = pl.BlockSpec(memory_space=pltpu.HBM)
    dma = pltpu.SemaphoreType.DMA

    def buf(*shape):
        return pltpu.VMEM(shape, BF16)

    def kept(*arrays, space=pltpu.VMEM):
        return [pltpu.with_memory_space_constraint(x, space) for x in arrays]

    def params(n):
        return pltpu.CompilerParams(collective_id=n, has_side_effects=True, vmem_limit_bytes=VMEM_LIMIT)

    placed, q2, do2, kv = pl.pallas_call(
        lambda *refs: gather_kernel(n_ctx, n_tp, *refs),
        out_shape=(
            buf(rows, vis), buf(2, rows, HEAD_DIM), buf(2, rows, HEAD_DIM), buf(n_ctx, rows, two),
        ),
        in_specs=[smem, smem, smem, vmem, hbm, hbm, vmem],
        out_specs=(vmem, vmem, vmem, vmem),
        scratch_shapes=[
            pltpu.VMEM((n_tp, piece, pw), BF16),
            pltpu.VMEM((n_tp, piece, pw), BF16),
            pltpu.VMEM((n_ctx, piece, pw), BF16),
            pltpu.VMEM((n_ctx, piece, pw), BF16),
            pltpu.VMEM((3, rows, width), BF16),
            pltpu.VMEM((3, vis, width), BF16),
            pltpu.VMEM((3, rows, width), BF16),
            pltpu.VMEM((2, half, two), BF16),
            pltpu.VMEM((rows, HEAD_DIM), BF16),
            pltpu.VMEM((rows, HEAD_DIM), BF16),
            dma((2,)), dma((n_tp,)), dma((n_tp,)), dma((n_ctx,)), dma((n_ctx,)), dma((2, 9)), dma((2, 9)),
            dma((4,)), dma((4,)), dma((2, 6)), dma((2, 6)), dma((2, 8)), dma((2, 8)),
        ],
        compiler_params=params(0),
        name="gather",
    )(
        frame_block, frame_slot, frame_live, frames,
        *kept(base_qkv, conn_w.transpose(1, 0, 2), space=pltpu.HBM), d_out,
    )

    o2, dq2, dkv = pl.pallas_call(
        attention_kernel,
        out_shape=(
            buf(2, rows, HEAD_DIM), buf(2, rows, HEAD_DIM), buf(n_ctx, rows, two),
        ),
        in_specs=[smem, vmem, vmem, vmem],
        out_specs=(vmem, vmem, vmem),
        scratch_shapes=[
            pltpu.VMEM((n_ctx * rows, two), F32),
            pltpu.VMEM((HEAD_DIM, rows), F32),
            pltpu.VMEM((1, rows), F32),
            pltpu.VMEM((1, rows), F32),
        ],
        compiler_params=pltpu.CompilerParams(vmem_limit_bytes=VMEM_LIMIT),
        name="attention",
    )(start_block, *kept(q2, do2, kv))

    vis_half = vis // 2
    n_chip = n_ctx // 2
    attn_out, qkv_grad, conn = pl.pallas_call(
        lambda *refs: reduce_kernel(n_ctx, *refs),
        out_shape=(buf(rows, width), buf(3, rows, width), buf(3, vis, width)),
        in_specs=[vmem, vmem, vmem, vmem],
        out_specs=(vmem, vmem, vmem),
        scratch_shapes=[
            pltpu.VMEM((8, rows, two), BF16),
            pltpu.VMEM((6, rows, two), BF16),
            pltpu.VMEM((2, half, two), BF16),
            pltpu.VMEM((2, half, two), BF16),
            pltpu.VMEM((2, rows, two), BF16),
            pltpu.VMEM((2, rows, two), BF16),
            pltpu.VMEM((2, rows, two), BF16),
            pltpu.VMEM((rows, two), BF16),
            pltpu.VMEM((rows, HEAD_DIM), BF16),
            pltpu.VMEM((rows, HEAD_DIM), BF16),
            pltpu.VMEM((vis, rows), BF16),
            pltpu.VMEM((3, vis_half, width), BF16),
            pltpu.VMEM((3, vis_half, width), BF16),
            pltpu.VMEM((3, vis_half, width), F32),
            pltpu.VMEM((3, vis_half, width), BF16),
            pltpu.VMEM((3, n_chip, vis_half // n_chip, width), BF16),
            dma((8,)), dma((8,)), dma((4,)), dma((4,)), dma((8,)), dma((8,)), dma((3,)), dma((3,)),
            dma((3,)), dma((3,)), dma((3, n_chip)), dma((3, n_chip)), dma((3, n_chip)), dma((3, n_chip)),
            dma((3,)), dma((3,)),
        ],
        compiler_params=params(1),
        name="reduce",
    )(*kept(dkv, dq2, o2, placed))
    return (attn_out, qkv_grad, conn.astype(F32).transpose(1, 0, 2))


def solution(mesh):
    return jax.shard_map(
        local,
        mesh=mesh,
        in_specs=(
            P(None, "ctx", "tp"),
            P(("ctx", "tp"), None, None),
            P(("ctx", "tp")),
            P(("ctx", "tp")),
            P(("ctx", "tp")),
            P(),
            P(None, None, "tp"),
            P("ctx", "tp"),
        ),
        out_specs=(P("ctx", "tp"), P(None, "ctx", "tp"), P(None, None, "tp")),
        check_vma=False,
    )
```

```python
import math

import jax
import jax.numpy as jnp
from jax import lax
from jax.experimental import pallas as pl
from jax.experimental.pallas import tpu as pltpu
from jax.sharding import PartitionSpec as P

HEAD_DIM = 128
FRAME_TOK = 32
MASK_BLK = 128
CODE_ROWS = 16
N_Z = 4
MASKED = -1e30
MESH = pl.DeviceIdType.MESH
F32 = jnp.float32
BF16 = jnp.bfloat16
VMEM_LIMIT = 20 * 1024 * 1024

NN = (((1,), (0,)), ((), ()))
TN = (((0,), (0,)), ((), ()))


def place():
    c = lax.axis_index("ctx")
    core = c % 2
    z = (c // 2) % N_Z
    xl = c // (2 * N_Z)
    return c, core, z, xl


def ctx_id(xl, z, core):
    return xl * (2 * N_Z) + lax.rem(z, N_Z) * 2 + core


def entry_barrier(n_ctx, n_tp, c, t):
    barrier = pltpu.get_barrier_semaphore()
    for k in range(1, n_tp):
        pl.semaphore_signal(barrier, inc=1, device_id={"tp": lax.rem(t + k, n_tp)}, device_id_type=MESH)
    for k in range(1, n_ctx):
        pl.semaphore_signal(barrier, inc=1, device_id={"ctx": lax.rem(c + k, n_ctx)}, device_id_type=MESH)
    pl.semaphore_wait(barrier, n_tp - 1 + n_ctx - 1)


def remote(src, dst, send, recv, **where):
    return pltpu.make_async_remote_copy(
        src_ref=src, dst_ref=dst, send_sem=send, recv_sem=recv, device_id=where, device_id_type=MESH
    )


def gather_kernel(
    n_ctx, n_tp, fb, fs, fl, frames_hbm, base_hbm, w_hbm, dout_hbm,
    placed, q2, do2, kv,
    s_a, r_a, s_b, r_b, frames, dout, base, w, qkv, xs, xq, xd,
    load_sem, a_send, a_recv, b_send, b_recv, c_send, c_recv,
    x_send, x_recv, z_send, z_recv, s_send, s_recv,
):
    c, core, z, xl = place()
    t = lax.axis_index("tp")
    pw = frames.shape[2] // n_tp
    rows = placed.shape[0]
    half = rows // 2
    ox = 1 - xl
    cx = ctx_id(ox, z, core)
    sib = ctx_id(xl, z, 1 - core)
    mine = pl.ds(pl.multiple_of(xl * HEAD_DIM, HEAD_DIM), HEAD_DIM)
    other = pl.ds(pl.multiple_of(ox * HEAD_DIM, HEAD_DIM), HEAD_DIM)

    load_f = pltpu.make_async_copy(frames_hbm, frames, load_sem.at[2])
    load_d = pltpu.make_async_copy(dout_hbm, dout, load_sem.at[3])
    load_w = pltpu.make_async_copy(w_hbm, w, load_sem.at[0])
    load_b = pltpu.make_async_copy(base_hbm, base, load_sem.at[1])
    load_f.start()
    load_w.start()
    load_b.start()
    load_d.start()

    code = jnp.where(fl[0] == 1, fb[0] * (rows // FRAME_TOK) + fs[0] + 1, 0).astype(F32)
    code_rows = jnp.full((CODE_ROWS, pw), code, F32).astype(BF16)
    load_f.wait()
    for p in range(n_tp):
        s_a[p, :FRAME_TOK, :] = frames[0, :, p * pw:(p + 1) * pw]
        s_a[p, FRAME_TOK:, :] = code_rows

    entry_barrier(n_ctx, n_tp, c, t)

    sends = []

    def go(copy):
        copy.start()
        sends.append(copy)

    for k in range(1, n_tp):
        p = lax.rem(t + k, n_tp)
        go(remote(s_a.at[p], r_a.at[t], a_send.at[k], a_recv.at[k], tp=p))
    r_a[t] = s_a[t]
    for k in range(1, n_tp):
        p = lax.rem(t + n_tp - k, n_tp)
        remote(s_a.at[p], r_a.at[p], a_send.at[k], a_recv.at[k], tp=p).wait_recv()

    slots = rows // FRAME_TOK
    pieces = r_a[...].astype(F32)
    codes = pieces[:, FRAME_TOK:FRAME_TOK + 1, :]
    for k in range(n_ctx):
        d = lax.rem(c + k, n_ctx)
        low = (d * slots).astype(F32)
        hit = (codes > low) & (codes < low + (slots + 0.5))
        s_b[k] = jnp.sum(jnp.where(hit, pieces, 0.0), axis=0).astype(BF16)
        if k:
            go(remote(s_b.at[k], r_b.at[c], b_send.at[k], b_recv.at[k], ctx=d))
    r_b[c] = s_b[0]
    for k in range(1, n_ctx):
        d = lax.rem(c + n_ctx - k, n_ctx)
        remote(s_b.at[k], r_b.at[d], b_send.at[k], b_recv.at[k], ctx=d).wait_recv()

    arrived = r_b[...].astype(F32)
    codes = arrived[:, FRAME_TOK:FRAME_TOK + 1, :]
    rows_in = arrived[:, :FRAME_TOK, :]
    y = t // 2
    xh = t % 2

    def tp_id(y_at, x_at):
        return lax.rem(y_at, n_tp // 2) * 2 + x_at

    def piece(p, first, count):
        return placed.at[pl.ds(first, count), pl.ds(pl.multiple_of(p * pw, pw), pw)]

    if n_tp > 1:
        n_y = n_tp // 2
        up, up_x = tp_id(y + 1, xh), tp_id(y + 1, 1 - xh)
        down, down_x = tp_id(y + n_y - 1, xh), tp_id(y + n_y - 1, 1 - xh)
        far, far_x = tp_id(y + 2, xh), tp_id(y + 2, 1 - xh)
        xp = tp_id(y, 1 - xh)

    def c_copy(r, n, p, to):
        ref = piece(p, r * half, half)
        return remote(ref, ref, c_send.at[r, n], c_recv.at[r, n], tp=to)

    for r in range(2):
        for s in range(r * slots // 2, (r + 1) * slots // 2):
            want = (c * slots + (s + 1)).astype(F32)
            piece(t, s * FRAME_TOK, FRAME_TOK)[...] = jnp.sum(
                jnp.where(codes == want, rows_in, 0.0), axis=0
            ).astype(BF16)
        if n_tp > 1:
            go(c_copy(r, 0, t, xp))
            go(c_copy(r, 1, t, up))
            go(c_copy(r, 2, t, down))
            go(c_copy(r, 3, t, far))
    if n_tp > 1:
        for r in range(2):
            c_copy(r, 0, xp, xp).wait_recv()
            go(c_copy(r, 4, xp, up))
            go(c_copy(r, 5, xp, down))
            go(c_copy(r, 6, xp, far))

    def wait_pieces(r):
        for n, p in ((1, down), (2, up), (3, far), (4, down_x), (5, up_x), (6, far_x)):
            c_copy(r, n, p, p).wait_recv()

    right = ctx_id(xl, z + 1, core)
    left = ctx_id(xl, z + N_Z - 1, core)
    opp = ctx_id(xl, z + 2, core)
    right_x = ctx_id(ox, z + 1, core)
    left_x = ctx_id(ox, z + N_Z - 1, core)
    opp_x = ctx_id(ox, z + 2, core)

    def unit(i, r):
        return kv.at[i, pl.ds(r * half, half)]

    def to_right(i, r, n):
        go(remote(unit(i, r), unit(i, r), z_send.at[0, n], z_recv.at[0, n], ctx=right))

    def to_left(i, r, n):
        go(remote(unit(i, r), unit(i, r), z_send.at[1, n], z_recv.at[1, n], ctx=left))

    def to_sib(i, r, n):
        go(remote(unit(i, r), unit(i, r), s_send.at[r, n], s_recv.at[r, n], ctx=sib))

    def from_left(i, r, n):
        remote(unit(i, r), unit(i, r), z_send.at[0, n], z_recv.at[0, n], ctx=left).wait_recv()

    def from_right(i, r, n):
        remote(unit(i, r), unit(i, r), z_send.at[1, n], z_recv.at[1, n], ctx=right).wait_recv()

    def from_partner(r):
        remote(xs.at[r], unit(cx, r), x_send.at[r], x_recv.at[r], ctx=cx).wait_recv()

    def project(i, r):
        at = slice(r * half, (r + 1) * half)
        term = jnp.dot(placed[at, :], w[i], preferred_element_type=F32)
        qkv[i, at, :] = (base[i, at, :].astype(F32) + term).astype(BF16)

    load_w.wait()
    load_b.wait()
    for r in range(2):
        at = slice(r * half, (r + 1) * half)
        if n_tp > 1:
            wait_pieces(r)
        project(1, r)
        project(2, r)
        xs[r, :, :HEAD_DIM] = qkv[1, at, other]
        xs[r, :, HEAD_DIM:] = qkv[2, at, other]
        kv[c, at, :HEAD_DIM] = qkv[1, at, mine]
        kv[c, at, HEAD_DIM:] = qkv[2, at, mine]
        go(remote(xs.at[r], unit(c, r), x_send.at[r], x_recv.at[r], ctx=cx))
        to_right(c, r, r)
        to_left(c, r, r)
        to_sib(c, r, 0)
    from_partner(0)
    to_right(cx, 0, 2)
    to_left(cx, 0, 2)
    to_sib(cx, 0, 1)
    project(0, 0)
    project(0, 1)
    xq[...] = qkv[0, :, other]
    q2[xl] = qkv[0, :, mine]
    load_d.wait()
    xd[...] = dout[:, other]
    do2[xl] = dout[:, mine]
    from_partner(1)
    to_right(cx, 1, 3)
    to_left(cx, 1, 3)
    to_sib(cx, 1, 1)
    go(remote(xq, q2.at[xl], x_send.at[2], x_recv.at[2], ctx=cx))
    go(remote(xd, do2.at[xl], x_send.at[3], x_recv.at[3], ctx=cx))
    from_left(left, 0, 0)
    to_right(left, 0, 4)
    to_sib(left, 0, 2)
    from_right(right, 0, 0)
    to_sib(right, 0, 3)
    from_left(left, 1, 1)
    to_sib(left, 1, 2)
    from_right(right, 1, 1)
    to_left(right, 1, 4)
    to_sib(right, 1, 3)
    from_left(left_x, 0, 2)
    to_right(left_x, 0, 5)
    to_sib(left_x, 0, 4)
    from_right(right_x, 0, 2)
    to_sib(right_x, 0, 5)
    from_left(left_x, 1, 3)
    to_sib(left_x, 1, 4)
    from_right(right_x, 1, 3)
    to_left(right_x, 1, 5)
    to_sib(right_x, 1, 5)
    from_left(opp, 0, 4)
    to_sib(opp, 0, 6)
    from_right(opp, 1, 4)
    to_sib(opp, 1, 6)
    from_left(opp_x, 0, 5)
    to_sib(opp_x, 0, 7)
    from_right(opp_x, 1, 5)
    to_sib(opp_x, 1, 7)

    remote(xq, q2.at[ox], x_send.at[2], x_recv.at[2], ctx=cx).wait_recv()
    remote(xd, do2.at[ox], x_send.at[3], x_recv.at[3], ctx=cx).wait_recv()
    sc = 1 - core
    theirs = [ctx_id(x, z + dz, sc) for x, dz in ((xl, 0), (ox, 0), (xl, 3), (xl, 1), (ox, 3), (ox, 1), (xl, 2), (ox, 2))]
    for n, i in enumerate(theirs):
        for r in range(2):
            remote(unit(i, r), unit(i, r), s_send.at[r, n], s_recv.at[r, n], ctx=sib).wait_recv()
    for copy in sends:
        copy.wait_send()


def attention_kernel(
    start, q2, do2, kv, o2, dq2, dk_out, dv_out, dkv_acc, acc, m_ref, l_ref
):
    c, core, z, xl = place()
    lower = lax.rem(c, 2 * N_Z)
    n_blk, rows, _ = kv.shape
    mask_per = rows // MASK_BLK
    scale = 1.0 / math.sqrt(HEAD_DIM)
    scale2 = scale * math.log2(math.e)

    def window(blk):
        first = start[blk * mask_per]
        last = start[blk * mask_per + mask_per - 1]
        low = jnp.minimum(first // mask_per, blk)
        clear = jnp.minimum((last + mask_per - 1) // mask_per, blk)
        return low, clear

    low_hi = window(lower + 2 * N_Z)[0]

    for qi in (1, 0):
        blk = lower + 2 * N_Z * qi
        q0 = blk * rows
        queries = q2[qi]
        out_grad = do2[qi]
        queries_t = queries.astype(F32).T.astype(BF16)
        grad_t = out_grad.astype(F32).T.astype(BF16)
        low, clear = window(blk)
        q_start = jnp.concatenate(
            [jnp.full((1, MASK_BLK), start[blk * mask_per + i] * MASK_BLK, jnp.int32) for i in range(mask_per)], axis=1
        )

        def allowed(b):
            key_pos = b * rows + lax.broadcasted_iota(jnp.int32, (rows, rows), 0)
            q_pos = q0 + lax.broadcasted_iota(jnp.int32, (rows, rows), 1)
            return (key_pos <= q_pos) & (key_pos >= q_start)

        m_ref[...] = jnp.full_like(m_ref, MASKED)
        l_ref[...] = jnp.zeros_like(l_ref)
        acc[...] = jnp.zeros_like(acc)

        def forward(blocks, masked):
            scores = [
                lax.dot_general(kv[b, :, :HEAD_DIM], queries_t, NN, preferred_element_type=F32) * scale2 for b in blocks
            ]
            if masked:
                scores = [jnp.where(allowed(b), s, MASKED) for b, s in zip(blocks, scores)]
            m_old = m_ref[...]
            m_new = m_old
            for s in scores:
                m_new = jnp.maximum(m_new, jnp.max(s, axis=0, keepdims=True))
            alpha = jnp.exp2(m_old - m_new)
            m_ref[...] = m_new
            total = l_ref[...] * alpha
            out = acc[...] * alpha
            for b, s in zip(blocks, scores):
                p = jnp.exp2(s - m_new)
                total = total + jnp.sum(p, axis=0, keepdims=True)
                out = out + lax.dot_general(kv[b, :, HEAD_DIM:], p.astype(BF16), TN, preferred_element_type=F32)
            l_ref[...] = total
            acc[...] = out

        def sweep(lo, hi, step):
            pairs = (hi - lo) // 2

            def body(i, carry):
                step([lo + i * 2, lo + i * 2 + 1], False)
                return carry

            def rest(b, carry):
                step([b], False)
                return carry

            lax.fori_loop(0, pairs, body, 0)
            lax.fori_loop(lo + pairs * 2, hi, rest, 0)

        def masked_sweep(lo, hi, step):
            def body(b, carry):
                step([b], True)
                return carry
            lax.fori_loop(lo, hi, body, 0)

        forward([blk], True)
        sweep(clear, blk, forward)
        masked_sweep(low, clear, forward)

        total = l_ref[...]
        out_t = (acc[...] / total).astype(BF16).astype(F32)
        o2[qi] = out_t.T.astype(BF16)
        row_dot = jnp.sum(out_t * out_grad.astype(F32).T, axis=0, keepdims=True)
        log_norm = m_ref[...] + jnp.log2(total)
        acc[...] = jnp.zeros_like(acc)

        def backward(blocks, masked):
            dq = acc[...]
            tiles = []
            for b in blocks:
                s = lax.dot_general(kv[b, :, :HEAD_DIM], queries_t, NN, preferred_element_type=F32)
                dp = lax.dot_general(kv[b, :, HEAD_DIM:], grad_t, NN, preferred_element_type=F32)
                tiles.append((b, s, dp))
            for b, s, dp in tiles:
                p = jnp.exp2(s * scale2 - log_norm)
                if masked:
                    p = jnp.where(allowed(b), p, 0.0)
                ds = (p * (dp - row_dot) * scale).astype(BF16)
                at = pl.ds(pl.multiple_of(b * rows, rows), rows)
                dk = jnp.dot(ds, queries, preferred_element_type=F32)
                dv = jnp.dot(p.astype(BF16), out_grad, preferred_element_type=F32)
                if qi == 1:
                    dkv_acc[at, :HEAD_DIM] = dk
                    dkv_acc[at, HEAD_DIM:] = dv
                else:
                    dkv_acc[at, :HEAD_DIM] += dk
                    dkv_acc[at, HEAD_DIM:] += dv
                dq = dq + lax.dot_general(kv[b, :, :HEAD_DIM], ds, TN, preferred_element_type=F32)
            acc[...] = dq

        if qi == 0:
            def clean(b, carry):
                dkv_acc[pl.ds(pl.multiple_of(b * rows, rows), rows), :] = jnp.zeros((rows, 2 * HEAD_DIM), F32)
                return carry
            lax.fori_loop(low, jnp.minimum(low_hi, blk + 1), clean, 0)
        backward([blk], True)
        sweep(clear, blk, backward)
        masked_sweep(low, clear, backward)
        dq2[qi] = acc[...].T.astype(BF16)

    low_lo = window(lower)[0]

    def write(b, carry):
        at = pl.ds(pl.multiple_of(b * rows, rows), rows)
        dk_out[b] = dkv_acc[at, :HEAD_DIM].astype(BF16)
        dv_out[b] = dkv_acc[at, HEAD_DIM:].astype(BF16)
        return carry

    def blank(b, carry):
        dk_out[b] = jnp.zeros((rows, HEAD_DIM), BF16)
        dv_out[b] = jnp.zeros((rows, HEAD_DIM), BF16)
        return carry

    mid = jnp.maximum(low_hi, lower + 1)
    lax.fori_loop(0, low_lo, blank, 0)
    lax.fori_loop(low_lo, lower + 1, write, 0)
    lax.fori_loop(lower + 1, mid, blank, 0)
    lax.fori_loop(mid, lower + 2 * N_Z + 1, write, 0)
    lax.fori_loop(lower + 2 * N_Z + 1, n_blk, blank, 0)


def reduce_kernel(
    n_ctx, dk, dv, dq2, o2, placed,
    attn_out, qkv_grad, cg,
    sb, part, far_l, far_r, in_l, in_r, res, gx, gdq, go_in,
    placed_t, cs_send, cs_recv, mine_sum, rs_out, rs_in,
    s_send, s_recv, f_send, f_recv, n_send, n_recv, x_send, x_recv,
    p_send, p_recv, r_send, r_recv, g_send, g_recv, e_send, e_recv,
):
    c, core, z, xl = place()
    ox = 1 - xl
    cx = ctx_id(ox, z, core)
    sib = ctx_id(xl, z, 1 - core)
    right = ctx_id(xl, z + 1, core)
    left = ctx_id(xl, z + N_Z - 1, core)
    rows = placed.shape[0]
    half = rows // 2
    mine = pl.ds(pl.multiple_of(xl * HEAD_DIM, HEAD_DIM), HEAD_DIM)
    other = pl.ds(pl.multiple_of(ox * HEAD_DIM, HEAD_DIM), HEAD_DIM)
    top, bottom = pl.ds(0, half), pl.ds(half, half)

    order = [(dz, x) for dz in (2, 1, 3, 0) for x in (ox, xl)]
    terms = (dk, dv)

    entry_barrier(n_ctx, 1, c, 0)
    sends = []

    def go(copy):
        copy.start()
        sends.append(copy)

    def sib_copy(v, j):
        dz, x = order[j]
        return remote(terms[v].at[ctx_id(x, z + dz, 1 - core)], sb.at[v, j], s_send.at[v, j], s_recv.at[v, j], ctx=sib)

    for v in (1, 0):
        for j in range(8):
            go(sib_copy(v, j))
    go(remote(dq2.at[ox], gdq, x_send.at[0], x_recv.at[0], ctx=cx))
    go(remote(o2.at[ox], go_in, x_send.at[1], x_recv.at[1], ctx=cx))

    def pair(v, j, at):
        dz, x = order[j]
        return terms[v][ctx_id(x, z + dz, core), at, :].astype(F32) + sb[v, j, at, :].astype(F32)

    def far_copy(v, n, to):
        e = n % 2
        at, buf = ((top, far_l), (bottom, far_r))[n // 2]
        return remote(part.at[v, e, at], buf.at[v, e], f_send.at[v, n], f_recv.at[v, n], ctx=to)

    def near_copy(v, n, to):
        e, way, late = n % 2, (n // 2) % 2, n // 4
        at = (bottom, top)[way] if late == 0 else (top, bottom)[way]
        buf = (in_l, in_r)[way]
        return remote(part.at[v, 2 + 2 * way + e, at], buf.at[v, e, at], n_send.at[v, n], n_recv.at[v, n], ctx=to)

    def send_far(v):
        for e in range(2):
            sib_copy(v, e).wait_recv()
            part[v, e] = pair(v, e, pl.ds(0, rows)).astype(BF16)
            go(far_copy(v, e, right))
            go(far_copy(v, 2 + e, left))

    def send_early(v):
        for e in range(2):
            sib_copy(v, 2 + e).wait_recv()
            part[v, 2 + e, bottom, :] = pair(v, 2 + e, bottom).astype(BF16)
            go(near_copy(v, e, right))
            sib_copy(v, 4 + e).wait_recv()
            part[v, 4 + e, top, :] = pair(v, 4 + e, top).astype(BF16)
            go(near_copy(v, 2 + e, left))

    def send_late(v):
        for e in range(2):
            far_copy(v, e, left).wait_recv()
            part[v, 2 + e, top, :] = (pair(v, 2 + e, top) + far_l[v, e].astype(F32)).astype(BF16)
            go(near_copy(v, 4 + e, right))
            far_copy(v, 2 + e, right).wait_recv()
            part[v, 4 + e, bottom, :] = (pair(v, 4 + e, bottom) + far_r[v, e].astype(F32)).astype(BF16)
            go(near_copy(v, 6 + e, left))

    def block_done(v):
        for e in range(2):
            sib_copy(v, 6 + e).wait_recv()
            for n, src in ((e, left), (2 + e, right), (4 + e, left), (6 + e, right)):
                near_copy(v, n, src).wait_recv()
            total = pair(v, 6 + e, pl.ds(0, rows)) + in_l[v, e].astype(F32) + in_r[v, e].astype(F32)
            res[v, e] = total.astype(BF16)
            if e == 0:
                go(remote(res.at[v, 0], gx.at[v], x_send.at[2 + v], x_recv.at[2 + v], ctx=cx))

    def take_grad(v):
        qkv_grad[1 + v, :, mine] = res[v, 1]
        remote(res.at[v, 0], gx.at[v], x_send.at[2 + v], x_recv.at[2 + v], ctx=cx).wait_recv()
        qkv_grad[1 + v, :, other] = gx[v]

    vis = placed.shape[1]
    vis_half = vis // 2
    n_chip = n_ctx // 2
    chunk = vis_half // n_chip
    chip = c // 2
    own_rows = pl.ds(pl.multiple_of(core * vis_half, vis_half), vis_half)
    sib_rows = pl.ds(pl.multiple_of((1 - core) * vis_half, vis_half), vis_half)

    def chunk_at(g):
        return pl.ds(pl.multiple_of(g * chunk, chunk), chunk)

    def final_at(g):
        return pl.ds(pl.multiple_of(core * vis_half + g * chunk, chunk), chunk)

    def conn_start(i):
        grads = qkv_grad[i]
        cs_send[i] = jnp.dot(placed_t[sib_rows, :], grads, preferred_element_type=F32).astype(BF16)
        go(remote(cs_send.at[i], cs_recv.at[i], p_send.at[i], p_recv.at[i], ctx=sib))
        mine_sum[i] = jnp.dot(placed_t[own_rows, :], grads, preferred_element_type=F32)

    def conn_scatter(i):
        remote(cs_send.at[i], cs_recv.at[i], p_send.at[i], p_recv.at[i], ctx=sib).wait_recv()
        total = mine_sum[i] + cs_recv[i].astype(F32)
        mine_sum[i] = total
        rs_out[i] = total.astype(BF16)
        for k in range(1, n_chip):
            g = lax.rem(chip + k, n_chip)
            go(remote(rs_out.at[i, chunk_at(g)], rs_in.at[i, k], r_send.at[i, k], r_recv.at[i, k], ctx=g * 2 + core))

    def conn_gather(i):
        total = mine_sum[i, chunk_at(chip), :]
        for k in range(1, n_chip):
            g = lax.rem(chip + n_chip - k, n_chip)
            remote(rs_out.at[i, chunk_at(g)], rs_in.at[i, k], r_send.at[i, k], r_recv.at[i, k], ctx=g * 2 + core).wait_recv()
            total = total + rs_in[i, k].astype(F32)
        cg[i, final_at(chip), :] = total.astype(BF16)
        for k in range(1, n_chip):
            g = lax.rem(chip + k, n_chip)
            ref = cg.at[i, final_at(chip)]
            go(remote(ref, ref, g_send.at[i, k], g_recv.at[i, k], ctx=g * 2 + core))

    def conn_share(i):
        for k in range(1, n_chip):
            g = lax.rem(chip + n_chip - k, n_chip)
            ref = cg.at[i, final_at(g)]
            remote(ref, ref, g_send.at[i, k], g_recv.at[i, k], ctx=g * 2 + core).wait_recv()
        ref = cg.at[i, own_rows]
        go(remote(ref, ref, e_send.at[i], e_recv.at[i], ctx=sib))

    def conn_finish(i):
        ref = cg.at[i, sib_rows]
        remote(ref, ref, e_send.at[i], e_recv.at[i], ctx=sib).wait_recv()

    send_far(1)
    send_early(1)
    send_far(0)
    send_early(0)
    placed_t[...] = placed[...].T
    send_late(1)
    send_late(0)
    remote(dq2.at[ox], gdq, x_send.at[0], x_recv.at[0], ctx=cx).wait_recv()
    qkv_grad[0, :, mine] = dq2[xl]
    qkv_grad[0, :, other] = gdq[...]
    conn_start(0)
    remote(o2.at[ox], go_in, x_send.at[1], x_recv.at[1], ctx=cx).wait_recv()
    attn_out[:, mine] = o2[xl]
    attn_out[:, other] = go_in[...]
    conn_scatter(0)
    block_done(1)
    take_grad(1)
    conn_start(2)
    conn_gather(0)
    conn_scatter(2)
    block_done(0)
    take_grad(0)
    conn_start(1)
    conn_scatter(1)
    conn_gather(2)
    conn_share(0)
    conn_gather(1)
    conn_share(2)
    conn_finish(0)
    conn_share(1)
    conn_finish(2)
    conn_finish(1)
    for copy in sends:
        copy.wait_send()


def finish_kernel(attn_in, grad_in, conn_in, attn_out, grad_out, conn_out, conn, sem):
    copies = [pltpu.make_async_copy(attn_in, attn_out, sem.at[0]), pltpu.make_async_copy(grad_in, grad_out, sem.at[1])]
    for copy in copies:
        copy.start()
    for i in range(3):
        conn[i] = conn_in[i].astype(F32)
        copy = pltpu.make_async_copy(conn.at[i], conn_out.at[i], sem.at[2 + i])
        copy.start()
        copies.append(copy)
    for copy in copies:
        copy.wait()


def local(base_qkv, frames, frame_block, frame_slot, frame_live, start_block, conn_w, d_out):
    n_ctx = lax.axis_size("ctx")
    n_tp = lax.axis_size("tp")
    _, rows, width = base_qkv.shape
    vis = frames.shape[2]
    pw = vis // n_tp
    half = rows // 2
    two = 2 * HEAD_DIM
    piece = FRAME_TOK + CODE_ROWS
    vmem = pl.BlockSpec(memory_space=pltpu.VMEM)
    smem = pl.BlockSpec(memory_space=pltpu.SMEM)
    hbm = pl.BlockSpec(memory_space=pltpu.HBM)
    dma = pltpu.SemaphoreType.DMA

    def buf(*shape):
        return pltpu.VMEM(shape, BF16)

    def kept(*arrays, space=pltpu.VMEM):
        return [pltpu.with_memory_space_constraint(x, space) for x in arrays]

    def params(n):
        return pltpu.CompilerParams(collective_id=n, has_side_effects=True, vmem_limit_bytes=VMEM_LIMIT)

    placed, q2, do2, kv = pl.pallas_call(
        lambda *refs: gather_kernel(n_ctx, n_tp, *refs),
        out_shape=(
            buf(rows, vis), buf(2, rows, HEAD_DIM), buf(2, rows, HEAD_DIM), buf(n_ctx, rows, two),
        ),
        in_specs=[smem, smem, smem, hbm, hbm, hbm, hbm],
        out_specs=(vmem, vmem, vmem, vmem),
        scratch_shapes=[
            pltpu.VMEM((n_tp, piece, pw), BF16),
            pltpu.VMEM((n_tp, piece, pw), BF16),
            pltpu.VMEM((n_ctx, piece, pw), BF16),
            pltpu.VMEM((n_ctx, piece, pw), BF16),
            pltpu.VMEM((1, FRAME_TOK, vis), BF16),
            pltpu.VMEM((rows, width), BF16),
            pltpu.VMEM((3, rows, width), BF16),
            pltpu.VMEM((3, vis, width), BF16),
            pltpu.VMEM((3, rows, width), BF16),
            pltpu.VMEM((2, half, two), BF16),
            pltpu.VMEM((rows, HEAD_DIM), BF16),
            pltpu.VMEM((rows, HEAD_DIM), BF16),
            dma((4,)), dma((n_tp,)), dma((n_tp,)), dma((n_ctx,)), dma((n_ctx,)), dma((2, 7)), dma((2, 7)),
            dma((4,)), dma((4,)), dma((2, 6)), dma((2, 6)), dma((2, 8)), dma((2, 8)),
        ],
        compiler_params=params(0),
        name="gather",
    )(
        frame_block, frame_slot, frame_live,
        *kept(frames, base_qkv, conn_w.transpose(1, 0, 2), d_out, space=pltpu.HBM),
    )

    o2, dq2, dk, dv = pl.pallas_call(
        attention_kernel,
        out_shape=(
            buf(2, rows, HEAD_DIM), buf(2, rows, HEAD_DIM), buf(n_ctx, rows, HEAD_DIM), buf(n_ctx, rows, HEAD_DIM),
        ),
        in_specs=[smem, vmem, vmem, vmem],
        out_specs=(vmem, vmem, vmem, vmem),
        scratch_shapes=[
            pltpu.VMEM((n_ctx * rows, two), F32),
            pltpu.VMEM((HEAD_DIM, rows), F32),
            pltpu.VMEM((1, rows), F32),
            pltpu.VMEM((1, rows), F32),
        ],
        compiler_params=pltpu.CompilerParams(vmem_limit_bytes=VMEM_LIMIT),
        name="attention",
    )(*kept(start_block, space=pltpu.SMEM), *kept(q2, do2, kv))

    vis_half = vis // 2
    n_chip = n_ctx // 2
    attn_out, qkv_grad, conn = pl.pallas_call(
        lambda *refs: reduce_kernel(n_ctx, *refs),
        out_shape=(buf(rows, width), buf(3, rows, width), buf(3, vis, width)),
        in_specs=[vmem] * 5,
        out_specs=(vmem, vmem, vmem),
        scratch_shapes=[
            pltpu.VMEM((2, 8, rows, HEAD_DIM), BF16),
            pltpu.VMEM((2, 6, rows, HEAD_DIM), BF16),
            pltpu.VMEM((2, 2, half, HEAD_DIM), BF16),
            pltpu.VMEM((2, 2, half, HEAD_DIM), BF16),
            pltpu.VMEM((2, 2, rows, HEAD_DIM), BF16),
            pltpu.VMEM((2, 2, rows, HEAD_DIM), BF16),
            pltpu.VMEM((2, 2, rows, HEAD_DIM), BF16),
            pltpu.VMEM((2, rows, HEAD_DIM), BF16),
            pltpu.VMEM((rows, HEAD_DIM), BF16),
            pltpu.VMEM((rows, HEAD_DIM), BF16),
            pltpu.VMEM((vis, rows), BF16),
            pltpu.VMEM((3, vis_half, width), BF16),
            pltpu.VMEM((3, vis_half, width), BF16),
            pltpu.VMEM((3, vis_half, width), F32),
            pltpu.VMEM((3, vis_half, width), BF16),
            pltpu.VMEM((3, n_chip, vis_half // n_chip, width), BF16),
            dma((2, 8)), dma((2, 8)), dma((2, 4)), dma((2, 4)), dma((2, 8)), dma((2, 8)), dma((4,)), dma((4,)),
            dma((3,)), dma((3,)), dma((3, n_chip)), dma((3, n_chip)), dma((3, n_chip)), dma((3, n_chip)),
            dma((3,)), dma((3,)),
        ],
        compiler_params=params(1),
        name="reduce",
    )(*kept(dk, dv, dq2, o2, placed))

    out = pl.BlockSpec(memory_space=pl.ANY)
    attn_out, qkv_grad, conn = pl.pallas_call(
        finish_kernel,
        out_shape=(
            jax.ShapeDtypeStruct((rows, width), BF16), jax.ShapeDtypeStruct((3, rows, width), BF16),
            jax.ShapeDtypeStruct((3, vis, width), F32),
        ),
        in_specs=[vmem] * 3,
        out_specs=(out, out, out),
        scratch_shapes=[pltpu.VMEM((3, vis, width), F32), dma((5,))],
        compiler_params=pltpu.CompilerParams(vmem_limit_bytes=VMEM_LIMIT),
        name="finish",
    )(*kept(attn_out, qkv_grad, conn))
    return (attn_out, qkv_grad, conn.transpose(1, 0, 2))


def solution(mesh):
    return jax.shard_map(
        local,
        mesh=mesh,
        in_specs=(
            P(None, "ctx", "tp"),
            P(("ctx", "tp"), None, None),
            P(("ctx", "tp")),
            P(("ctx", "tp")),
            P(("ctx", "tp")),
            P(),
            P(None, None, "tp"),
            P("ctx", "tp"),
        ),
        out_specs=(P("ctx", "tp"), P(None, "ctx", "tp"), P(None, None, "tp")),
        check_vma=False,
    )
```

```python
import math

import jax
import jax.numpy as jnp
from jax import lax
from jax.experimental import pallas as pl
from jax.experimental.pallas import tpu as pltpu
from jax.sharding import PartitionSpec as P

HEAD_DIM = 128
FRAME_TOK = 32
MASK_BLK = 128
CODE_ROWS = 16
N_Z = 4
N_PART = 4
MASKED = -1e30
MESH = pl.DeviceIdType.MESH
F32 = jnp.float32
BF16 = jnp.bfloat16
VMEM_LIMIT = 20 * 1024 * 1024

NN = (((1,), (0,)), ((), ()))
TN = (((0,), (0,)), ((), ()))


def place():
    c = lax.axis_index("ctx")
    core = c % 2
    z = (c // 2) % N_Z
    xl = c // (2 * N_Z)
    return c, core, z, xl


def ctx_id(xl, z, core):
    return xl * (2 * N_Z) + lax.rem(z, N_Z) * 2 + core


def entry_barrier(n_ctx, n_tp, c, t):
    barrier = pltpu.get_barrier_semaphore()
    for k in range(1, n_tp):
        pl.semaphore_signal(barrier, inc=1, device_id={"tp": lax.rem(t + k, n_tp)}, device_id_type=MESH)
    for k in range(1, n_ctx):
        pl.semaphore_signal(barrier, inc=1, device_id={"ctx": lax.rem(c + k, n_ctx)}, device_id_type=MESH)
    pl.semaphore_wait(barrier, n_tp - 1 + n_ctx - 1)


def remote(src, dst, send, recv, **where):
    return pltpu.make_async_remote_copy(
        src_ref=src, dst_ref=dst, send_sem=send, recv_sem=recv, device_id=where, device_id_type=MESH
    )


def gather_kernel(
    n_ctx, n_tp, fb, fs, fl, frames_hbm, base_hbm, w_hbm, dout_hbm,
    placed, q2, do2, kv, px,
    s_a, r_a, s_b, r_b, frames, dout, base, w, qkv, xs, xq, xd,
    load_sem, a_send, a_recv, b_send, b_recv, c_send, c_recv,
    x_send, x_recv, z_send, z_recv, s_send, s_recv,
):
    c, core, z, xl = place()
    t = lax.axis_index("tp")
    pw = frames.shape[2] // n_tp
    rows = placed.shape[0]
    part = rows // N_PART
    ox = 1 - xl
    cx = ctx_id(ox, z, core)
    sib = ctx_id(xl, z, 1 - core)
    mine = pl.ds(pl.multiple_of(xl * HEAD_DIM, HEAD_DIM), HEAD_DIM)
    other = pl.ds(pl.multiple_of(ox * HEAD_DIM, HEAD_DIM), HEAD_DIM)

    load_f = pltpu.make_async_copy(frames_hbm, frames, load_sem.at[2])
    load_d = pltpu.make_async_copy(dout_hbm, dout, load_sem.at[3])
    load_w = pltpu.make_async_copy(w_hbm, w, load_sem.at[0])
    load_b = pltpu.make_async_copy(base_hbm, base, load_sem.at[1])
    load_f.start()
    load_w.start()
    load_b.start()
    load_d.start()

    code = jnp.where(fl[0] == 1, fb[0] * (rows // FRAME_TOK) + fs[0] + 1, 0).astype(F32)
    code_rows = jnp.full((CODE_ROWS, pw), code, F32).astype(BF16)
    load_f.wait()
    for p in range(n_tp):
        s_a[p, :FRAME_TOK, :] = frames[0, :, p * pw:(p + 1) * pw]
        s_a[p, FRAME_TOK:, :] = code_rows

    entry_barrier(n_ctx, n_tp, c, t)

    sends = []

    def go(copy):
        copy.start()
        sends.append(copy)

    for k in range(1, n_tp):
        p = lax.rem(t + k, n_tp)
        go(remote(s_a.at[p], r_a.at[t], a_send.at[k], a_recv.at[k], tp=p))
    r_a[t] = s_a[t]
    load_d.wait()
    xd[...] = dout[:, other]
    do2[xl] = dout[:, mine]
    go(remote(xd, do2.at[xl], x_send.at[N_PART + 1], x_recv.at[N_PART + 1], ctx=cx))
    for k in range(1, n_tp):
        p = lax.rem(t + n_tp - k, n_tp)
        remote(s_a.at[p], r_a.at[p], a_send.at[k], a_recv.at[k], tp=p).wait_recv()

    slots = rows // FRAME_TOK
    pieces = r_a[...].astype(F32)
    codes = pieces[:, FRAME_TOK:FRAME_TOK + 1, :]
    for k in range(n_ctx):
        d = lax.rem(c + k, n_ctx)
        low = (d * slots).astype(F32)
        hit = (codes > low) & (codes < low + (slots + 0.5))
        s_b[k] = jnp.sum(jnp.where(hit, pieces, 0.0), axis=0).astype(BF16)
        if k:
            go(remote(s_b.at[k], r_b.at[c], b_send.at[k], b_recv.at[k], ctx=d))
    r_b[c] = s_b[0]
    for k in range(1, n_ctx):
        d = lax.rem(c + n_ctx - k, n_ctx)
        remote(s_b.at[k], r_b.at[d], b_send.at[k], b_recv.at[k], ctx=d).wait_recv()

    arrived = r_b[...].astype(F32)
    codes = arrived[:, FRAME_TOK:FRAME_TOK + 1, :]
    rows_in = arrived[:, :FRAME_TOK, :]
    y = t // 2
    xh = t % 2

    def tp_id(y_at, x_at):
        return lax.rem(y_at, n_tp // 2) * 2 + x_at

    def piece(p, first, count):
        return placed.at[pl.ds(first, count), pl.ds(pl.multiple_of(p * pw, pw), pw)]

    if n_tp > 1:
        n_y = n_tp // 2
        up, up_x = tp_id(y + 1, xh), tp_id(y + 1, 1 - xh)
        down, down_x = tp_id(y + n_y - 1, xh), tp_id(y + n_y - 1, 1 - xh)
        far, far_x = tp_id(y + 2, xh), tp_id(y + 2, 1 - xh)
        xp = tp_id(y, 1 - xh)

    def c_copy(r, n, p, to):
        ref = piece(p, r * part, part)
        return remote(ref, ref, c_send.at[r, n], c_recv.at[r, n], tp=to)

    def place_rows(r):
        for s in range(r * slots // N_PART, (r + 1) * slots // N_PART):
            want = (c * slots + (s + 1)).astype(F32)
            piece(t, s * FRAME_TOK, FRAME_TOK)[...] = jnp.sum(
                jnp.where(codes == want, rows_in, 0.0), axis=0
            ).astype(BF16)

    def send_pieces(r):
        if n_tp > 1 and r < N_PART:
            go(c_copy(r, 0, t, xp))
            go(c_copy(r, 1, t, up))
            go(c_copy(r, 2, t, down))
            go(c_copy(r, 3, t, far))

    def relay_pieces(r):
        if n_tp > 1 and r < N_PART:
            c_copy(r, 0, xp, xp).wait_recv()
            go(c_copy(r, 4, xp, up))
            go(c_copy(r, 5, xp, down))
            c_copy(r, 3, far, far).wait_recv()
            go(c_copy(r, 6, far, xp))

    def wait_pieces(r):
        if n_tp > 1:
            for n, p in ((1, down), (2, up), (4, down_x), (5, up_x), (6, far_x)):
                c_copy(r, n, p, p).wait_recv()

    place_rows(0)
    send_pieces(0)
    place_rows(1)
    send_pieces(1)
    for r in range(2, N_PART):
        place_rows(r)
    relay_pieces(0)
    send_pieces(2)
    relay_pieces(1)

    right = ctx_id(xl, z + 1, core)
    left = ctx_id(xl, z + N_Z - 1, core)
    opp = ctx_id(xl, z + 2, core)
    right_x = ctx_id(ox, z + 1, core)
    left_x = ctx_id(ox, z + N_Z - 1, core)
    opp_x = ctx_id(ox, z + 2, core)

    def unit(i, r):
        return kv.at[i, pl.ds(r * part, part)]

    def to_right(i, r, n):
        go(remote(unit(i, r), unit(i, r), z_send.at[0, r, n], z_recv.at[0, r, n], ctx=right))

    def to_left(i, r, n):
        go(remote(unit(i, r), unit(i, r), z_send.at[1, r, n], z_recv.at[1, r, n], ctx=left))

    def to_sib(i, r, n):
        go(remote(unit(i, r), unit(i, r), s_send.at[r, n], s_recv.at[r, n], ctx=sib))

    def from_left(i, r, n):
        remote(unit(i, r), unit(i, r), z_send.at[0, r, n], z_recv.at[0, r, n], ctx=left).wait_recv()

    def from_right(i, r, n):
        remote(unit(i, r), unit(i, r), z_send.at[1, r, n], z_recv.at[1, r, n], ctx=right).wait_recv()

    def spread(i, r, n):
        to_right(i, r, n)
        to_left(i, r, n)
        to_sib(i, r, n)

    def from_partner(r):
        remote(xs.at[r], unit(cx, r), x_send.at[r], x_recv.at[r], ctx=cx).wait_recv()
        spread(cx, r, 1)

    def project(i, r):
        at = slice(r * part, (r + 1) * part)
        term = jnp.dot(placed[at, :], w[i], preferred_element_type=F32)
        qkv[i, at, :] = (base[i, at, :].astype(F32) + term).astype(BF16)

    load_w.wait()
    load_b.wait()
    for r in range(N_PART):
        at = slice(r * part, (r + 1) * part)
        wait_pieces(r)
        project(1, r)
        project(2, r)
        xs[r, :, :HEAD_DIM] = qkv[1, at, other]
        xs[r, :, HEAD_DIM:] = qkv[2, at, other]
        kv[c, at, :HEAD_DIM] = qkv[1, at, mine]
        kv[c, at, HEAD_DIM:] = qkv[2, at, mine]
        go(remote(xs.at[r], unit(c, r), x_send.at[r], x_recv.at[r], ctx=cx))
        spread(c, r, 0)
        send_pieces(r + 3)
        relay_pieces(r + 2)
        if r >= 2:
            from_partner(r - 2)
    for r in range(N_PART):
        project(0, r)
    xq[...] = qkv[0, :, other]
    q2[xl] = qkv[0, :, mine]
    from_partner(N_PART - 2)
    from_partner(N_PART - 1)
    go(remote(xq, q2.at[xl], x_send.at[N_PART], x_recv.at[N_PART], ctx=cx))
    px_copy = remote(placed.at[pl.ds(0, rows // 2)], px, x_send.at[N_PART + 2], x_recv.at[N_PART + 2], ctx=cx)
    go(px_copy)
    for n, (a, b) in enumerate(((left, right), (left_x, right_x))):
        for r in range(N_PART):
            from_left(a, r, n)
            if r < N_PART // 2:
                to_right(a, r, 2 + n)
            to_sib(a, r, 2 + 3 * n)
            from_right(b, r, n)
            if r >= N_PART // 2:
                to_left(b, r, 2 + n)
            to_sib(b, r, 3 + 3 * n)
    for n, i in enumerate((opp, opp_x)):
        for r in range(N_PART):
            if r < N_PART // 2:
                from_left(i, r, 2 + n)
            else:
                from_right(i, r, 2 + n)
            to_sib(i, r, 4 + 3 * n)

    remote(xq, q2.at[ox], x_send.at[N_PART], x_recv.at[N_PART], ctx=cx).wait_recv()
    remote(xd, do2.at[ox], x_send.at[N_PART + 1], x_recv.at[N_PART + 1], ctx=cx).wait_recv()
    px_copy.wait_recv()
    sc = 1 - core
    theirs = [ctx_id(x, z + dz, sc) for x, dz in ((xl, 0), (ox, 0), (xl, 3), (xl, 1), (ox, 3), (ox, 1), (xl, 2), (ox, 2))]
    for n, i in enumerate(theirs):
        for r in range(N_PART):
            remote(unit(i, r), unit(i, r), s_send.at[r, n], s_recv.at[r, n], ctx=sib).wait_recv()
    for copy in sends:
        copy.wait_send()


def attention_kernel(
    start, q2, do2, kv, o2, dq2, dk_out, dv_out, dkv_acc, acc, m_ref, l_ref
):
    c, core, z, xl = place()
    lower = lax.rem(c, 2 * N_Z)
    n_blk, rows, _ = kv.shape
    mask_per = rows // MASK_BLK
    scale = 1.0 / math.sqrt(HEAD_DIM)
    scale2 = scale * math.log2(math.e)

    def window(blk):
        first = start[blk * mask_per]
        last = start[blk * mask_per + mask_per - 1]
        low = jnp.minimum(first // mask_per, blk)
        clear = jnp.minimum((last + mask_per - 1) // mask_per, blk)
        return low, clear

    low_hi = window(lower + 2 * N_Z)[0]

    for qi in (1, 0):
        blk = lower + 2 * N_Z * qi
        q0 = blk * rows
        queries = q2[qi]
        out_grad = do2[qi]
        queries_t = queries.astype(F32).T.astype(BF16)
        grad_t = out_grad.astype(F32).T.astype(BF16)
        low, clear = window(blk)
        q_start = jnp.concatenate(
            [jnp.full((1, MASK_BLK), start[blk * mask_per + i] * MASK_BLK, jnp.int32) for i in range(mask_per)], axis=1
        )

        def allowed(b):
            key_pos = b * rows + lax.broadcasted_iota(jnp.int32, (rows, rows), 0)
            q_pos = q0 + lax.broadcasted_iota(jnp.int32, (rows, rows), 1)
            return (key_pos <= q_pos) & (key_pos >= q_start)

        m_ref[...] = jnp.full_like(m_ref, MASKED)
        l_ref[...] = jnp.zeros_like(l_ref)
        acc[...] = jnp.zeros_like(acc)

        def forward(blocks, masked):
            scores = [
                lax.dot_general(kv[b, :, :HEAD_DIM], queries_t, NN, preferred_element_type=F32) * scale2 for b in blocks
            ]
            if masked:
                scores = [jnp.where(allowed(b), s, MASKED) for b, s in zip(blocks, scores)]
            m_old = m_ref[...]
            m_new = m_old
            for s in scores:
                m_new = jnp.maximum(m_new, jnp.max(s, axis=0, keepdims=True))
            alpha = jnp.exp2(m_old - m_new)
            m_ref[...] = m_new
            total = l_ref[...] * alpha
            out = acc[...] * alpha
            for b, s in zip(blocks, scores):
                p = jnp.exp2(s - m_new)
                total = total + jnp.sum(p, axis=0, keepdims=True)
                out = out + lax.dot_general(kv[b, :, HEAD_DIM:], p.astype(BF16), TN, preferred_element_type=F32)
            l_ref[...] = total
            acc[...] = out

        def sweep(lo, hi, step):
            pairs = (hi - lo) // 2

            def body(i, carry):
                step([lo + i * 2, lo + i * 2 + 1], False)
                return carry

            def rest(b, carry):
                step([b], False)
                return carry

            lax.fori_loop(0, pairs, body, 0)
            lax.fori_loop(lo + pairs * 2, hi, rest, 0)

        def masked_sweep(lo, hi, step):
            def body(b, carry):
                step([b], True)
                return carry
            lax.fori_loop(lo, hi, body, 0)

        forward([blk], True)
        sweep(clear, blk, forward)
        masked_sweep(low, clear, forward)

        total = l_ref[...]
        out_t = (acc[...] / total).astype(BF16).astype(F32)
        o2[qi] = out_t.T.astype(BF16)
        row_dot = jnp.sum(out_t * out_grad.astype(F32).T, axis=0, keepdims=True)
        log_norm = m_ref[...] + jnp.log2(total)
        acc[...] = jnp.zeros_like(acc)

        def backward(blocks, masked):
            dq = acc[...]
            tiles = []
            for b in blocks:
                s = lax.dot_general(kv[b, :, :HEAD_DIM], queries_t, NN, preferred_element_type=F32)
                dp = lax.dot_general(kv[b, :, HEAD_DIM:], grad_t, NN, preferred_element_type=F32)
                tiles.append((b, s, dp))
            for b, s, dp in tiles:
                p = jnp.exp2(s * scale2 - log_norm)
                if masked:
                    p = jnp.where(allowed(b), p, 0.0)
                ds = (p * (dp - row_dot) * scale).astype(BF16)
                at = pl.ds(pl.multiple_of(b * rows, rows), rows)
                dk = jnp.dot(ds, queries, preferred_element_type=F32)
                dv = jnp.dot(p.astype(BF16), out_grad, preferred_element_type=F32)
                if qi == 1:
                    dkv_acc[at, :HEAD_DIM] = dk
                    dkv_acc[at, HEAD_DIM:] = dv
                else:
                    dkv_acc[at, :HEAD_DIM] += dk
                    dkv_acc[at, HEAD_DIM:] += dv
                dq = dq + lax.dot_general(kv[b, :, :HEAD_DIM], ds, TN, preferred_element_type=F32)
            acc[...] = dq

        if qi == 0:
            def clean(b, carry):
                dkv_acc[pl.ds(pl.multiple_of(b * rows, rows), rows), :] = jnp.zeros((rows, 2 * HEAD_DIM), F32)
                return carry
            lax.fori_loop(low, jnp.minimum(low_hi, blk + 1), clean, 0)
        backward([blk], True)
        sweep(clear, blk, backward)
        masked_sweep(low, clear, backward)
        dq2[qi] = acc[...].T.astype(BF16)

    low_lo = window(lower)[0]

    def write(b, carry):
        at = pl.ds(pl.multiple_of(b * rows, rows), rows)
        dk_out[b] = dkv_acc[at, :HEAD_DIM].astype(BF16)
        dv_out[b] = dkv_acc[at, HEAD_DIM:].astype(BF16)
        return carry

    def blank(b, carry):
        dk_out[b] = jnp.zeros((rows, HEAD_DIM), BF16)
        dv_out[b] = jnp.zeros((rows, HEAD_DIM), BF16)
        return carry

    mid = jnp.maximum(low_hi, lower + 1)
    lax.fori_loop(0, low_lo, blank, 0)
    lax.fori_loop(low_lo, lower + 1, write, 0)
    lax.fori_loop(lower + 1, mid, blank, 0)
    lax.fori_loop(mid, lower + 2 * N_Z + 1, write, 0)
    lax.fori_loop(lower + 2 * N_Z + 1, n_blk, blank, 0)


def reduce_kernel(
    n_ctx, dk, dv, dq2, o2, placed, px_top,
    attn_out, qkv_grad, cg,
    sb, part, far_l, far_r, in_l, in_r, res, gx, gdq, go_in,
    px, placed_t, placed_xt, cs_send, cs_recv, mine_sum, rs_out, rs_in,
    s_send, s_recv, f_send, f_recv, n_send, n_recv, x_send, x_recv,
    p_send, p_recv, r_send, r_recv, g_send, g_recv, e_send, e_recv,
):
    c, core, z, xl = place()
    ox = 1 - xl
    cx = ctx_id(ox, z, core)
    sib = ctx_id(xl, z, 1 - core)
    right = ctx_id(xl, z + 1, core)
    left = ctx_id(xl, z + N_Z - 1, core)
    rows = placed.shape[0]
    half = rows // 2
    mine = pl.ds(pl.multiple_of(xl * HEAD_DIM, HEAD_DIM), HEAD_DIM)
    other = pl.ds(pl.multiple_of(ox * HEAD_DIM, HEAD_DIM), HEAD_DIM)
    top, bottom = pl.ds(0, half), pl.ds(half, half)

    order = [(dz, x) for dz in (2, 1, 3, 0) for x in (ox, xl)]
    terms = (dk, dv)

    entry_barrier(n_ctx, 1, c, 0)
    sends = []

    def go(copy):
        copy.start()
        sends.append(copy)

    def sib_copy(v, j):
        dz, x = order[j]
        return remote(terms[v].at[ctx_id(x, z + dz, 1 - core)], sb.at[v, j], s_send.at[v, j], s_recv.at[v, j], ctx=sib)

    for v in (1, 0):
        for j in range(8):
            go(sib_copy(v, j))
    px_copy = remote(placed.at[bottom], px, x_send.at[4], x_recv.at[4], ctx=cx)
    go(px_copy)

    def pair(v, j, at):
        dz, x = order[j]
        return terms[v][ctx_id(x, z + dz, core), at, :].astype(F32) + sb[v, j, at, :].astype(F32)

    def far_copy(v, n, to):
        e = n % 2
        at, buf = ((top, far_l), (bottom, far_r))[n // 2]
        return remote(part.at[v, e, at], buf.at[v, e], f_send.at[v, n], f_recv.at[v, n], ctx=to)

    def near_copy(v, n, to):
        e, way, late = n % 2, (n // 2) % 2, n // 4
        at = (bottom, top)[way] if late == 0 else (top, bottom)[way]
        buf = (in_l, in_r)[way]
        return remote(part.at[v, 2 + 2 * way + e, at], buf.at[v, e, at], n_send.at[v, n], n_recv.at[v, n], ctx=to)

    def send_far(v):
        for e in range(2):
            sib_copy(v, e).wait_recv()
            part[v, e] = pair(v, e, pl.ds(0, rows)).astype(BF16)
            go(far_copy(v, e, right))
            go(far_copy(v, 2 + e, left))

    def send_early(v):
        for e in range(2):
            sib_copy(v, 2 + e).wait_recv()
            part[v, 2 + e, bottom, :] = pair(v, 2 + e, bottom).astype(BF16)
            go(near_copy(v, e, right))
            sib_copy(v, 4 + e).wait_recv()
            part[v, 4 + e, top, :] = pair(v, 4 + e, top).astype(BF16)
            go(near_copy(v, 2 + e, left))

    def send_late(v):
        for e in range(2):
            far_copy(v, e, left).wait_recv()
            part[v, 2 + e, top, :] = (pair(v, 2 + e, top) + far_l[v, e].astype(F32)).astype(BF16)
            go(near_copy(v, 4 + e, right))
            far_copy(v, 2 + e, right).wait_recv()
            part[v, 4 + e, bottom, :] = (pair(v, 4 + e, bottom) + far_r[v, e].astype(F32)).astype(BF16)
            go(near_copy(v, 6 + e, left))

    def block_done(v):
        for e in range(2):
            sib_copy(v, 6 + e).wait_recv()
            for n, src in ((e, left), (2 + e, right), (4 + e, left), (6 + e, right)):
                near_copy(v, n, src).wait_recv()
            total = pair(v, 6 + e, pl.ds(0, rows)) + in_l[v, e].astype(F32) + in_r[v, e].astype(F32)
            res[v, e] = total.astype(BF16)
            if e == 0:
                go(remote(res.at[v, 0], gx.at[v], x_send.at[2 + v], x_recv.at[2 + v], ctx=cx))

    def take_grad(v):
        qkv_grad[1 + v, :, mine] = res[v, 1]
        remote(res.at[v, 0], gx.at[v], x_send.at[2 + v], x_recv.at[2 + v], ctx=cx).wait_recv()
        qkv_grad[1 + v, :, other] = gx[v]

    vis = placed.shape[1]
    vis_half = vis // 2
    n_chip = n_ctx // 2
    chunk = vis_half // N_Z
    chip = c // 2
    own_rows = pl.ds(pl.multiple_of(core * vis_half, vis_half), vis_half)
    sib_rows = pl.ds(pl.multiple_of((1 - core) * vis_half, vis_half), vis_half)

    def chunk_at(zz):
        return pl.ds(pl.multiple_of(zz * chunk, chunk), chunk)

    def final(i, g):
        first = core * vis_half + lax.rem(g, N_Z) * chunk
        cols = pl.ds(pl.multiple_of(g // N_Z * HEAD_DIM, HEAD_DIM), HEAD_DIM)
        return cg.at[i, pl.ds(pl.multiple_of(first, chunk), chunk), cols]

    def conn_start(i, grads, grads_x):
        def term(at):
            return jnp.dot(placed_t[at, :], grads, preferred_element_type=F32) + jnp.dot(
                placed_xt[at, :], grads_x, preferred_element_type=F32
            )

        cs_send[i] = term(sib_rows).astype(BF16)
        go(remote(cs_send.at[i], cs_recv.at[i], p_send.at[i], p_recv.at[i], ctx=sib))
        mine_sum[i] = term(own_rows)

    def scatter_copy(i, k, zz):
        return remote(rs_out.at[i, chunk_at(zz)], rs_in.at[i, k], r_send.at[i, k], r_recv.at[i, k], ctx=ctx_id(xl, zz, core))

    def conn_scatter(i):
        remote(cs_send.at[i], cs_recv.at[i], p_send.at[i], p_recv.at[i], ctx=sib).wait_recv()
        total = mine_sum[i] + cs_recv[i].astype(F32)
        mine_sum[i] = total
        rs_out[i] = total.astype(BF16)
        for k in range(1, N_Z):
            go(scatter_copy(i, k, lax.rem(z + k, N_Z)))

    def conn_gather(i):
        total = mine_sum[i, chunk_at(z), :]
        for k in range(1, N_Z):
            scatter_copy(i, k, lax.rem(z + N_Z - k, N_Z)).wait_recv()
            total = total + rs_in[i, k].astype(F32)
        final(i, chip)[...] = total.astype(BF16)
        for k in range(1, n_chip):
            g = lax.rem(chip + k, n_chip)
            go(remote(final(i, chip), final(i, chip), g_send.at[i, k], g_recv.at[i, k], ctx=g * 2 + core))

    def conn_share(i):
        for k in range(1, n_chip):
            g = lax.rem(chip + n_chip - k, n_chip)
            remote(final(i, g), final(i, g), g_send.at[i, k], g_recv.at[i, k], ctx=g * 2 + core).wait_recv()
        ref = cg.at[i, own_rows]
        go(remote(ref, ref, e_send.at[i], e_recv.at[i], ctx=sib))

    def conn_finish(i):
        ref = cg.at[i, sib_rows]
        remote(ref, ref, e_send.at[i], e_recv.at[i], ctx=sib).wait_recv()

    send_far(1)
    send_early(1)
    send_far(0)
    send_early(0)
    placed_t[...] = placed[...].T
    placed_xt[:, top] = px_top[...].T
    send_late(1)
    send_late(0)
    px_copy.wait_recv()
    placed_xt[:, bottom] = px[...].T
    conn_start(0, dq2[xl], dq2[ox])
    block_done(1)
    conn_start(2, res[1, 1], res[1, 0])
    conn_scatter(0)
    conn_scatter(2)
    block_done(0)
    conn_start(1, res[0, 1], res[0, 0])
    go(remote(dq2.at[ox], gdq, x_send.at[0], x_recv.at[0], ctx=cx))
    go(remote(o2.at[ox], go_in, x_send.at[1], x_recv.at[1], ctx=cx))
    conn_gather(0)
    conn_scatter(1)
    conn_gather(2)
    conn_gather(1)
    take_grad(1)
    take_grad(0)
    remote(dq2.at[ox], gdq, x_send.at[0], x_recv.at[0], ctx=cx).wait_recv()
    qkv_grad[0, :, mine] = dq2[xl]
    qkv_grad[0, :, other] = gdq[...]
    remote(o2.at[ox], go_in, x_send.at[1], x_recv.at[1], ctx=cx).wait_recv()
    attn_out[:, mine] = o2[xl]
    attn_out[:, other] = go_in[...]
    for i in (0, 2, 1):
        conn_share(i)
    for i in (0, 2, 1):
        conn_finish(i)
    for copy in sends:
        copy.wait_send()


def finish_kernel(attn_in, grad_in, conn_in, attn_out, grad_out, conn_out, conn, sem):
    copies = [pltpu.make_async_copy(attn_in, attn_out, sem.at[0]), pltpu.make_async_copy(grad_in, grad_out, sem.at[1])]
    for copy in copies:
        copy.start()
    for i in range(3):
        conn[i] = conn_in[i].astype(F32)
        copy = pltpu.make_async_copy(conn.at[i], conn_out.at[i], sem.at[2 + i])
        copy.start()
        copies.append(copy)
    for copy in copies:
        copy.wait()


def local(base_qkv, frames, frame_block, frame_slot, frame_live, start_block, conn_w, d_out):
    n_ctx = lax.axis_size("ctx")
    n_tp = lax.axis_size("tp")
    _, rows, width = base_qkv.shape
    vis = frames.shape[2]
    pw = vis // n_tp
    half = rows // 2
    two = 2 * HEAD_DIM
    piece = FRAME_TOK + CODE_ROWS
    vmem = pl.BlockSpec(memory_space=pltpu.VMEM)
    smem = pl.BlockSpec(memory_space=pltpu.SMEM)
    hbm = pl.BlockSpec(memory_space=pltpu.HBM)
    dma = pltpu.SemaphoreType.DMA

    def buf(*shape):
        return pltpu.VMEM(shape, BF16)

    def kept(*arrays, space=pltpu.VMEM):
        return [pltpu.with_memory_space_constraint(x, space) for x in arrays]

    def params(n):
        return pltpu.CompilerParams(collective_id=n, has_side_effects=True, vmem_limit_bytes=VMEM_LIMIT)

    placed, q2, do2, kv, px = pl.pallas_call(
        lambda *refs: gather_kernel(n_ctx, n_tp, *refs),
        out_shape=(
            buf(rows, vis), buf(2, rows, HEAD_DIM), buf(2, rows, HEAD_DIM), buf(n_ctx, rows, two),
            buf(rows // 2, vis),
        ),
        in_specs=[smem, smem, smem, hbm, hbm, hbm, hbm],
        out_specs=(vmem,) * 5,
        scratch_shapes=[
            pltpu.VMEM((n_tp, piece, pw), BF16),
            pltpu.VMEM((n_tp, piece, pw), BF16),
            pltpu.VMEM((n_ctx, piece, pw), BF16),
            pltpu.VMEM((n_ctx, piece, pw), BF16),
            pltpu.VMEM((1, FRAME_TOK, vis), BF16),
            pltpu.VMEM((rows, width), BF16),
            pltpu.VMEM((3, rows, width), BF16),
            pltpu.VMEM((3, vis, width), BF16),
            pltpu.VMEM((3, rows, width), BF16),
            pltpu.VMEM((N_PART, rows // N_PART, two), BF16),
            pltpu.VMEM((rows, HEAD_DIM), BF16),
            pltpu.VMEM((rows, HEAD_DIM), BF16),
            dma((4,)), dma((n_tp,)), dma((n_tp,)), dma((n_ctx,)), dma((n_ctx,)), dma((N_PART, 7)), dma((N_PART, 7)),
            dma((N_PART + 3,)), dma((N_PART + 3,)), dma((2, N_PART, 4)), dma((2, N_PART, 4)),
            dma((N_PART, 8)), dma((N_PART, 8)),
        ],
        compiler_params=params(0),
        name="gather",
    )(
        frame_block, frame_slot, frame_live,
        *kept(frames, base_qkv, conn_w.transpose(1, 0, 2), d_out, space=pltpu.HBM),
    )

    o2, dq2, dk, dv = pl.pallas_call(
        attention_kernel,
        out_shape=(
            buf(2, rows, HEAD_DIM), buf(2, rows, HEAD_DIM), buf(n_ctx, rows, HEAD_DIM), buf(n_ctx, rows, HEAD_DIM),
        ),
        in_specs=[smem, vmem, vmem, vmem],
        out_specs=(vmem, vmem, vmem, vmem),
        scratch_shapes=[
            pltpu.VMEM((n_ctx * rows, two), F32),
            pltpu.VMEM((HEAD_DIM, rows), F32),
            pltpu.VMEM((1, rows), F32),
            pltpu.VMEM((1, rows), F32),
        ],
        compiler_params=pltpu.CompilerParams(vmem_limit_bytes=VMEM_LIMIT),
        name="attention",
    )(*kept(start_block, space=pltpu.SMEM), *kept(q2, do2, kv))

    vis_half = vis // 2
    n_chip = n_ctx // 2
    attn_out, qkv_grad, conn = pl.pallas_call(
        lambda *refs: reduce_kernel(n_ctx, *refs),
        out_shape=(buf(rows, width), buf(3, rows, width), buf(3, vis, width)),
        in_specs=[vmem] * 6,
        out_specs=(vmem, vmem, vmem),
        scratch_shapes=[
            pltpu.VMEM((2, 8, rows, HEAD_DIM), BF16),
            pltpu.VMEM((2, 6, rows, HEAD_DIM), BF16),
            pltpu.VMEM((2, 2, half, HEAD_DIM), BF16),
            pltpu.VMEM((2, 2, half, HEAD_DIM), BF16),
            pltpu.VMEM((2, 2, rows, HEAD_DIM), BF16),
            pltpu.VMEM((2, 2, rows, HEAD_DIM), BF16),
            pltpu.VMEM((2, 2, rows, HEAD_DIM), BF16),
            pltpu.VMEM((2, rows, HEAD_DIM), BF16),
            pltpu.VMEM((rows, HEAD_DIM), BF16),
            pltpu.VMEM((rows, HEAD_DIM), BF16),
            pltpu.VMEM((half, vis), BF16),
            pltpu.VMEM((vis, rows), BF16),
            pltpu.VMEM((vis, rows), BF16),
            pltpu.VMEM((3, vis_half, HEAD_DIM), BF16),
            pltpu.VMEM((3, vis_half, HEAD_DIM), BF16),
            pltpu.VMEM((3, vis_half, HEAD_DIM), F32),
            pltpu.VMEM((3, vis_half, HEAD_DIM), BF16),
            pltpu.VMEM((3, N_Z, vis_half // N_Z, HEAD_DIM), BF16),
            dma((2, 8)), dma((2, 8)), dma((2, 4)), dma((2, 4)), dma((2, 8)), dma((2, 8)), dma((5,)), dma((5,)),
            dma((3,)), dma((3,)), dma((3, N_Z)), dma((3, N_Z)), dma((3, n_chip)), dma((3, n_chip)),
            dma((3,)), dma((3,)),
        ],
        compiler_params=params(1),
        name="reduce",
    )(*kept(dk, dv, dq2, o2, placed, px))

    out = pl.BlockSpec(memory_space=pl.ANY)
    attn_out, qkv_grad, conn = pl.pallas_call(
        finish_kernel,
        out_shape=(
            jax.ShapeDtypeStruct((rows, width), BF16), jax.ShapeDtypeStruct((3, rows, width), BF16),
            jax.ShapeDtypeStruct((3, vis, width), F32),
        ),
        in_specs=[vmem] * 3,
        out_specs=(out, out, out),
        scratch_shapes=[pltpu.VMEM((3, vis, width), F32), dma((5,))],
        compiler_params=pltpu.CompilerParams(vmem_limit_bytes=VMEM_LIMIT),
        name="finish",
    )(*kept(attn_out, qkv_grad, conn))
    return (attn_out, qkv_grad, conn.transpose(1, 0, 2))


def solution(mesh):
    return jax.shard_map(
        local,
        mesh=mesh,
        in_specs=(
            P(None, "ctx", "tp"),
            P(("ctx", "tp"), None, None),
            P(("ctx", "tp")),
            P(("ctx", "tp")),
            P(("ctx", "tp")),
            P(),
            P(None, None, "tp"),
            P("ctx", "tp"),
        ),
        out_specs=(P("ctx", "tp"), P(None, "ctx", "tp"), P(None, None, "tp")),
        check_vma=False,
    )
```

```python
import math

import jax
import jax.numpy as jnp
from jax import lax
from jax.experimental import pallas as pl
from jax.experimental.pallas import tpu as pltpu
from jax.sharding import PartitionSpec as P

HEAD_DIM = 128
FRAME_TOK = 32
MASK_BLK = 128
CODE_ROWS = 16
N_Z = 4
N_PART = 4
MASKED = -1e30
MESH = pl.DeviceIdType.MESH
F32 = jnp.float32
BF16 = jnp.bfloat16
VMEM_LIMIT = 20 * 1024 * 1024

NN = (((1,), (0,)), ((), ()))
TN = (((0,), (0,)), ((), ()))


def place():
    c = lax.axis_index("ctx")
    core = c % 2
    z = (c // 2) % N_Z
    xl = c // (2 * N_Z)
    return c, core, z, xl


def ctx_id(xl, z, core):
    return xl * (2 * N_Z) + lax.rem(z, N_Z) * 2 + core


def entry_barrier(n_ctx, n_tp, c, t):
    barrier = pltpu.get_barrier_semaphore()
    for k in range(1, n_tp):
        pl.semaphore_signal(barrier, inc=1, device_id={"tp": lax.rem(t + k, n_tp)}, device_id_type=MESH)
    for k in range(1, n_ctx):
        pl.semaphore_signal(barrier, inc=1, device_id={"ctx": lax.rem(c + k, n_ctx)}, device_id_type=MESH)
    pl.semaphore_wait(barrier, n_tp - 1 + n_ctx - 1)


def remote(src, dst, send, recv, **where):
    return pltpu.make_async_remote_copy(
        src_ref=src, dst_ref=dst, send_sem=send, recv_sem=recv, device_id=where, device_id_type=MESH
    )


def gather_kernel(
    n_ctx, n_tp, fb, fs, fl, frames_hbm, base_hbm, w_hbm, dout_hbm,
    placed, q2, do2, kv, px,
    s_a, r_a, s_b, r_b, frames, dout, base, w, qkv, xs, xq, xd,
    load_sem, a_send, a_recv, b_send, b_recv, c_send, c_recv,
    x_send, x_recv, z_send, z_recv, s_send, s_recv,
):
    c, core, z, xl = place()
    t = lax.axis_index("tp")
    pw = frames.shape[2] // n_tp
    rows = placed.shape[0]
    part = rows // N_PART
    ox = 1 - xl
    cx = ctx_id(ox, z, core)
    sib = ctx_id(xl, z, 1 - core)
    mine = pl.ds(pl.multiple_of(xl * HEAD_DIM, HEAD_DIM), HEAD_DIM)
    other = pl.ds(pl.multiple_of(ox * HEAD_DIM, HEAD_DIM), HEAD_DIM)

    load_f = pltpu.make_async_copy(frames_hbm, frames, load_sem.at[2])
    load_d = pltpu.make_async_copy(dout_hbm, dout, load_sem.at[3])
    load_w = pltpu.make_async_copy(w_hbm, w, load_sem.at[0])
    load_b = pltpu.make_async_copy(base_hbm, base, load_sem.at[1])
    load_f.start()
    load_w.start()
    load_b.start()
    load_d.start()

    code = jnp.where(fl[0] == 1, fb[0] * (rows // FRAME_TOK) + fs[0] + 1, 0).astype(F32)
    code_rows = jnp.full((CODE_ROWS, pw), code, F32).astype(BF16)
    load_f.wait()
    for p in range(n_tp):
        s_a[p, :FRAME_TOK, :] = frames[0, :, p * pw:(p + 1) * pw]
        s_a[p, FRAME_TOK:, :] = code_rows

    entry_barrier(n_ctx, n_tp, c, t)

    sends = []

    def go(copy):
        copy.start()
        sends.append(copy)

    for k in range(1, n_tp):
        p = lax.rem(t + k, n_tp)
        go(remote(s_a.at[p], r_a.at[t], a_send.at[k], a_recv.at[k], tp=p))
    r_a[t] = s_a[t]
    load_d.wait()
    xd[...] = dout[:, other]
    do2[xl] = dout[:, mine]
    go(remote(xd, do2.at[xl], x_send.at[N_PART + 1], x_recv.at[N_PART + 1], ctx=cx))
    for k in range(1, n_tp):
        p = lax.rem(t + n_tp - k, n_tp)
        remote(s_a.at[p], r_a.at[p], a_send.at[k], a_recv.at[k], tp=p).wait_recv()

    slots = rows // FRAME_TOK
    pieces = r_a[...].astype(F32)
    codes = pieces[:, FRAME_TOK:FRAME_TOK + 1, :]
    for k in range(n_ctx):
        d = lax.rem(c + k, n_ctx)
        low = (d * slots).astype(F32)
        hit = (codes > low) & (codes < low + (slots + 0.5))
        s_b[k] = jnp.sum(jnp.where(hit, pieces, 0.0), axis=0).astype(BF16)
        if k:
            go(remote(s_b.at[k], r_b.at[c], b_send.at[k], b_recv.at[k], ctx=d))
    r_b[c] = s_b[0]
    for k in range(1, n_ctx):
        d = lax.rem(c + n_ctx - k, n_ctx)
        remote(s_b.at[k], r_b.at[d], b_send.at[k], b_recv.at[k], ctx=d).wait_recv()

    arrived = r_b[...].astype(F32)
    codes = arrived[:, FRAME_TOK:FRAME_TOK + 1, :]
    rows_in = arrived[:, :FRAME_TOK, :]
    y = t // 2
    xh = t % 2

    def tp_id(y_at, x_at):
        return lax.rem(y_at, n_tp // 2) * 2 + x_at

    def piece(p, first, count):
        return placed.at[pl.ds(first, count), pl.ds(pl.multiple_of(p * pw, pw), pw)]

    if n_tp > 1:
        n_y = n_tp // 2
        up, up_x = tp_id(y + 1, xh), tp_id(y + 1, 1 - xh)
        down, down_x = tp_id(y + n_y - 1, xh), tp_id(y + n_y - 1, 1 - xh)
        far, far_x = tp_id(y + 2, xh), tp_id(y + 2, 1 - xh)
        xp = tp_id(y, 1 - xh)

    def c_copy(r, n, p, to):
        ref = piece(p, r * part, part)
        return remote(ref, ref, c_send.at[r, n], c_recv.at[r, n], tp=to)

    def place_rows(r):
        for s in range(r * slots // N_PART, (r + 1) * slots // N_PART):
            want = (c * slots + (s + 1)).astype(F32)
            piece(t, s * FRAME_TOK, FRAME_TOK)[...] = jnp.sum(
                jnp.where(codes == want, rows_in, 0.0), axis=0
            ).astype(BF16)

    def send_pieces(r):
        if n_tp > 1 and r < N_PART:
            go(c_copy(r, 0, t, xp))
            go(c_copy(r, 1, t, up))
            go(c_copy(r, 2, t, down))
            go(c_copy(r, 3, t, far))

    def relay_pieces(r):
        if n_tp > 1 and r < N_PART:
            c_copy(r, 0, xp, xp).wait_recv()
            go(c_copy(r, 4, xp, up))
            go(c_copy(r, 5, xp, down))
            c_copy(r, 3, far, far).wait_recv()
            go(c_copy(r, 6, far, xp))

    def wait_pieces(r):
        if n_tp > 1:
            for n, p in ((1, down), (2, up), (4, down_x), (5, up_x), (6, far_x)):
                c_copy(r, n, p, p).wait_recv()

    place_rows(0)
    send_pieces(0)
    place_rows(1)
    send_pieces(1)
    for r in range(2, N_PART):
        place_rows(r)
    relay_pieces(0)
    send_pieces(2)
    relay_pieces(1)

    right = ctx_id(xl, z + 1, core)
    left = ctx_id(xl, z + N_Z - 1, core)
    opp = ctx_id(xl, z + 2, core)
    right_x = ctx_id(ox, z + 1, core)
    left_x = ctx_id(ox, z + N_Z - 1, core)
    opp_x = ctx_id(ox, z + 2, core)

    def unit(i, r):
        return kv.at[i, pl.ds(r * part, part)]

    def to_right(i, r, n):
        go(remote(unit(i, r), unit(i, r), z_send.at[0, r, n], z_recv.at[0, r, n], ctx=right))

    def to_left(i, r, n):
        go(remote(unit(i, r), unit(i, r), z_send.at[1, r, n], z_recv.at[1, r, n], ctx=left))

    def to_sib(i, r, n):
        go(remote(unit(i, r), unit(i, r), s_send.at[r, n], s_recv.at[r, n], ctx=sib))

    def from_left(i, r, n):
        remote(unit(i, r), unit(i, r), z_send.at[0, r, n], z_recv.at[0, r, n], ctx=left).wait_recv()

    def from_right(i, r, n):
        remote(unit(i, r), unit(i, r), z_send.at[1, r, n], z_recv.at[1, r, n], ctx=right).wait_recv()

    def spread(i, r, n):
        to_right(i, r, n)
        to_left(i, r, n)
        to_sib(i, r, n)

    def from_partner(r):
        remote(xs.at[r], unit(cx, r), x_send.at[r], x_recv.at[r], ctx=cx).wait_recv()
        spread(cx, r, 1)

    def project(i, r):
        at = slice(r * part, (r + 1) * part)
        term = jnp.dot(placed[at, :], w[i], preferred_element_type=F32)
        qkv[i, at, :] = (base[i, at, :].astype(F32) + term).astype(BF16)

    load_w.wait()
    load_b.wait()
    for r in range(N_PART):
        at = slice(r * part, (r + 1) * part)
        wait_pieces(r)
        project(1, r)
        project(2, r)
        xs[r, :, :HEAD_DIM] = qkv[1, at, other]
        xs[r, :, HEAD_DIM:] = qkv[2, at, other]
        kv[c, at, :HEAD_DIM] = qkv[1, at, mine]
        kv[c, at, HEAD_DIM:] = qkv[2, at, mine]
        go(remote(xs.at[r], unit(c, r), x_send.at[r], x_recv.at[r], ctx=cx))
        spread(c, r, 0)
        send_pieces(r + 3)
        relay_pieces(r + 2)
        if r >= 2:
            from_partner(r - 2)
    for r in range(N_PART):
        project(0, r)
    xq[...] = qkv[0, :, other]
    q2[xl] = qkv[0, :, mine]
    from_partner(N_PART - 2)
    from_partner(N_PART - 1)
    go(remote(xq, q2.at[xl], x_send.at[N_PART], x_recv.at[N_PART], ctx=cx))
    px_copy = remote(placed.at[pl.ds(0, rows // 2)], px, x_send.at[N_PART + 2], x_recv.at[N_PART + 2], ctx=cx)
    go(px_copy)
    for n, (a, b) in enumerate(((left, right), (left_x, right_x))):
        for r in range(N_PART):
            from_left(a, r, n)
            if r < N_PART // 2:
                to_right(a, r, 2 + n)
            to_sib(a, r, 2 + 3 * n)
            from_right(b, r, n)
            if r >= N_PART // 2:
                to_left(b, r, 2 + n)
            to_sib(b, r, 3 + 3 * n)
    for n, i in enumerate((opp, opp_x)):
        for r in range(N_PART):
            if r < N_PART // 2:
                from_left(i, r, 2 + n)
            else:
                from_right(i, r, 2 + n)
            to_sib(i, r, 4 + 3 * n)

    remote(xq, q2.at[ox], x_send.at[N_PART], x_recv.at[N_PART], ctx=cx).wait_recv()
    remote(xd, do2.at[ox], x_send.at[N_PART + 1], x_recv.at[N_PART + 1], ctx=cx).wait_recv()
    px_copy.wait_recv()
    sc = 1 - core
    theirs = [ctx_id(x, z + dz, sc) for x, dz in ((xl, 0), (ox, 0), (xl, 3), (xl, 1), (ox, 3), (ox, 1), (xl, 2), (ox, 2))]
    for n, i in enumerate(theirs):
        for r in range(N_PART):
            remote(unit(i, r), unit(i, r), s_send.at[r, n], s_recv.at[r, n], ctx=sib).wait_recv()
    for copy in sends:
        copy.wait_send()


def attention_kernel(
    start, q2, do2, kv, o2, dq2, dk_out, dv_out, dkv_acc, acc, m_ref, l_ref
):
    c, core, z, xl = place()
    lower = lax.rem(c, 2 * N_Z)
    n_blk, rows, _ = kv.shape
    half = rows // 2
    mask_per = rows // MASK_BLK
    scale = 1.0 / math.sqrt(HEAD_DIM)
    scale2 = scale * math.log2(math.e)

    def window(blk):
        first = start[blk * mask_per]
        last = start[blk * mask_per + mask_per - 1]
        low = jnp.minimum(first // mask_per, blk)
        clear = jnp.minimum((last + mask_per - 1) // mask_per, blk)
        return low, clear

    low_hi = window(lower + 2 * N_Z)[0]

    for qi in (1, 0):
        blk = lower + 2 * N_Z * qi
        q0 = blk * rows
        queries = q2[qi]
        out_grad = do2[qi]
        queries_t = queries.astype(F32).T.astype(BF16)
        grad_t = out_grad.astype(F32).T.astype(BF16)
        low, clear = window(blk)
        q_start = jnp.concatenate(
            [jnp.full((1, MASK_BLK), start[blk * mask_per + i] * MASK_BLK, jnp.int32) for i in range(mask_per)], axis=1
        )

        def allowed(b, n_key=rows, qo=0, n_q=rows):
            key_pos = b * rows + lax.broadcasted_iota(jnp.int32, (n_key, n_q), 0)
            q_pos = q0 + qo + lax.broadcasted_iota(jnp.int32, (n_key, n_q), 1)
            return (key_pos <= q_pos) & (key_pos >= q_start[:, qo:qo + n_q])

        diagonal = ((rows, half, half), (half, 0, half))

        def forward_diagonal():
            for n_key, qo, n_q in diagonal:
                at = slice(qo, qo + n_q)
                s = jnp.dot(kv[blk, :n_key, :HEAD_DIM], queries_t[:, at], preferred_element_type=F32) * scale2
                s = jnp.where(allowed(blk, n_key, qo, n_q), s, MASKED)
                top = jnp.max(s, axis=0, keepdims=True)
                p = jnp.exp2(s - top)
                m_ref[:, at] = top
                l_ref[:, at] = jnp.sum(p, axis=0, keepdims=True)
                acc[:, at] = lax.dot_general(
                    kv[blk, :n_key, HEAD_DIM:], p.astype(BF16), TN, preferred_element_type=F32
                )

        def forward(blocks, masked):
            scores = [
                lax.dot_general(kv[b, :, :HEAD_DIM], queries_t, NN, preferred_element_type=F32) * scale2 for b in blocks
            ]
            if masked:
                scores = [jnp.where(allowed(b), s, MASKED) for b, s in zip(blocks, scores)]
            m_old = m_ref[...]
            m_new = m_old
            for s in scores:
                m_new = jnp.maximum(m_new, jnp.max(s, axis=0, keepdims=True))
            alpha = jnp.exp2(m_old - m_new)
            m_ref[...] = m_new
            total = l_ref[...] * alpha
            out = acc[...] * alpha
            for b, s in zip(blocks, scores):
                p = jnp.exp2(s - m_new)
                total = total + jnp.sum(p, axis=0, keepdims=True)
                out = out + lax.dot_general(kv[b, :, HEAD_DIM:], p.astype(BF16), TN, preferred_element_type=F32)
            l_ref[...] = total
            acc[...] = out

        def sweep(lo, hi, step):
            pairs = (hi - lo) // 2

            def body(i, carry):
                step([lo + i * 2, lo + i * 2 + 1], False)
                return carry

            def rest(b, carry):
                step([b], False)
                return carry

            lax.fori_loop(0, pairs, body, 0)
            lax.fori_loop(lo + pairs * 2, hi, rest, 0)

        def masked_sweep(lo, hi, step):
            def body(b, carry):
                step([b], True)
                return carry
            lax.fori_loop(lo, hi, body, 0)

        forward_diagonal()
        sweep(clear, blk, forward)
        masked_sweep(low, clear, forward)

        total = l_ref[...]
        out_t = (acc[...] / total).astype(BF16).astype(F32)
        o2[qi] = out_t.T.astype(BF16)
        row_dot = jnp.sum(out_t * out_grad.astype(F32).T, axis=0, keepdims=True)
        log_norm = m_ref[...] + jnp.log2(total)

        def store(b, dk, dv):
            at = pl.ds(pl.multiple_of(b * rows, rows), rows)
            if qi == 1:
                dkv_acc[at, :HEAD_DIM] = dk
                dkv_acc[at, HEAD_DIM:] = dv
            else:
                dk = dk + dkv_acc[at, :HEAD_DIM]
                dv = dv + dkv_acc[at, HEAD_DIM:]
            dk_out[b] = dk.astype(BF16)
            dv_out[b] = dv.astype(BF16)

        def backward_diagonal():
            parts = []
            for n_key, qo, n_q in diagonal:
                at = slice(qo, qo + n_q)
                keys = kv[blk, :n_key, :HEAD_DIM]
                s = jnp.dot(keys, queries_t[:, at], preferred_element_type=F32)
                dp = jnp.dot(kv[blk, :n_key, HEAD_DIM:], grad_t[:, at], preferred_element_type=F32)
                p = jnp.where(allowed(blk, n_key, qo, n_q), jnp.exp2(s * scale2 - log_norm[:, at]), 0.0)
                ds = (p * (dp - row_dot[:, at]) * scale).astype(BF16)
                parts.append((
                    jnp.dot(ds, queries[at], preferred_element_type=F32),
                    jnp.dot(p.astype(BF16), out_grad[at], preferred_element_type=F32),
                ))
                acc[:, at] = lax.dot_general(keys, ds, TN, preferred_element_type=F32)
            (dk, dv), (dk_top, dv_top) = parts
            store(
                blk,
                jnp.concatenate([dk[:half] + dk_top, dk[half:]], axis=0),
                jnp.concatenate([dv[:half] + dv_top, dv[half:]], axis=0),
            )

        def backward(blocks, masked):
            dq = acc[...]
            tiles = []
            for b in blocks:
                s = lax.dot_general(kv[b, :, :HEAD_DIM], queries_t, NN, preferred_element_type=F32)
                dp = lax.dot_general(kv[b, :, HEAD_DIM:], grad_t, NN, preferred_element_type=F32)
                tiles.append((b, s, dp))
            for b, s, dp in tiles:
                p = jnp.exp2(s * scale2 - log_norm)
                if masked:
                    p = jnp.where(allowed(b), p, 0.0)
                ds = (p * (dp - row_dot) * scale).astype(BF16)
                store(
                    b,
                    jnp.dot(ds, queries, preferred_element_type=F32),
                    jnp.dot(p.astype(BF16), out_grad, preferred_element_type=F32),
                )
                dq = dq + lax.dot_general(kv[b, :, :HEAD_DIM], ds, TN, preferred_element_type=F32)
            acc[...] = dq

        if qi == 0:
            def clean(b, carry):
                dkv_acc[pl.ds(pl.multiple_of(b * rows, rows), rows), :] = jnp.zeros((rows, 2 * HEAD_DIM), F32)
                return carry
            lax.fori_loop(low, jnp.minimum(low_hi, blk + 1), clean, 0)
        backward_diagonal()
        sweep(clear, blk, backward)
        masked_sweep(low, clear, backward)
        dq2[qi] = acc[...].T.astype(BF16)

    low_lo = window(lower)[0]

    def blank(b, carry):
        dk_out[b] = jnp.zeros((rows, HEAD_DIM), BF16)
        dv_out[b] = jnp.zeros((rows, HEAD_DIM), BF16)
        return carry

    mid = jnp.maximum(low_hi, lower + 1)
    lax.fori_loop(0, low_lo, blank, 0)
    lax.fori_loop(lower + 1, mid, blank, 0)
    lax.fori_loop(lower + 2 * N_Z + 1, n_blk, blank, 0)


def reduce_kernel(
    n_ctx, dk, dv, dq2, o2, placed, px_top,
    attn_out, qkv_grad, cg,
    sb, part, far_l, far_r, in_l, in_r, res, gx, gdq, go_in,
    px, placed_t, placed_xt, cs_send, cs_recv, mine_sum, rs_out, rs_in,
    s_send, s_recv, f_send, f_recv, n_send, n_recv, x_send, x_recv,
    p_send, p_recv, r_send, r_recv, g_send, g_recv, e_send, e_recv,
):
    c, core, z, xl = place()
    ox = 1 - xl
    cx = ctx_id(ox, z, core)
    sib = ctx_id(xl, z, 1 - core)
    right = ctx_id(xl, z + 1, core)
    left = ctx_id(xl, z + N_Z - 1, core)
    rows = placed.shape[0]
    half = rows // 2
    mine = pl.ds(pl.multiple_of(xl * HEAD_DIM, HEAD_DIM), HEAD_DIM)
    other = pl.ds(pl.multiple_of(ox * HEAD_DIM, HEAD_DIM), HEAD_DIM)
    top, bottom = pl.ds(0, half), pl.ds(half, half)

    order = [(dz, x) for dz in (2, 1, 3, 0) for x in (ox, xl)]
    terms = (dk, dv)

    entry_barrier(n_ctx, 1, c, 0)
    sends = []

    def go(copy):
        copy.start()
        sends.append(copy)

    def sib_copy(v, j):
        dz, x = order[j]
        return remote(terms[v].at[ctx_id(x, z + dz, 1 - core)], sb.at[v, j], s_send.at[v, j], s_recv.at[v, j], ctx=sib)

    for v in (1, 0):
        for j in range(8):
            go(sib_copy(v, j))
    px_copy = remote(placed.at[bottom], px, x_send.at[4], x_recv.at[4], ctx=cx)
    go(px_copy)

    def pair(v, j, at):
        dz, x = order[j]
        return terms[v][ctx_id(x, z + dz, core), at, :].astype(F32) + sb[v, j, at, :].astype(F32)

    def far_copy(v, n, to):
        e = n % 2
        at, buf = ((top, far_l), (bottom, far_r))[n // 2]
        return remote(part.at[v, e, at], buf.at[v, e], f_send.at[v, n], f_recv.at[v, n], ctx=to)

    def near_copy(v, n, to):
        e, way, late = n % 2, (n // 2) % 2, n // 4
        at = (bottom, top)[way] if late == 0 else (top, bottom)[way]
        buf = (in_l, in_r)[way]
        return remote(part.at[v, 2 + 2 * way + e, at], buf.at[v, e, at], n_send.at[v, n], n_recv.at[v, n], ctx=to)

    def send_far(v):
        for e in range(2):
            sib_copy(v, e).wait_recv()
            part[v, e] = pair(v, e, pl.ds(0, rows)).astype(BF16)
            go(far_copy(v, e, right))
            go(far_copy(v, 2 + e, left))

    def send_early(v):
        for e in range(2):
            sib_copy(v, 2 + e).wait_recv()
            part[v, 2 + e, bottom, :] = pair(v, 2 + e, bottom).astype(BF16)
            go(near_copy(v, e, right))
            sib_copy(v, 4 + e).wait_recv()
            part[v, 4 + e, top, :] = pair(v, 4 + e, top).astype(BF16)
            go(near_copy(v, 2 + e, left))

    def send_late(v):
        for e in range(2):
            far_copy(v, e, left).wait_recv()
            part[v, 2 + e, top, :] = (pair(v, 2 + e, top) + far_l[v, e].astype(F32)).astype(BF16)
            go(near_copy(v, 4 + e, right))
            far_copy(v, 2 + e, right).wait_recv()
            part[v, 4 + e, bottom, :] = (pair(v, 4 + e, bottom) + far_r[v, e].astype(F32)).astype(BF16)
            go(near_copy(v, 6 + e, left))

    def block_done(v):
        for e in range(2):
            sib_copy(v, 6 + e).wait_recv()
            for n, src in ((e, left), (2 + e, right), (4 + e, left), (6 + e, right)):
                near_copy(v, n, src).wait_recv()
            total = pair(v, 6 + e, pl.ds(0, rows)) + in_l[v, e].astype(F32) + in_r[v, e].astype(F32)
            res[v, e] = total.astype(BF16)
            if e == 0:
                go(remote(res.at[v, 0], gx.at[v], x_send.at[2 + v], x_recv.at[2 + v], ctx=cx))

    def take_grad(v):
        qkv_grad[1 + v, :, mine] = res[v, 1]
        remote(res.at[v, 0], gx.at[v], x_send.at[2 + v], x_recv.at[2 + v], ctx=cx).wait_recv()
        qkv_grad[1 + v, :, other] = gx[v]

    vis = placed.shape[1]
    vis_half = vis // 2
    n_chip = n_ctx // 2
    chunk = vis_half // N_Z
    chip = c // 2
    own_rows = pl.ds(pl.multiple_of(core * vis_half, vis_half), vis_half)
    sib_rows = pl.ds(pl.multiple_of((1 - core) * vis_half, vis_half), vis_half)

    def chunk_at(zz):
        return pl.ds(pl.multiple_of(zz * chunk, chunk), chunk)

    def final(i, g):
        first = core * vis_half + lax.rem(g, N_Z) * chunk
        cols = pl.ds(pl.multiple_of(g // N_Z * HEAD_DIM, HEAD_DIM), HEAD_DIM)
        return cg.at[i, pl.ds(pl.multiple_of(first, chunk), chunk), cols]

    def conn_start(i, grads, grads_x):
        def term(at):
            return jnp.dot(placed_t[at, :], grads, preferred_element_type=F32) + jnp.dot(
                placed_xt[at, :], grads_x, preferred_element_type=F32
            )

        cs_send[i] = term(sib_rows).astype(BF16)
        go(remote(cs_send.at[i], cs_recv.at[i], p_send.at[i], p_recv.at[i], ctx=sib))
        mine_sum[i] = term(own_rows)

    def scatter_copy(i, k, zz):
        return remote(rs_out.at[i, chunk_at(zz)], rs_in.at[i, k], r_send.at[i, k], r_recv.at[i, k], ctx=ctx_id(xl, zz, core))

    def conn_scatter(i):
        remote(cs_send.at[i], cs_recv.at[i], p_send.at[i], p_recv.at[i], ctx=sib).wait_recv()
        total = mine_sum[i] + cs_recv[i].astype(F32)
        mine_sum[i] = total
        rs_out[i] = total.astype(BF16)
        for k in range(1, N_Z):
            go(scatter_copy(i, k, lax.rem(z + k, N_Z)))

    def conn_gather(i):
        total = mine_sum[i, chunk_at(z), :]
        for k in range(1, N_Z):
            scatter_copy(i, k, lax.rem(z + N_Z - k, N_Z)).wait_recv()
            total = total + rs_in[i, k].astype(F32)
        final(i, chip)[...] = total.astype(BF16)
        for k in range(1, n_chip):
            g = lax.rem(chip + k, n_chip)
            go(remote(final(i, chip), final(i, chip), g_send.at[i, k], g_recv.at[i, k], ctx=g * 2 + core))

    def conn_share(i):
        for k in range(1, n_chip):
            g = lax.rem(chip + n_chip - k, n_chip)
            remote(final(i, g), final(i, g), g_send.at[i, k], g_recv.at[i, k], ctx=g * 2 + core).wait_recv()
        ref = cg.at[i, own_rows]
        go(remote(ref, ref, e_send.at[i], e_recv.at[i], ctx=sib))

    def conn_finish(i):
        ref = cg.at[i, sib_rows]
        remote(ref, ref, e_send.at[i], e_recv.at[i], ctx=sib).wait_recv()

    send_far(1)
    send_early(1)
    send_far(0)
    send_early(0)
    placed_t[...] = placed[...].T
    placed_xt[:, top] = px_top[...].T
    send_late(1)
    send_late(0)
    px_copy.wait_recv()
    placed_xt[:, bottom] = px[...].T
    conn_start(0, dq2[xl], dq2[ox])
    block_done(1)
    conn_start(2, res[1, 1], res[1, 0])
    block_done(0)
    conn_start(1, res[0, 1], res[0, 0])
    conn_scatter(0)
    conn_scatter(2)
    conn_scatter(1)
    go(remote(dq2.at[ox], gdq, x_send.at[0], x_recv.at[0], ctx=cx))
    go(remote(o2.at[ox], go_in, x_send.at[1], x_recv.at[1], ctx=cx))
    conn_gather(0)
    conn_gather(2)
    conn_gather(1)
    take_grad(1)
    take_grad(0)
    remote(dq2.at[ox], gdq, x_send.at[0], x_recv.at[0], ctx=cx).wait_recv()
    qkv_grad[0, :, mine] = dq2[xl]
    qkv_grad[0, :, other] = gdq[...]
    remote(o2.at[ox], go_in, x_send.at[1], x_recv.at[1], ctx=cx).wait_recv()
    attn_out[:, mine] = o2[xl]
    attn_out[:, other] = go_in[...]
    for i in (0, 2, 1):
        conn_share(i)
    for i in (0, 2, 1):
        conn_finish(i)
    for copy in sends:
        copy.wait_send()


def finish_kernel(attn_in, grad_in, conn_in, attn_out, grad_out, conn_out, conn, sem):
    copies = [pltpu.make_async_copy(attn_in, attn_out, sem.at[0]), pltpu.make_async_copy(grad_in, grad_out, sem.at[1])]
    for copy in copies:
        copy.start()
    for i in range(3):
        conn[i] = conn_in[i].astype(F32)
        copy = pltpu.make_async_copy(conn.at[i], conn_out.at[i], sem.at[2 + i])
        copy.start()
        copies.append(copy)
    for copy in copies:
        copy.wait()


def local(base_qkv, frames, frame_block, frame_slot, frame_live, start_block, conn_w, d_out):
    n_ctx = lax.axis_size("ctx")
    n_tp = lax.axis_size("tp")
    _, rows, width = base_qkv.shape
    vis = frames.shape[2]
    pw = vis // n_tp
    half = rows // 2
    two = 2 * HEAD_DIM
    piece = FRAME_TOK + CODE_ROWS
    vmem = pl.BlockSpec(memory_space=pltpu.VMEM)
    smem = pl.BlockSpec(memory_space=pltpu.SMEM)
    hbm = pl.BlockSpec(memory_space=pltpu.HBM)
    dma = pltpu.SemaphoreType.DMA

    def buf(*shape):
        return pltpu.VMEM(shape, BF16)

    def kept(*arrays, space=pltpu.VMEM):
        return [pltpu.with_memory_space_constraint(x, space) for x in arrays]

    def params(n):
        return pltpu.CompilerParams(collective_id=n, has_side_effects=True, vmem_limit_bytes=VMEM_LIMIT)

    placed, q2, do2, kv, px = pl.pallas_call(
        lambda *refs: gather_kernel(n_ctx, n_tp, *refs),
        out_shape=(
            buf(rows, vis), buf(2, rows, HEAD_DIM), buf(2, rows, HEAD_DIM), buf(n_ctx, rows, two),
            buf(rows // 2, vis),
        ),
        in_specs=[smem, smem, smem, hbm, hbm, hbm, hbm],
        out_specs=(vmem,) * 5,
        scratch_shapes=[
            pltpu.VMEM((n_tp, piece, pw), BF16),
            pltpu.VMEM((n_tp, piece, pw), BF16),
            pltpu.VMEM((n_ctx, piece, pw), BF16),
            pltpu.VMEM((n_ctx, piece, pw), BF16),
            pltpu.VMEM((1, FRAME_TOK, vis), BF16),
            pltpu.VMEM((rows, width), BF16),
            pltpu.VMEM((3, rows, width), BF16),
            pltpu.VMEM((3, vis, width), BF16),
            pltpu.VMEM((3, rows, width), BF16),
            pltpu.VMEM((N_PART, rows // N_PART, two), BF16),
            pltpu.VMEM((rows, HEAD_DIM), BF16),
            pltpu.VMEM((rows, HEAD_DIM), BF16),
            dma((4,)), dma((n_tp,)), dma((n_tp,)), dma((n_ctx,)), dma((n_ctx,)), dma((N_PART, 7)), dma((N_PART, 7)),
            dma((N_PART + 3,)), dma((N_PART + 3,)), dma((2, N_PART, 4)), dma((2, N_PART, 4)),
            dma((N_PART, 8)), dma((N_PART, 8)),
        ],
        compiler_params=params(0),
        name="gather",
    )(
        frame_block, frame_slot, frame_live,
        *kept(frames, base_qkv, conn_w.transpose(1, 0, 2), d_out, space=pltpu.HBM),
    )

    o2, dq2, dk, dv = pl.pallas_call(
        attention_kernel,
        out_shape=(
            buf(2, rows, HEAD_DIM), buf(2, rows, HEAD_DIM), buf(n_ctx, rows, HEAD_DIM), buf(n_ctx, rows, HEAD_DIM),
        ),
        in_specs=[smem, vmem, vmem, vmem],
        out_specs=(vmem, vmem, vmem, vmem),
        scratch_shapes=[
            pltpu.VMEM((n_ctx * rows, two), F32),
            pltpu.VMEM((HEAD_DIM, rows), F32),
            pltpu.VMEM((1, rows), F32),
            pltpu.VMEM((1, rows), F32),
        ],
        compiler_params=pltpu.CompilerParams(vmem_limit_bytes=VMEM_LIMIT),
        name="attention",
    )(*kept(start_block, space=pltpu.SMEM), *kept(q2, do2, kv))

    vis_half = vis // 2
    n_chip = n_ctx // 2
    attn_out, qkv_grad, conn = pl.pallas_call(
        lambda *refs: reduce_kernel(n_ctx, *refs),
        out_shape=(buf(rows, width), buf(3, rows, width), buf(3, vis, width)),
        in_specs=[vmem] * 6,
        out_specs=(vmem, vmem, vmem),
        scratch_shapes=[
            pltpu.VMEM((2, 8, rows, HEAD_DIM), BF16),
            pltpu.VMEM((2, 6, rows, HEAD_DIM), BF16),
            pltpu.VMEM((2, 2, half, HEAD_DIM), BF16),
            pltpu.VMEM((2, 2, half, HEAD_DIM), BF16),
            pltpu.VMEM((2, 2, rows, HEAD_DIM), BF16),
            pltpu.VMEM((2, 2, rows, HEAD_DIM), BF16),
            pltpu.VMEM((2, 2, rows, HEAD_DIM), BF16),
            pltpu.VMEM((2, rows, HEAD_DIM), BF16),
            pltpu.VMEM((rows, HEAD_DIM), BF16),
            pltpu.VMEM((rows, HEAD_DIM), BF16),
            pltpu.VMEM((half, vis), BF16),
            pltpu.VMEM((vis, rows), BF16),
            pltpu.VMEM((vis, rows), BF16),
            pltpu.VMEM((3, vis_half, HEAD_DIM), BF16),
            pltpu.VMEM((3, vis_half, HEAD_DIM), BF16),
            pltpu.VMEM((3, vis_half, HEAD_DIM), F32),
            pltpu.VMEM((3, vis_half, HEAD_DIM), BF16),
            pltpu.VMEM((3, N_Z, vis_half // N_Z, HEAD_DIM), BF16),
            dma((2, 8)), dma((2, 8)), dma((2, 4)), dma((2, 4)), dma((2, 8)), dma((2, 8)), dma((5,)), dma((5,)),
            dma((3,)), dma((3,)), dma((3, N_Z)), dma((3, N_Z)), dma((3, n_chip)), dma((3, n_chip)),
            dma((3,)), dma((3,)),
        ],
        compiler_params=params(1),
        name="reduce",
    )(*kept(dk, dv, dq2, o2, placed, px))

    out = pl.BlockSpec(memory_space=pl.ANY)
    attn_out, qkv_grad, conn = pl.pallas_call(
        finish_kernel,
        out_shape=(
            jax.ShapeDtypeStruct((rows, width), BF16), jax.ShapeDtypeStruct((3, rows, width), BF16),
            jax.ShapeDtypeStruct((3, vis, width), F32),
        ),
        in_specs=[vmem] * 3,
        out_specs=(out, out, out),
        scratch_shapes=[pltpu.VMEM((3, vis, width), F32), dma((5,))],
        compiler_params=pltpu.CompilerParams(vmem_limit_bytes=VMEM_LIMIT),
        name="finish",
    )(*kept(attn_out, qkv_grad, conn))
    return (attn_out, qkv_grad, conn.transpose(1, 0, 2))


def solution(mesh):
    return jax.shard_map(
        local,
        mesh=mesh,
        in_specs=(
            P(None, "ctx", "tp"),
            P(("ctx", "tp"), None, None),
            P(("ctx", "tp")),
            P(("ctx", "tp")),
            P(("ctx", "tp")),
            P(),
            P(None, None, "tp"),
            P("ctx", "tp"),
        ),
        out_specs=(P("ctx", "tp"), P(None, "ctx", "tp"), P(None, None, "tp")),
        check_vma=False,
    )
```

```python
import math

import jax
import jax.numpy as jnp
from jax import lax
from jax.experimental import pallas as pl
from jax.experimental.pallas import tpu as pltpu
from jax.sharding import PartitionSpec as P

HEAD_DIM = 128
FRAME_TOK = 32
MASK_BLK = 128
CODE_ROWS = 16
N_Z = 4
N_PART = 4
MASKED = -1e30
MESH = pl.DeviceIdType.MESH
F32 = jnp.float32
BF16 = jnp.bfloat16
VMEM_LIMIT = 20 * 1024 * 1024

NN = (((1,), (0,)), ((), ()))
TN = (((0,), (0,)), ((), ()))


def place():
    c = lax.axis_index("ctx")
    core = c % 2
    z = (c // 2) % N_Z
    xl = c // (2 * N_Z)
    return c, core, z, xl


def ctx_id(xl, z, core):
    return xl * (2 * N_Z) + lax.rem(z, N_Z) * 2 + core


def entry_barrier(n_ctx, n_tp, c, t):
    barrier = pltpu.get_barrier_semaphore()
    for k in range(1, n_tp):
        pl.semaphore_signal(barrier, inc=1, device_id={"tp": lax.rem(t + k, n_tp)}, device_id_type=MESH)
    for k in range(1, n_ctx):
        pl.semaphore_signal(barrier, inc=1, device_id={"ctx": lax.rem(c + k, n_ctx)}, device_id_type=MESH)
    pl.semaphore_wait(barrier, n_tp - 1 + n_ctx - 1)


def remote(src, dst, send, recv, **where):
    return pltpu.make_async_remote_copy(
        src_ref=src, dst_ref=dst, send_sem=send, recv_sem=recv, device_id=where, device_id_type=MESH
    )


def gather_kernel(
    n_ctx, n_tp, fb, fs, fl, frames_hbm, base_hbm, w_hbm, dout_hbm,
    placed, q2, do2, kv, px,
    s_a, r_a, s_b, r_b, frames, dout, base, w, qkv, xs, xq, xd,
    load_sem, a_send, a_recv, b_send, b_recv, c_send, c_recv,
    x_send, x_recv, z_send, z_recv, s_send, s_recv,
):
    c, core, z, xl = place()
    t = lax.axis_index("tp")
    pw = frames.shape[2] // n_tp
    rows = placed.shape[0]
    part = rows // N_PART
    ox = 1 - xl
    cx = ctx_id(ox, z, core)
    sib = ctx_id(xl, z, 1 - core)
    mine = pl.ds(pl.multiple_of(xl * HEAD_DIM, HEAD_DIM), HEAD_DIM)
    other = pl.ds(pl.multiple_of(ox * HEAD_DIM, HEAD_DIM), HEAD_DIM)

    load_f = pltpu.make_async_copy(frames_hbm, frames, load_sem.at[2])
    load_d = pltpu.make_async_copy(dout_hbm, dout, load_sem.at[3])
    load_w = pltpu.make_async_copy(w_hbm, w, load_sem.at[0])
    load_b = pltpu.make_async_copy(base_hbm, base, load_sem.at[1])
    load_f.start()
    load_w.start()
    load_b.start()
    load_d.start()

    code = jnp.where(fl[0] == 1, fb[0] * (rows // FRAME_TOK) + fs[0] + 1, 0).astype(F32)
    code_rows = jnp.full((CODE_ROWS, pw), code, F32).astype(BF16)
    load_f.wait()
    for p in range(n_tp):
        s_a[p, :FRAME_TOK, :] = frames[0, :, p * pw:(p + 1) * pw]
        s_a[p, FRAME_TOK:, :] = code_rows

    entry_barrier(n_ctx, n_tp, c, t)

    sends = []

    def go(copy):
        copy.start()
        sends.append(copy)

    for k in range(1, n_tp):
        p = lax.rem(t + k, n_tp)
        go(remote(s_a.at[p], r_a.at[t], a_send.at[k], a_recv.at[k], tp=p))
    r_a[t] = s_a[t]
    load_d.wait()
    xd[...] = dout[:, other]
    do2[xl] = dout[:, mine]
    go(remote(xd, do2.at[xl], x_send.at[N_PART + 1], x_recv.at[N_PART + 1], ctx=cx))
    for k in range(1, n_tp):
        p = lax.rem(t + n_tp - k, n_tp)
        remote(s_a.at[p], r_a.at[p], a_send.at[k], a_recv.at[k], tp=p).wait_recv()

    slots = rows // FRAME_TOK
    pieces = r_a[...].astype(F32)
    codes = pieces[:, FRAME_TOK:FRAME_TOK + 1, :]
    for k in range(n_ctx):
        d = lax.rem(c + k, n_ctx)
        low = (d * slots).astype(F32)
        hit = (codes > low) & (codes < low + (slots + 0.5))
        s_b[k] = jnp.sum(jnp.where(hit, pieces, 0.0), axis=0).astype(BF16)
        if k:
            go(remote(s_b.at[k], r_b.at[c], b_send.at[k], b_recv.at[k], ctx=d))
    r_b[c] = s_b[0]
    for k in range(1, n_ctx):
        d = lax.rem(c + n_ctx - k, n_ctx)
        remote(s_b.at[k], r_b.at[d], b_send.at[k], b_recv.at[k], ctx=d).wait_recv()

    arrived = r_b[...].astype(F32)
    codes = arrived[:, FRAME_TOK:FRAME_TOK + 1, :]
    rows_in = arrived[:, :FRAME_TOK, :]
    y = t // 2
    xh = t % 2

    def tp_id(y_at, x_at):
        return lax.rem(y_at, n_tp // 2) * 2 + x_at

    def piece(p, first, count):
        return placed.at[pl.ds(first, count), pl.ds(pl.multiple_of(p * pw, pw), pw)]

    if n_tp > 1:
        n_y = n_tp // 2
        up, up_x = tp_id(y + 1, xh), tp_id(y + 1, 1 - xh)
        down, down_x = tp_id(y + n_y - 1, xh), tp_id(y + n_y - 1, 1 - xh)
        far, far_x = tp_id(y + 2, xh), tp_id(y + 2, 1 - xh)
        xp = tp_id(y, 1 - xh)

    def c_copy(r, n, p, to):
        ref = piece(p, r * part, part)
        return remote(ref, ref, c_send.at[r, n], c_recv.at[r, n], tp=to)

    def place_rows(r):
        for s in range(r * slots // N_PART, (r + 1) * slots // N_PART):
            want = (c * slots + (s + 1)).astype(F32)
            piece(t, s * FRAME_TOK, FRAME_TOK)[...] = jnp.sum(
                jnp.where(codes == want, rows_in, 0.0), axis=0
            ).astype(BF16)

    def send_pieces(r):
        if n_tp > 1 and r < N_PART:
            go(c_copy(r, 0, t, xp))
            go(c_copy(r, 1, t, up))
            go(c_copy(r, 2, t, down))
            go(c_copy(r, 3, t, far))

    def relay_pieces(r):
        if n_tp > 1 and r < N_PART:
            c_copy(r, 0, xp, xp).wait_recv()
            go(c_copy(r, 4, xp, up))
            go(c_copy(r, 5, xp, down))
            c_copy(r, 3, far, far).wait_recv()
            go(c_copy(r, 6, far, xp))

    def wait_pieces(r):
        if n_tp > 1:
            for n, p in ((1, down), (2, up), (4, down_x), (5, up_x), (6, far_x)):
                c_copy(r, n, p, p).wait_recv()

    place_rows(0)
    send_pieces(0)
    place_rows(1)
    send_pieces(1)
    for r in range(2, N_PART):
        place_rows(r)
    relay_pieces(0)
    send_pieces(2)
    relay_pieces(1)

    right = ctx_id(xl, z + 1, core)
    left = ctx_id(xl, z + N_Z - 1, core)
    opp = ctx_id(xl, z + 2, core)
    right_x = ctx_id(ox, z + 1, core)
    left_x = ctx_id(ox, z + N_Z - 1, core)
    opp_x = ctx_id(ox, z + 2, core)

    def unit(i, r):
        return kv.at[i, pl.ds(r * part, part)]

    def to_right(i, r, n):
        go(remote(unit(i, r), unit(i, r), z_send.at[0, r, n], z_recv.at[0, r, n], ctx=right))

    def to_left(i, r, n):
        go(remote(unit(i, r), unit(i, r), z_send.at[1, r, n], z_recv.at[1, r, n], ctx=left))

    def to_sib(i, r, n):
        go(remote(unit(i, r), unit(i, r), s_send.at[r, n], s_recv.at[r, n], ctx=sib))

    def from_left(i, r, n):
        remote(unit(i, r), unit(i, r), z_send.at[0, r, n], z_recv.at[0, r, n], ctx=left).wait_recv()

    def from_right(i, r, n):
        remote(unit(i, r), unit(i, r), z_send.at[1, r, n], z_recv.at[1, r, n], ctx=right).wait_recv()

    def spread(i, r, n):
        to_right(i, r, n)
        to_left(i, r, n)
        to_sib(i, r, n)

    def from_partner(r):
        remote(xs.at[r], unit(cx, r), x_send.at[r], x_recv.at[r], ctx=cx).wait_recv()
        spread(cx, r, 1)

    def project(i, r):
        at = slice(r * part, (r + 1) * part)
        term = jnp.dot(placed[at, :], w[i], preferred_element_type=F32)
        qkv[i, at, :] = (base[i, at, :].astype(F32) + term).astype(BF16)

    load_w.wait()
    load_b.wait()
    for r in range(N_PART):
        at = slice(r * part, (r + 1) * part)
        wait_pieces(r)
        project(1, r)
        project(2, r)
        xs[r, :, :HEAD_DIM] = qkv[1, at, other]
        xs[r, :, HEAD_DIM:] = qkv[2, at, other]
        kv[c, at, :HEAD_DIM] = qkv[1, at, mine]
        kv[c, at, HEAD_DIM:] = qkv[2, at, mine]
        go(remote(xs.at[r], unit(c, r), x_send.at[r], x_recv.at[r], ctx=cx))
        spread(c, r, 0)
        send_pieces(r + 3)
        relay_pieces(r + 2)
        if r >= 2:
            from_partner(r - 2)
    for r in range(N_PART):
        project(0, r)
    xq[...] = qkv[0, :, other]
    q2[xl] = qkv[0, :, mine]
    from_partner(N_PART - 2)
    from_partner(N_PART - 1)
    go(remote(xq, q2.at[xl], x_send.at[N_PART], x_recv.at[N_PART], ctx=cx))
    px_copy = remote(placed.at[pl.ds(0, rows // 2)], px, x_send.at[N_PART + 2], x_recv.at[N_PART + 2], ctx=cx)
    go(px_copy)
    for n, (a, b) in enumerate(((left, right), (left_x, right_x))):
        for r in range(N_PART):
            from_left(a, r, n)
            if r < N_PART // 2:
                to_right(a, r, 2 + n)
            to_sib(a, r, 2 + 3 * n)
            from_right(b, r, n)
            if r >= N_PART // 2:
                to_left(b, r, 2 + n)
            to_sib(b, r, 3 + 3 * n)
    for n, i in enumerate((opp, opp_x)):
        for r in range(N_PART):
            if r < N_PART // 2:
                from_left(i, r, 2 + n)
            else:
                from_right(i, r, 2 + n)
            to_sib(i, r, 4 + 3 * n)

    remote(xq, q2.at[ox], x_send.at[N_PART], x_recv.at[N_PART], ctx=cx).wait_recv()
    remote(xd, do2.at[ox], x_send.at[N_PART + 1], x_recv.at[N_PART + 1], ctx=cx).wait_recv()
    px_copy.wait_recv()
    sc = 1 - core
    theirs = [ctx_id(x, z + dz, sc) for x, dz in ((xl, 0), (ox, 0), (xl, 3), (xl, 1), (ox, 3), (ox, 1), (xl, 2), (ox, 2))]
    for n, i in enumerate(theirs):
        for r in range(N_PART):
            remote(unit(i, r), unit(i, r), s_send.at[r, n], s_recv.at[r, n], ctx=sib).wait_recv()
    for copy in sends:
        copy.wait_send()


def attention_kernel(
    start, q2, do2, kv, o2, dq2, dk_out, dv_out, dkv_acc, acc, m_ref, l_ref
):
    c, core, z, xl = place()
    lower = lax.rem(c, 2 * N_Z)
    n_blk, rows, _ = kv.shape
    half = rows // 2
    mask_per = rows // MASK_BLK
    scale = 1.0 / math.sqrt(HEAD_DIM)
    scale2 = scale * math.log2(math.e)

    def window(blk):
        first = start[blk * mask_per]
        last = start[blk * mask_per + mask_per - 1]
        low = jnp.minimum(first // mask_per, blk)
        clear = jnp.minimum((last + mask_per - 1) // mask_per, blk)
        return low, clear

    low_hi = window(lower + 2 * N_Z)[0]

    for qi in (1, 0):
        blk = lower + 2 * N_Z * qi
        q0 = blk * rows
        queries = q2[qi]
        out_grad = do2[qi]
        queries_t = queries.astype(F32).T.astype(BF16)
        grad_t = out_grad.astype(F32).T.astype(BF16)
        low, clear = window(blk)
        q_start = jnp.concatenate(
            [jnp.full((1, MASK_BLK), start[blk * mask_per + i] * MASK_BLK, jnp.int32) for i in range(mask_per)], axis=1
        )

        def allowed(b, n_key=rows, qo=0, n_q=rows):
            key_pos = b * rows + lax.broadcasted_iota(jnp.int32, (n_key, n_q), 0)
            q_pos = q0 + qo + lax.broadcasted_iota(jnp.int32, (n_key, n_q), 1)
            return (key_pos <= q_pos) & (key_pos >= q_start[:, qo:qo + n_q])

        diagonal = ((rows, half, half), (half, 0, half))

        def forward_diagonal():
            for n_key, qo, n_q in diagonal:
                at = slice(qo, qo + n_q)
                s = jnp.dot(kv[blk, :n_key, :HEAD_DIM], queries_t[:, at], preferred_element_type=F32) * scale2
                s = jnp.where(allowed(blk, n_key, qo, n_q), s, MASKED)
                top = jnp.max(s, axis=0, keepdims=True)
                p = jnp.exp2(s - top)
                m_ref[:, at] = top
                l_ref[:, at] = jnp.sum(p, axis=0, keepdims=True)
                acc[:, at] = lax.dot_general(
                    kv[blk, :n_key, HEAD_DIM:], p.astype(BF16), TN, preferred_element_type=F32
                )

        def forward(blocks, masked):
            scores = [
                lax.dot_general(kv[b, :, :HEAD_DIM], queries_t, NN, preferred_element_type=F32) * scale2 for b in blocks
            ]
            if masked:
                scores = [jnp.where(allowed(b), s, MASKED) for b, s in zip(blocks, scores)]
            m_old = m_ref[...]
            m_new = m_old
            for s in scores:
                m_new = jnp.maximum(m_new, jnp.max(s, axis=0, keepdims=True))
            alpha = jnp.exp2(m_old - m_new)
            m_ref[...] = m_new
            total = l_ref[...] * alpha
            out = acc[...] * alpha
            for b, s in zip(blocks, scores):
                p = jnp.exp2(s - m_new)
                total = total + jnp.sum(p, axis=0, keepdims=True)
                out = out + lax.dot_general(kv[b, :, HEAD_DIM:], p.astype(BF16), TN, preferred_element_type=F32)
            l_ref[...] = total
            acc[...] = out

        def sweep(lo, hi, step):
            pairs = (hi - lo) // 2

            def body(i, carry):
                step([lo + i * 2, lo + i * 2 + 1], False)
                return carry

            def rest(b, carry):
                step([b], False)
                return carry

            lax.fori_loop(0, pairs, body, 0)
            lax.fori_loop(lo + pairs * 2, hi, rest, 0)

        def masked_sweep(lo, hi, step):
            def body(b, carry):
                step([b], True)
                return carry
            lax.fori_loop(lo, hi, body, 0)

        forward_diagonal()
        sweep(clear, blk, forward)
        masked_sweep(low, clear, forward)

        total = l_ref[...]
        out_t = (acc[...] / total).astype(BF16).astype(F32)
        o2[qi] = out_t.T.astype(BF16)
        row_dot = jnp.sum(out_t * out_grad.astype(F32).T, axis=0, keepdims=True)
        log_norm = m_ref[...] + jnp.log2(total)

        def store(b, dk, dv):
            at = pl.ds(pl.multiple_of(b * rows, rows), rows)
            if qi == 1:
                dkv_acc[at, :HEAD_DIM] = dk
                dkv_acc[at, HEAD_DIM:] = dv
            else:
                dk = dk + dkv_acc[at, :HEAD_DIM]
                dv = dv + dkv_acc[at, HEAD_DIM:]
            dk_out[b] = dk.astype(BF16)
            dv_out[b] = dv.astype(BF16)

        def backward_diagonal():
            parts = []
            for n_key, qo, n_q in diagonal:
                at = slice(qo, qo + n_q)
                keys = kv[blk, :n_key, :HEAD_DIM]
                s = jnp.dot(keys, queries_t[:, at], preferred_element_type=F32)
                dp = jnp.dot(kv[blk, :n_key, HEAD_DIM:], grad_t[:, at], preferred_element_type=F32)
                p = jnp.where(allowed(blk, n_key, qo, n_q), jnp.exp2(s * scale2 - log_norm[:, at]), 0.0)
                ds = (p * (dp - row_dot[:, at]) * scale).astype(BF16)
                parts.append((
                    jnp.dot(ds, queries[at], preferred_element_type=F32),
                    jnp.dot(p.astype(BF16), out_grad[at], preferred_element_type=F32),
                ))
                acc[:, at] = lax.dot_general(keys, ds, TN, preferred_element_type=F32)
            (dk, dv), (dk_top, dv_top) = parts
            store(
                blk,
                jnp.concatenate([dk[:half] + dk_top, dk[half:]], axis=0),
                jnp.concatenate([dv[:half] + dv_top, dv[half:]], axis=0),
            )

        def backward(blocks, masked):
            dq = acc[...]
            tiles = []
            for b in blocks:
                s = lax.dot_general(kv[b, :, :HEAD_DIM], queries_t, NN, preferred_element_type=F32)
                dp = lax.dot_general(kv[b, :, HEAD_DIM:], grad_t, NN, preferred_element_type=F32)
                tiles.append((b, s, dp))
            for b, s, dp in tiles:
                p = jnp.exp2(s * scale2 - log_norm)
                if masked:
                    p = jnp.where(allowed(b), p, 0.0)
                ds = (p * (dp - row_dot) * scale).astype(BF16)
                store(
                    b,
                    jnp.dot(ds, queries, preferred_element_type=F32),
                    jnp.dot(p.astype(BF16), out_grad, preferred_element_type=F32),
                )
                dq = dq + lax.dot_general(kv[b, :, :HEAD_DIM], ds, TN, preferred_element_type=F32)
            acc[...] = dq

        if qi == 0:
            def clean(b, carry):
                dkv_acc[pl.ds(pl.multiple_of(b * rows, rows), rows), :] = jnp.zeros((rows, 2 * HEAD_DIM), F32)
                return carry
            lax.fori_loop(low, jnp.minimum(low_hi, blk + 1), clean, 0)
        backward_diagonal()
        sweep(clear, blk, backward)
        masked_sweep(low, clear, backward)
        dq2[qi] = acc[...].T.astype(BF16)

    low_lo = window(lower)[0]

    def blank(b, carry):
        dk_out[b] = jnp.zeros((rows, HEAD_DIM), BF16)
        dv_out[b] = jnp.zeros((rows, HEAD_DIM), BF16)
        return carry

    mid = jnp.maximum(low_hi, lower + 1)
    lax.fori_loop(0, low_lo, blank, 0)
    lax.fori_loop(lower + 1, mid, blank, 0)
    lax.fori_loop(lower + 2 * N_Z + 1, n_blk, blank, 0)


def reduce_kernel(
    n_ctx, dk, dv, dq2, o2, placed, px_top,
    attn_out, qkv_grad, cg,
    sb, part, far_l, far_r, in_l, in_r, res, gx, gdq, go_in,
    px, placed_t, placed_xt, cs_send, cs_recv, mine_sum, rs_out, rs_in,
    s_send, s_recv, f_send, f_recv, n_send, n_recv, x_send, x_recv,
    p_send, p_recv, r_send, r_recv, g_send, g_recv, e_send, e_recv,
):
    c, core, z, xl = place()
    ox = 1 - xl
    cx = ctx_id(ox, z, core)
    sib = ctx_id(xl, z, 1 - core)
    right = ctx_id(xl, z + 1, core)
    left = ctx_id(xl, z + N_Z - 1, core)
    rows = placed.shape[0]
    half = rows // 2
    mine = pl.ds(pl.multiple_of(xl * HEAD_DIM, HEAD_DIM), HEAD_DIM)
    other = pl.ds(pl.multiple_of(ox * HEAD_DIM, HEAD_DIM), HEAD_DIM)
    top, bottom = pl.ds(0, half), pl.ds(half, half)

    order = [(dz, x) for dz in (2, 1, 3, 0) for x in (ox, xl)]
    terms = (dk, dv)

    barrier = pltpu.get_barrier_semaphore()
    pl.semaphore_signal(barrier, inc=1, device_id={"ctx": sib}, device_id_type=MESH)
    for k in range(1, n_ctx // 2):
        pl.semaphore_signal(barrier, inc=1, device_id={"ctx": lax.rem(c + 2 * k, n_ctx)}, device_id_type=MESH)
    pl.semaphore_wait(barrier, n_ctx // 2)
    sends = []

    def go(copy):
        copy.start()
        sends.append(copy)

    def sib_copy(v, j):
        dz, x = order[j]
        return remote(terms[v].at[ctx_id(x, z + dz, 1 - core)], sb.at[v, j], s_send.at[v, j], s_recv.at[v, j], ctx=sib)

    for v in (1, 0):
        for j in range(8):
            go(sib_copy(v, j))
    px_copy = remote(placed.at[bottom], px, x_send.at[4], x_recv.at[4], ctx=cx)
    go(px_copy)

    def pair(v, j, at):
        dz, x = order[j]
        return terms[v][ctx_id(x, z + dz, core), at, :].astype(F32) + sb[v, j, at, :].astype(F32)

    def far_copy(v, n, to):
        e = n % 2
        at, buf = ((top, far_l), (bottom, far_r))[n // 2]
        return remote(part.at[v, e, at], buf.at[v, e], f_send.at[v, n], f_recv.at[v, n], ctx=to)

    def near_copy(v, n, to):
        e, way, late = n % 2, (n // 2) % 2, n // 4
        at = (bottom, top)[way] if late == 0 else (top, bottom)[way]
        buf = (in_l, in_r)[way]
        return remote(part.at[v, 2 + 2 * way + e, at], buf.at[v, e, at], n_send.at[v, n], n_recv.at[v, n], ctx=to)

    def send_far(v):
        for e in range(2):
            sib_copy(v, e).wait_recv()
            part[v, e] = pair(v, e, pl.ds(0, rows)).astype(BF16)
            go(far_copy(v, e, right))
            go(far_copy(v, 2 + e, left))

    def send_early(v):
        for e in range(2):
            sib_copy(v, 2 + e).wait_recv()
            part[v, 2 + e, bottom, :] = pair(v, 2 + e, bottom).astype(BF16)
            go(near_copy(v, e, right))
            sib_copy(v, 4 + e).wait_recv()
            part[v, 4 + e, top, :] = pair(v, 4 + e, top).astype(BF16)
            go(near_copy(v, 2 + e, left))

    def send_late(v):
        for e in range(2):
            far_copy(v, e, left).wait_recv()
            part[v, 2 + e, top, :] = (pair(v, 2 + e, top) + far_l[v, e].astype(F32)).astype(BF16)
            go(near_copy(v, 4 + e, right))
            far_copy(v, 2 + e, right).wait_recv()
            part[v, 4 + e, bottom, :] = (pair(v, 4 + e, bottom) + far_r[v, e].astype(F32)).astype(BF16)
            go(near_copy(v, 6 + e, left))

    def block_done(v):
        for e in range(2):
            sib_copy(v, 6 + e).wait_recv()
            for n, src in ((e, left), (2 + e, right), (4 + e, left), (6 + e, right)):
                near_copy(v, n, src).wait_recv()
            total = pair(v, 6 + e, pl.ds(0, rows)) + in_l[v, e].astype(F32) + in_r[v, e].astype(F32)
            res[v, e] = total.astype(BF16)
            if e == 0:
                go(remote(res.at[v, 0], gx.at[v], x_send.at[2 + v], x_recv.at[2 + v], ctx=cx))

    def take_grad(v):
        qkv_grad[1 + v, :, mine] = res[v, 1]
        remote(res.at[v, 0], gx.at[v], x_send.at[2 + v], x_recv.at[2 + v], ctx=cx).wait_recv()
        qkv_grad[1 + v, :, other] = gx[v]

    vis = placed.shape[1]
    vis_half = vis // 2
    n_chip = n_ctx // 2
    chunk = vis_half // N_Z
    chip = c // 2
    own_rows = pl.ds(pl.multiple_of(core * vis_half, vis_half), vis_half)
    sib_rows = pl.ds(pl.multiple_of((1 - core) * vis_half, vis_half), vis_half)

    def chunk_at(zz):
        return pl.ds(pl.multiple_of(zz * chunk, chunk), chunk)

    def final(i, g):
        first = core * vis_half + lax.rem(g, N_Z) * chunk
        cols = pl.ds(pl.multiple_of(g // N_Z * HEAD_DIM, HEAD_DIM), HEAD_DIM)
        return cg.at[i, pl.ds(pl.multiple_of(first, chunk), chunk), cols]

    def conn_start(i, grads, grads_x):
        def term(at):
            return jnp.dot(placed_t[at, :], grads, preferred_element_type=F32) + jnp.dot(
                placed_xt[at, :], grads_x, preferred_element_type=F32
            )

        cs_send[i] = term(sib_rows).astype(BF16)
        go(remote(cs_send.at[i], cs_recv.at[i], p_send.at[i], p_recv.at[i], ctx=sib))
        mine_sum[i] = term(own_rows)

    def scatter_copy(i, k, zz):
        return remote(rs_out.at[i, chunk_at(zz)], rs_in.at[i, k], r_send.at[i, k], r_recv.at[i, k], ctx=ctx_id(xl, zz, core))

    def conn_scatter(i):
        remote(cs_send.at[i], cs_recv.at[i], p_send.at[i], p_recv.at[i], ctx=sib).wait_recv()
        total = mine_sum[i] + cs_recv[i].astype(F32)
        mine_sum[i] = total
        rs_out[i] = total.astype(BF16)
        for k in range(1, N_Z):
            go(scatter_copy(i, k, lax.rem(z + k, N_Z)))

    def conn_gather(i):
        total = mine_sum[i, chunk_at(z), :]
        for k in range(1, N_Z):
            scatter_copy(i, k, lax.rem(z + N_Z - k, N_Z)).wait_recv()
            total = total + rs_in[i, k].astype(F32)
        final(i, chip)[...] = total.astype(BF16)
        for k in range(1, n_chip):
            g = lax.rem(chip + k, n_chip)
            go(remote(final(i, chip), final(i, chip), g_send.at[i, k], g_recv.at[i, k], ctx=g * 2 + core))

    def conn_share(i):
        for k in range(1, n_chip):
            g = lax.rem(chip + n_chip - k, n_chip)
            remote(final(i, g), final(i, g), g_send.at[i, k], g_recv.at[i, k], ctx=g * 2 + core).wait_recv()
        ref = cg.at[i, own_rows]
        go(remote(ref, ref, e_send.at[i], e_recv.at[i], ctx=sib))

    def conn_finish(i):
        ref = cg.at[i, sib_rows]
        remote(ref, ref, e_send.at[i], e_recv.at[i], ctx=sib).wait_recv()

    send_far(1)
    send_early(1)
    send_far(0)
    send_early(0)
    placed_t[...] = placed[...].T
    placed_xt[:, top] = px_top[...].T
    send_late(1)
    send_late(0)
    px_copy.wait_recv()
    placed_xt[:, bottom] = px[...].T
    conn_start(0, dq2[xl], dq2[ox])
    block_done(1)
    conn_start(2, res[1, 1], res[1, 0])
    block_done(0)
    conn_start(1, res[0, 1], res[0, 0])
    conn_scatter(0)
    conn_scatter(2)
    conn_scatter(1)
    go(remote(dq2.at[ox], gdq, x_send.at[0], x_recv.at[0], ctx=cx))
    go(remote(o2.at[ox], go_in, x_send.at[1], x_recv.at[1], ctx=cx))
    conn_gather(0)
    conn_gather(2)
    conn_gather(1)
    take_grad(1)
    take_grad(0)
    remote(dq2.at[ox], gdq, x_send.at[0], x_recv.at[0], ctx=cx).wait_recv()
    qkv_grad[0, :, mine] = dq2[xl]
    qkv_grad[0, :, other] = gdq[...]
    remote(o2.at[ox], go_in, x_send.at[1], x_recv.at[1], ctx=cx).wait_recv()
    attn_out[:, mine] = o2[xl]
    attn_out[:, other] = go_in[...]
    for i in (0, 2, 1):
        conn_share(i)
    for i in (0, 2, 1):
        conn_finish(i)
    for copy in sends:
        copy.wait_send()


def finish_kernel(attn_in, grad_in, conn_in, attn_out, grad_out, conn_out, conn, sem):
    copies = [pltpu.make_async_copy(attn_in, attn_out, sem.at[0]), pltpu.make_async_copy(grad_in, grad_out, sem.at[1])]
    for copy in copies:
        copy.start()
    part = conn.shape[1] // 4
    for n in range(12):
        i, at = n // 4, pl.ds(n % 4 * part, part)
        conn[i, at, :] = conn_in[i, at, :].astype(F32)
        copy = pltpu.make_async_copy(conn.at[i, at], conn_out.at[i, at], sem.at[2 + n])
        copy.start()
        copies.append(copy)
    for copy in copies:
        copy.wait()


def local(base_qkv, frames, frame_block, frame_slot, frame_live, start_block, conn_w, d_out):
    n_ctx = lax.axis_size("ctx")
    n_tp = lax.axis_size("tp")
    _, rows, width = base_qkv.shape
    vis = frames.shape[2]
    pw = vis // n_tp
    half = rows // 2
    two = 2 * HEAD_DIM
    piece = FRAME_TOK + CODE_ROWS
    vmem = pl.BlockSpec(memory_space=pltpu.VMEM)
    smem = pl.BlockSpec(memory_space=pltpu.SMEM)
    hbm = pl.BlockSpec(memory_space=pltpu.HBM)
    dma = pltpu.SemaphoreType.DMA

    def buf(*shape):
        return pltpu.VMEM(shape, BF16)

    def kept(*arrays, space=pltpu.VMEM):
        return [pltpu.with_memory_space_constraint(x, space) for x in arrays]

    def params(n):
        return pltpu.CompilerParams(collective_id=n, has_side_effects=True, vmem_limit_bytes=VMEM_LIMIT)

    placed, q2, do2, kv, px = pl.pallas_call(
        lambda *refs: gather_kernel(n_ctx, n_tp, *refs),
        out_shape=(
            buf(rows, vis), buf(2, rows, HEAD_DIM), buf(2, rows, HEAD_DIM), buf(n_ctx, rows, two),
            buf(rows // 2, vis),
        ),
        in_specs=[smem, smem, smem, hbm, hbm, hbm, hbm],
        out_specs=(vmem,) * 5,
        scratch_shapes=[
            pltpu.VMEM((n_tp, piece, pw), BF16),
            pltpu.VMEM((n_tp, piece, pw), BF16),
            pltpu.VMEM((n_ctx, piece, pw), BF16),
            pltpu.VMEM((n_ctx, piece, pw), BF16),
            pltpu.VMEM((1, FRAME_TOK, vis), BF16),
            pltpu.VMEM((rows, width), BF16),
            pltpu.VMEM((3, rows, width), BF16),
            pltpu.VMEM((3, vis, width), BF16),
            pltpu.VMEM((3, rows, width), BF16),
            pltpu.VMEM((N_PART, rows // N_PART, two), BF16),
            pltpu.VMEM((rows, HEAD_DIM), BF16),
            pltpu.VMEM((rows, HEAD_DIM), BF16),
            dma((4,)), dma((n_tp,)), dma((n_tp,)), dma((n_ctx,)), dma((n_ctx,)), dma((N_PART, 7)), dma((N_PART, 7)),
            dma((N_PART + 3,)), dma((N_PART + 3,)), dma((2, N_PART, 4)), dma((2, N_PART, 4)),
            dma((N_PART, 8)), dma((N_PART, 8)),
        ],
        compiler_params=params(0),
        name="gather",
    )(
        frame_block, frame_slot, frame_live,
        *kept(frames, base_qkv, conn_w.transpose(1, 0, 2), d_out, space=pltpu.HBM),
    )

    o2, dq2, dk, dv = pl.pallas_call(
        attention_kernel,
        out_shape=(
            buf(2, rows, HEAD_DIM), buf(2, rows, HEAD_DIM), buf(n_ctx, rows, HEAD_DIM), buf(n_ctx, rows, HEAD_DIM),
        ),
        in_specs=[smem, vmem, vmem, vmem],
        out_specs=(vmem, vmem, vmem, vmem),
        scratch_shapes=[
            pltpu.VMEM((n_ctx * rows, two), F32),
            pltpu.VMEM((HEAD_DIM, rows), F32),
            pltpu.VMEM((1, rows), F32),
            pltpu.VMEM((1, rows), F32),
        ],
        compiler_params=pltpu.CompilerParams(vmem_limit_bytes=VMEM_LIMIT),
        name="attention",
    )(*kept(start_block, space=pltpu.SMEM), *kept(q2, do2, kv))

    vis_half = vis // 2
    n_chip = n_ctx // 2
    attn_out, qkv_grad, conn = pl.pallas_call(
        lambda *refs: reduce_kernel(n_ctx, *refs),
        out_shape=(buf(rows, width), buf(3, rows, width), buf(3, vis, width)),
        in_specs=[vmem] * 6,
        out_specs=(vmem, vmem, vmem),
        scratch_shapes=[
            pltpu.VMEM((2, 8, rows, HEAD_DIM), BF16),
            pltpu.VMEM((2, 6, rows, HEAD_DIM), BF16),
            pltpu.VMEM((2, 2, half, HEAD_DIM), BF16),
            pltpu.VMEM((2, 2, half, HEAD_DIM), BF16),
            pltpu.VMEM((2, 2, rows, HEAD_DIM), BF16),
            pltpu.VMEM((2, 2, rows, HEAD_DIM), BF16),
            pltpu.VMEM((2, 2, rows, HEAD_DIM), BF16),
            pltpu.VMEM((2, rows, HEAD_DIM), BF16),
            pltpu.VMEM((rows, HEAD_DIM), BF16),
            pltpu.VMEM((rows, HEAD_DIM), BF16),
            pltpu.VMEM((half, vis), BF16),
            pltpu.VMEM((vis, rows), BF16),
            pltpu.VMEM((vis, rows), BF16),
            pltpu.VMEM((3, vis_half, HEAD_DIM), BF16),
            pltpu.VMEM((3, vis_half, HEAD_DIM), BF16),
            pltpu.VMEM((3, vis_half, HEAD_DIM), F32),
            pltpu.VMEM((3, vis_half, HEAD_DIM), BF16),
            pltpu.VMEM((3, N_Z, vis_half // N_Z, HEAD_DIM), BF16),
            dma((2, 8)), dma((2, 8)), dma((2, 4)), dma((2, 4)), dma((2, 8)), dma((2, 8)), dma((5,)), dma((5,)),
            dma((3,)), dma((3,)), dma((3, N_Z)), dma((3, N_Z)), dma((3, n_chip)), dma((3, n_chip)),
            dma((3,)), dma((3,)),
        ],
        compiler_params=params(1),
        name="reduce",
    )(*kept(dk, dv, dq2, o2, placed, px))

    out = pl.BlockSpec(memory_space=pl.ANY)
    attn_out, qkv_grad, conn = pl.pallas_call(
        finish_kernel,
        out_shape=(
            jax.ShapeDtypeStruct((rows, width), BF16), jax.ShapeDtypeStruct((3, rows, width), BF16),
            jax.ShapeDtypeStruct((3, vis, width), F32),
        ),
        in_specs=[vmem] * 3,
        out_specs=(out, out, out),
        scratch_shapes=[pltpu.VMEM((3, vis, width), F32), dma((14,))],
        compiler_params=pltpu.CompilerParams(vmem_limit_bytes=VMEM_LIMIT),
        name="finish",
    )(*kept(attn_out, qkv_grad, conn))
    return (attn_out, qkv_grad, conn.transpose(1, 0, 2))


def solution(mesh):
    return jax.shard_map(
        local,
        mesh=mesh,
        in_specs=(
            P(None, "ctx", "tp"),
            P(("ctx", "tp"), None, None),
            P(("ctx", "tp")),
            P(("ctx", "tp")),
            P(("ctx", "tp")),
            P(),
            P(None, None, "tp"),
            P("ctx", "tp"),
        ),
        out_specs=(P("ctx", "tp"), P(None, "ctx", "tp"), P(None, None, "tp")),
        check_vma=False,
    )
```
